32 devices in a mesh: groups: 2 (over x), dp: 16 (over z, y, core).
Axes of the slice: x: 2, y: 2, z: 4, core: 2. Of those that a mesh axis runs over, the one named last changes fastest.
Arguments:
- tokens: bfloat16 [4096, 5120], P(('groups', 'dp')), parts along dimension 0, may hold values from -6 to 6
- cotangent: bfloat16 [4096, 5120], P(('groups', 'dp')), parts along dimension 0, may hold values from -6 to 6
- segments: int32 [32, 1, 3], P('groups'), parts along dimension 0, may hold values from 0 to 15, as said below
- owner_map: int32 [32], P('groups'), parts along dimension 0, may hold values from 0 to 15, each once
- down_t: bfloat16 [32, 64, 5120], P(('groups', 'dp')), parts along dimension 0, may hold values from -0.078125 to 0.078125
- up: bfloat16 [32, 64, 5120], P(('groups', 'dp')), parts along dimension 0, may hold values from -0.75 to 0.75
Outputs:
- grad_tokens: bfloat16 [4096, 5120], P(('groups', 'dp')), parts along dimension 0
- grad_down: bfloat16 [32, 64, 5120], P(('groups', 'dp')), parts along dimension 0
- grad_up: bfloat16 [32, 64, 5120], P(('groups', 'dp')), parts along dimension 0
The draws below stay inside these ranges and needn't reach their ends.
There are 2 independent parts, one for each index of `groups`. The reference program is written for one: setup_inputs(seed, part) draws one part's arguments, and reference() takes and returns one part's arrays. A program takes and returns all parts, laid end to end along the dimension named above; each array names one. Nothing has to cross between parts.
Inputs may be any that keep to these rules, and one draw needn't show every extreme that they name: In segments[d] the live entries (count 1 or more) come first, cover blocks 0 to 0 in order without gaps, and the rest are (0, 0, 0); ids name adapters, some far more often than others.
All inputs are finite; a program needn't handle non-finite values.
Results may differ from the reference program's by a relative error of at most 0.0075.
Values may be sent and summed in bfloat16 or wider, within the bound.
No kernel may reach another device: no remote copies, remote signals or barrier semaphores. Data moves between devices by JAX's collectives and lax.ppermute only.
A program may use at most 64 MiB of HBM per device.

```python
import jax
import jax.numpy as jnp
from jax import lax

D = 5120
R = 64
BLOCK = 128
BLK_DEV = 1
ADAPTERS = 16
TOKENS = 2048
N_DP = 16


def draw_segments(key, part):
    key = jax.random.fold_in(key, 11)
    key_flag, key_first, key_second, key_device = jax.random.split(key, 4)
    flags = jax.random.randint(key_flag, (N_DP, BLK_DEV), 0, 2)
    flags = jnp.where(jnp.arange(BLK_DEV)[None, :] == 0, 1, flags)
    member_index = jnp.cumsum(flags, axis=1) - 1
    entry = jnp.arange(BLK_DEV)
    member = member_index[:, None, :] == entry[None, :, None]
    counts = jnp.sum(member.astype(jnp.int32), axis=2)
    first = member & (flags[:, None, :] == 1)
    starts = jnp.sum(jnp.where(first, entry[None, None, :], 0), axis=2)
    first_draw = jax.random.randint(key_first, (N_DP, BLK_DEV), 0, ADAPTERS)
    second_draw = jax.random.randint(key_second, (N_DP, BLK_DEV), 0, ADAPTERS)
    ids = ADAPTERS - 1 - first_draw * second_draw // ADAPTERS
    chosen = jax.random.randint(key_device, (), 0, N_DP)
    forced = (jnp.arange(N_DP)[:, None] == chosen) & (entry[None, :] == 0)
    ids = jnp.where(forced, ADAPTERS - 1, ids)
    live = counts > 0
    ids = jnp.where(live, ids, 0)
    starts = jnp.where(live, starts, 0)
    return jnp.stack([ids, starts, counts], axis=-1).astype(jnp.int32)


def shard_levels(rng, dims, cuts, low, high):
    loudness = 1.0
    for position, blocks in cuts:
        draws = jax.random.uniform(jax.random.fold_in(jax.random.fold_in(rng, 6), position), (blocks,), jnp.float32, low / len(cuts), high / len(cuts))
        loudness = loudness * jnp.repeat(jnp.exp(draws), dims[position] // blocks).reshape((-1,) + (1,) * (len(dims) - 1 - position))
    return loudness


def normal_values(own_key, dims, deviation, reach, shards=(), kind=jnp.bfloat16):
    entries = jax.random.normal(own_key, dims, jnp.float32) * deviation
    if len(shards) > 0:
        entries = shard_levels(own_key, dims, shards, -0.22, 0.18) * entries
    return jnp.clip(entries, min=-reach, max=reach).astype(kind)


def setup_inputs(seed: int = 0, part: int = 0) -> dict:
    key_list = jax.random.split(jax.random.key(seed), 7)
    part_keys = jax.random.split(jax.random.fold_in(key_list[6], part), 7)
    return {
        "tokens": normal_values(part_keys[0], (TOKENS, D), 1.0, 6.0, ((0, 16),)),
        "cotangent": normal_values(part_keys[1], (TOKENS, D), 1.0, 6.0, ((0, 16),)),
        "segments": draw_segments(jax.random.fold_in(jax.random.fold_in(key_list[6], part), 71), part),
        "owner_map": jax.random.permutation(part_keys[3], ADAPTERS).astype(jnp.int32),
        "down_t": normal_values(part_keys[4], (ADAPTERS, R, D), D ** -0.5, 0.078125, ((0, 16),)),
        "up": normal_values(part_keys[5], (ADAPTERS, R, D), R ** -0.5, 0.75, ((0, 16),)),
    }


def block_slots(segments, owner_map, blocks, count_adapters):
    index = jnp.arange(blocks, dtype=jnp.int32)
    ids = segments[:, :, 0]
    starts = segments[:, :, 1]
    counts = segments[:, :, 2]
    inside = (index[None, None, :] >= starts[:, :, None]) & (index[None, None, :] < (starts + counts)[:, :, None])
    adapter = jnp.sum(jnp.where(inside, ids[:, :, None], 0), axis=1).astype(jnp.int32)
    match = adapter[:, :, None] == jnp.arange(count_adapters, dtype=jnp.int32)[None, None, :]
    slots = jnp.sum(jnp.where(match, owner_map[None, None, :], 0), axis=2).astype(jnp.int32)
    return slots.reshape(-1)


def reference(tokens, cotangent, segments, owner_map, down_t, up):
    slots = block_slots(segments, owner_map, BLK_DEV, ADAPTERS)
    rows = tokens.reshape(N_DP * BLK_DEV, BLOCK, D)
    cots = cotangent.reshape(N_DP * BLK_DEV, BLOCK, D)

    def step(carry, item):
        sum_down, sum_up = carry
        block_rows, block_cot, slot = item
        w_down = lax.dynamic_index_in_dim(down_t, slot, 0, keepdims=False).astype(jnp.float32)
        w_up = lax.dynamic_index_in_dim(up, slot, 0, keepdims=False).astype(jnp.float32)
        xf = block_rows.astype(jnp.float32)
        gf = block_cot.astype(jnp.float32)
        hidden = jnp.einsum("td,rd->tr", xf, w_down).astype(jnp.bfloat16).astype(jnp.float32)
        inner = jnp.einsum("td,rd->tr", gf, w_up).astype(jnp.bfloat16).astype(jnp.float32)
        grad_rows = jnp.einsum("tr,rd->td", inner, w_down).astype(jnp.bfloat16)
        term_down = jnp.einsum("tr,td->rd", inner, xf)
        term_up = jnp.einsum("tr,td->rd", hidden, gf)
        sum_down = sum_down.at[slot].add(term_down)
        sum_up = sum_up.at[slot].add(term_up)
        return (sum_down, sum_up), grad_rows

    start = (jnp.zeros((ADAPTERS, R, D), jnp.float32), jnp.zeros((ADAPTERS, R, D), jnp.float32))
    (sum_down, sum_up), grad_rows = lax.scan(step, start, (rows, cots, slots))
    scale = 1.0 / BLOCK
    grad_tokens = grad_rows.reshape(N_DP * BLK_DEV * BLOCK, D)
    return grad_tokens, (sum_down * scale).astype(jnp.bfloat16), (sum_up * scale).astype(jnp.bfloat16)
```

```python
import jax
import jax.numpy as jnp
from jax import lax
from jax.sharding import PartitionSpec as P

BLOCK = 128


def block_slots(segments, owner_map, blocks, count_adapters):
    index = jnp.arange(blocks, dtype=jnp.int32)
    ids = segments[:, :, 0]
    starts = segments[:, :, 1]
    counts = segments[:, :, 2]
    inside = (index[None, None, :] >= starts[:, :, None]) & (
        index[None, None, :] < (starts + counts)[:, :, None]
    )
    adapter = jnp.sum(jnp.where(inside, ids[:, :, None], 0), axis=1)
    match = adapter[:, :, None] == jnp.arange(count_adapters, dtype=jnp.int32)[None, None, :]
    slots = jnp.sum(jnp.where(match, owner_map[None, None, :], 0), axis=2)
    return slots.reshape(-1)


def shards(tokens, cotangent, segments, owner_map, down_t, up):
    devices = lax.axis_size("dp")
    width = tokens.shape[1]
    rank = down_t.shape[1]
    slots = block_slots(segments, owner_map, 1, devices)
    scale = 1.0 / BLOCK
    piece = 2 * rank // devices
    stack = jnp.concatenate([down_t[0], up[0]], axis=0).reshape(devices, piece, width)
    table = lax.all_to_all(stack, "dp", split_axis=0, concat_axis=0, tiled=True)
    chosen = jnp.take(table, slots, axis=0, mode="clip")
    mine = lax.all_to_all(chosen, "dp", split_axis=0, concat_axis=0, tiled=True)
    mine = mine.reshape(2 * rank, width)
    down, up_ = mine[:rank], mine[rank:]
    f32 = jnp.float32
    hidden = jnp.einsum("td,rd->tr", tokens, down, preferred_element_type=f32).astype(jnp.bfloat16)
    inner = jnp.einsum("td,rd->tr", cotangent, up_, preferred_element_type=f32).astype(jnp.bfloat16)
    term_down = jnp.einsum("tr,td->rd", inner, tokens, preferred_element_type=f32)
    term_up = jnp.einsum("tr,td->rd", hidden, cotangent, preferred_element_type=f32)
    terms = jnp.concatenate([term_down, term_up], axis=0).astype(jnp.bfloat16)
    grad_rows = jnp.einsum("tr,rd->td", inner, down, preferred_element_type=f32).astype(jnp.bfloat16)
    pieces = lax.all_to_all(
        terms.reshape(devices, piece, width), "dp", split_axis=0, concat_axis=0, tiled=True
    )
    onehot = (slots[None, :] == jnp.arange(devices, dtype=jnp.int32)[:, None]).astype(jnp.bfloat16)
    summed = jnp.einsum("kb,bpd->kpd", onehot, pieces, preferred_element_type=f32) * scale
    grads = lax.all_to_all(
        summed.astype(jnp.bfloat16), "dp", split_axis=0, concat_axis=0, tiled=True
    ).reshape(2, rank, width)
    return grad_rows, grads[:1], grads[1:]


def solution(mesh):
    in_specs = (
        P(("groups", "dp"), None),
        P(("groups", "dp"), None),
        P("groups", None, None),
        P("groups"),
        P(("groups", "dp"), None, None),
        P(("groups", "dp"), None, None),
    )
    out_specs = (
        P(("groups", "dp"), None),
        P(("groups", "dp"), None, None),
        P(("groups", "dp"), None, None),
    )
    return jax.shard_map(shards, mesh=mesh, in_specs=in_specs, out_specs=out_specs, check_vma=False)
```

```python
import functools

import jax
import jax.numpy as jnp
from jax import lax
from jax.experimental import pallas as pl
from jax.experimental.pallas import tpu as pltpu
from jax.sharding import PartitionSpec as P

BLOCK = 128
F32 = jnp.float32
BF16 = jnp.bfloat16
I32 = jnp.int32


def block_slots(segments, owner_map, blocks, count_adapters):
    index = jnp.arange(blocks, dtype=I32)
    ids = segments[:, :, 0]
    starts = segments[:, :, 1]
    counts = segments[:, :, 2]
    inside = (index[None, None, :] >= starts[:, :, None]) & (
        index[None, None, :] < (starts + counts)[:, :, None]
    )
    adapter = jnp.sum(jnp.where(inside, ids[:, :, None], 0), axis=1)
    match = adapter[:, :, None] == jnp.arange(count_adapters, dtype=I32)[None, None, :]
    slots = jnp.sum(jnp.where(match, owner_map[None, None, :], 0), axis=2)
    return slots.reshape(-1)


def padded(shape, itemsize):
    rows = -(-shape[-2] // 16) * 16
    size = rows * shape[-1] * itemsize
    for extent in shape[:-2]:
        size *= extent
    return size


def vmem(shapes):
    return pltpu.CompilerParams(
        vmem_limit_bytes=sum(padded(shape, size) for shape, size in shapes) + (4 << 20)
    )


def select_pieces(index, sources, count):
    shape = (count,) + sources[0].shape[1:]
    sizes = [source.shape[0] for source in sources]

    def kernel(index_ref, *refs):
        out_ref = refs[-1]

        def body(j, carry):
            place = index_ref[j]
            low = 0
            for size, ref in zip(sizes, refs[:-1]):

                @pl.when((place >= low) & (place < low + size))
                def _(ref=ref, low=low):
                    out_ref[j] = ref[place - low]

                low += size
            return carry

        lax.fori_loop(0, count, body, 0)

    whole = pl.BlockSpec(memory_space=pltpu.VMEM)
    return pl.pallas_call(
        kernel,
        out_shape=jax.ShapeDtypeStruct(shape, sources[0].dtype),
        in_specs=[pl.BlockSpec(memory_space=pltpu.SMEM)] + [whole] * len(sources),
        out_specs=whole,
        compiler_params=vmem([(source.shape, 2) for source in sources] + [(shape, 2)]),
    )(index, *sources)


def sum_pieces(indices, sources, count, scale):
    shape = (count,) + sources[0].shape[1:]
    total_shape = (count + 1,) + sources[0].shape[1:]
    many = len(sources)

    def kernel(*refs):
        index_refs, source_refs = refs[:many], refs[many : 2 * many]
        out_ref, total_ref = refs[2 * many :]
        total_ref[...] = jnp.zeros_like(total_ref)
        for index_ref, source_ref in zip(index_refs, source_refs):

            def body(d, carry, index_ref=index_ref, source_ref=source_ref):
                place = index_ref[d]
                total_ref[place] = total_ref[place] + source_ref[d].astype(F32)
                return carry

            lax.fori_loop(0, source_ref.shape[0], body, 0)

        def finish(k, carry):
            out_ref[k] = (total_ref[k] * scale).astype(BF16)
            return carry

        lax.fori_loop(0, count, finish, 0)

    whole = pl.BlockSpec(memory_space=pltpu.VMEM)
    return pl.pallas_call(
        kernel,
        out_shape=jax.ShapeDtypeStruct(shape, BF16),
        in_specs=[pl.BlockSpec(memory_space=pltpu.SMEM)] * many + [whole] * many,
        out_specs=whole,
        scratch_shapes=[pltpu.VMEM(total_shape, F32)],
        compiler_params=vmem(
            [(source.shape, 2) for source in sources] + [(shape, 2), (total_shape, 4)]
        ),
    )(*indices, *sources)


def dot(spec, a, b):
    return jnp.einsum(spec, a, b, preferred_element_type=F32)


def two_step(slots, tokens, cotangent, down_t, up):
    devices = lax.axis_size("dp")
    rank, width = down_t.shape[1:]
    piece = 2 * rank // devices
    exchange = functools.partial(
        lax.all_to_all, axis_name="dp", split_axis=0, concat_axis=0, tiled=True
    )
    stack = jnp.concatenate([down_t[0], up[0]], axis=0).reshape(devices, piece, width)
    table = exchange(stack)
    mine = exchange(jnp.take(table, slots, axis=0, mode="clip")).reshape(2 * rank, width)
    down, up_ = mine[:rank], mine[rank:]
    hidden = dot("td,rd->tr", tokens, down).astype(BF16)
    inner = dot("td,rd->tr", cotangent, up_).astype(BF16)
    grad_rows = dot("tr,rd->td", inner, down).astype(BF16)
    terms = jnp.concatenate(
        [dot("tr,td->rd", inner, tokens), dot("tr,td->rd", hidden, cotangent)], axis=0
    ).astype(BF16)
    pieces = exchange(terms.reshape(devices, piece, width))
    onehot = (slots[None, :] == jnp.arange(devices, dtype=I32)[:, None]).astype(BF16)
    summed = dot("kb,bpd->kpd", onehot, pieces) * (1.0 / BLOCK)
    grads = exchange(summed.astype(BF16)).reshape(2, rank, width)
    return grad_rows, grads[:1], grads[1:]


def crossing(slots, devices):
    half = devices // 2
    k = jnp.arange(devices, dtype=I32)
    side = k // half
    uses = slots[:, None] == k[None, :]
    need = jnp.any(uses & (side[:, None] != side[None, :]), axis=0)
    before = need[None, :] & (side[None, :] == side[:, None]) & (k[None, :] < k[:, None])
    place = jnp.sum(before.astype(I32), axis=1)
    counts = jnp.stack([jnp.sum(need[:half].astype(I32)), jnp.sum(need[half:].astype(I32))])
    return need, place, counts


def three_step(capacity, slots, need, place, counts, tokens, cotangent, down_t, up):
    devices = lax.axis_size("dp")
    half = devices // 2
    rank, width = down_t.shape[1:]
    piece = rank // half
    groups = [list(range(half)), list(range(half, devices))]
    pairs = [(i, (i + half) % devices) for i in range(devices)]
    exchange = functools.partial(
        lax.all_to_all,
        axis_name="dp",
        split_axis=0,
        concat_axis=0,
        tiled=True,
        axis_index_groups=groups,
    )
    cross = functools.partial(lax.ppermute, axis_name="dp", perm=pairs)
    side = lax.axis_index("dp") // half
    k = jnp.arange(half, dtype=I32)
    j = jnp.arange(capacity, dtype=I32)
    my_need = lax.dynamic_slice(need, (side * half,), (half,))
    my_place = lax.dynamic_slice(place, (side * half,), (half,))
    my_count = lax.dynamic_slice(counts, (side,), (1,))
    my_slots = lax.dynamic_slice(slots, (side * half,), (half,))
    match = my_need[None, :] & (my_place[None, :] == j[:, None])
    send = jnp.sum(jnp.where(match, k[None, :], 0), axis=1)
    local = my_slots // half == side
    slot_place = jnp.sum(
        jnp.where(my_slots[:, None] == jnp.arange(devices, dtype=I32)[None, :], place[None, :], 0),
        axis=1,
    )
    fetch = jnp.where(local, my_slots % half, half + slot_place)
    to_cross = jnp.where(local, capacity, slot_place)
    to_local = jnp.where(local, my_slots % half, half)
    to_arrived = jnp.where(j < my_count, send, half)

    def spread(adapter):
        return exchange(adapter.reshape(half, piece, width))

    def send_across(table):
        return cross(select_pieces(send, [table], capacity))

    def gather(table, arrived):
        return exchange(select_pieces(fetch, [table, arrived], half)).reshape(rank, width)

    def sums_across(pieces):
        return cross(sum_pieces([to_cross], [pieces], capacity, 1.0))

    def collect(pieces, arrived):
        summed = sum_pieces([to_local, to_arrived], [pieces, arrived], half, 1.0 / BLOCK)
        return exchange(summed).reshape(1, rank, width)

    table_down = spread(down_t)
    arrived_down = send_across(table_down)
    table_up = spread(up)
    arrived_up = send_across(table_up)
    down = gather(table_down, arrived_down)
    hidden = dot("td,rd->tr", tokens, down).astype(BF16)
    term_up = dot("tr,td->rd", hidden, cotangent).astype(BF16)
    up_ = gather(table_up, arrived_up)
    pieces_up = spread(term_up)
    inner = dot("td,rd->tr", cotangent, up_).astype(BF16)
    term_down = dot("tr,td->rd", inner, tokens).astype(BF16)
    sums_up = sums_across(pieces_up)
    pieces_down = spread(term_down)
    sums_down = sums_across(pieces_down)
    grad_rows = dot("tr,rd->td", inner, down).astype(BF16)
    grad_up = collect(pieces_up, sums_up)
    grad_down = collect(pieces_down, sums_down)
    return grad_rows, grad_down, grad_up


def shards(tokens, cotangent, segments, owner_map, down_t, up):
    devices = lax.axis_size("dp")
    slots = block_slots(segments, owner_map, 1, devices)
    need, place, counts = crossing(slots, devices)
    capacity = devices // 4

    def few(*args):
        return three_step(capacity, slots, need, place, counts, *args)

    def many(*args):
        return two_step(slots, *args)

    return lax.cond(jnp.max(counts) <= capacity, few, many, tokens, cotangent, down_t, up)


def solution(mesh):
    in_specs = (
        P(("groups", "dp"), None),
        P(("groups", "dp"), None),
        P("groups", None, None),
        P("groups"),
        P(("groups", "dp"), None, None),
        P(("groups", "dp"), None, None),
    )
    out_specs = (
        P(("groups", "dp"), None),
        P(("groups", "dp"), None, None),
        P(("groups", "dp"), None, None),
    )
    return jax.shard_map(shards, mesh=mesh, in_specs=in_specs, out_specs=out_specs, check_vma=False)
```

```python
import functools

import jax
import jax.numpy as jnp
from jax import lax
from jax.experimental import pallas as pl
from jax.experimental.pallas import tpu as pltpu
from jax.sharding import PartitionSpec as P

BLOCK = 128
F32 = jnp.float32
BF16 = jnp.bfloat16
I32 = jnp.int32
VMEM = pl.BlockSpec(memory_space=pltpu.VMEM)
SMEM = pl.BlockSpec(memory_space=pltpu.SMEM)


def block_slots(segments, owner_map, blocks, count_adapters):
    index = jnp.arange(blocks, dtype=I32)
    ids = segments[:, :, 0]
    starts = segments[:, :, 1]
    counts = segments[:, :, 2]
    inside = (index[None, None, :] >= starts[:, :, None]) & (
        index[None, None, :] < (starts + counts)[:, :, None]
    )
    adapter = jnp.sum(jnp.where(inside, ids[:, :, None], 0), axis=1)
    match = adapter[:, :, None] == jnp.arange(count_adapters, dtype=I32)[None, None, :]
    slots = jnp.sum(jnp.where(match, owner_map[None, None, :], 0), axis=2)
    return slots.reshape(-1)


def dot(spec, a, b):
    return jnp.einsum(spec, a, b, preferred_element_type=F32)


def two_step(slots, tokens, cotangent, down_t, up):
    devices = lax.axis_size("dp")
    rank, width = down_t.shape[1:]
    piece = 2 * rank // devices
    exchange = functools.partial(
        lax.all_to_all, axis_name="dp", split_axis=0, concat_axis=0, tiled=True
    )
    stack = jnp.concatenate([down_t[0], up[0]], axis=0).reshape(devices, piece, width)
    table = exchange(stack)
    mine = exchange(jnp.take(table, slots, axis=0, mode="clip")).reshape(2 * rank, width)
    down, up_ = mine[:rank], mine[rank:]
    hidden = dot("td,rd->tr", tokens, down).astype(BF16)
    inner = dot("td,rd->tr", cotangent, up_).astype(BF16)
    grad_rows = dot("tr,rd->td", inner, down).astype(BF16)
    terms = jnp.concatenate(
        [dot("tr,td->rd", inner, tokens), dot("tr,td->rd", hidden, cotangent)], axis=0
    ).astype(BF16)
    pieces = exchange(terms.reshape(devices, piece, width))
    onehot = (slots[None, :] == jnp.arange(devices, dtype=I32)[:, None]).astype(BF16)
    summed = dot("kb,bpd->kpd", onehot, pieces) * (1.0 / BLOCK)
    grads = exchange(summed.astype(BF16)).reshape(2, rank, width)
    return grad_rows, grads[:1], grads[1:]


def params(*shapes):
    size = 8 << 20
    for shape, width in shapes:
        extent = width
        for value in shape:
            extent *= value
        size += extent
    return pltpu.CompilerParams(vmem_limit_bytes=size)


def call(kernel, scalars, arrays, outs, scratch=()):
    sizes = [(a.shape, a.dtype.itemsize) for a in arrays]
    sizes += [(o.shape, o.dtype.itemsize) for o in outs]
    sizes += [(s.shape, s.dtype.itemsize) for s in scratch]
    return pl.pallas_call(
        kernel,
        out_shape=outs,
        in_specs=[SMEM] * len(scalars) + [VMEM] * len(arrays),
        out_specs=[VMEM] * len(outs),
        scratch_shapes=[pltpu.VMEM(s.shape, s.dtype) for s in scratch],
        compiler_params=params(*sizes),
    )(*scalars, *arrays)


def split_pieces(places, stacked):
    half = stacked.shape[0]

    def kernel(places_ref, stacked_ref, *out_refs):
        for r in range(half):
            out_refs[r][...] = stacked_ref[places_ref[r]]

    piece = jax.ShapeDtypeStruct(stacked.shape[1:], BF16)
    return call(kernel, [places], [stacked], [piece] * half)


def join_pieces(places, pieces):
    half = len(pieces)

    def kernel(places_ref, *refs):
        for r in range(half):
            refs[half][places_ref[r]] = refs[r][...]

    out = jax.ShapeDtypeStruct((half,) + pieces[0].shape, BF16)
    return call(kernel, [places], pieces, [out])[0]


def pick_stacked(index, pieces, count):
    half = len(pieces)
    shape = pieces[0].shape

    def kernel(index_ref, *refs):
        out_ref, all_ref = refs[half:]
        for r in range(half):
            all_ref[r] = refs[r][...]
        for j in range(count):
            out_ref[j] = all_ref[index_ref[j]]

    out = jax.ShapeDtypeStruct((count,) + shape, BF16)
    return call(kernel, [index], pieces, [out], [jax.ShapeDtypeStruct((half,) + shape, BF16)])[0]


def pick_pieces(index, pieces, arrived):
    half = len(pieces)
    count = arrived.shape[0]
    shape = pieces[0].shape

    def kernel(index_ref, *refs):
        out_refs, all_ref = refs[half + 1 : -1], refs[-1]
        for r in range(half):
            all_ref[r] = refs[r][...]
        for j in range(count):
            all_ref[half + j] = refs[half][j]
        for r in range(half):
            out_refs[r][...] = all_ref[index_ref[r]]

    out = jax.ShapeDtypeStruct(shape, BF16)
    scratch = jax.ShapeDtypeStruct((half + count,) + shape, BF16)
    return call(kernel, [index], list(pieces) + [arrived], [out] * half, [scratch])


def sum_stacked(index, pieces, count):
    half = len(pieces)
    shape = pieces[0].shape

    def kernel(index_ref, *refs):
        out_ref, total_ref = refs[half:]
        total_ref[...] = jnp.zeros_like(total_ref)
        for r in range(half):
            place = index_ref[r]
            total_ref[place] = total_ref[place] + refs[r][...].astype(F32)
        for k in range(count):
            out_ref[k] = total_ref[k].astype(BF16)

    out = jax.ShapeDtypeStruct((count,) + shape, BF16)
    scratch = jax.ShapeDtypeStruct((half + 1,) + shape, F32)
    return call(kernel, [index], pieces, [out], [scratch])[0]


def sum_pieces(index, arrived_index, places, pieces, arrived):
    half = len(pieces)
    count = arrived.shape[0]
    shape = pieces[0].shape

    def kernel(index_ref, arrived_index_ref, places_ref, *refs):
        out_refs, total_ref = refs[half + 1 : -1], refs[-1]
        total_ref[...] = jnp.zeros_like(total_ref)
        for r in range(half):
            place = index_ref[r]
            total_ref[place] = total_ref[place] + refs[r][...].astype(F32)
        for j in range(count):
            place = arrived_index_ref[j]
            total_ref[place] = total_ref[place] + refs[half][j].astype(F32)
        for r in range(half):
            out_refs[r][...] = (total_ref[places_ref[r]] * (1.0 / BLOCK)).astype(BF16)

    out = jax.ShapeDtypeStruct(shape, BF16)
    scratch = jax.ShapeDtypeStruct((half + 1,) + shape, F32)
    return call(
        kernel, [index, arrived_index, places], list(pieces) + [arrived], [out] * half, [scratch]
    )


def term_pieces(places, pieces, first, second):
    half = len(pieces)
    rows, width = first.shape
    piece = pieces[0].shape[0]
    rank = half * piece
    step = max(s for s in (128, 256, 512, 640, 1024) if width % s == 0)

    def kernel(places_ref, *refs):
        first_ref, second_ref = refs[half : half + 2]
        adapter_ref, projected_ref = refs[half + 2 : half + 4]
        out_refs, term_ref = refs[half + 4 : -1], refs[-1]
        for r in range(half):
            adapter_ref[places_ref[r]] = refs[r][...]
        total = jnp.zeros((rows, rank), F32)
        for low in range(0, width, step):
            total += lax.dot_general(
                first_ref[:, low : low + step],
                adapter_ref[:, :, low : low + step].reshape(rank, step),
                (((1,), (1,)), ((), ())),
                preferred_element_type=F32,
            )
        projected = total.astype(BF16)
        projected_ref[...] = projected
        turned = total.T.astype(BF16)
        for low in range(0, width, step):
            term = jnp.dot(turned, second_ref[:, low : low + step], preferred_element_type=F32)
            term_ref[:, :, low : low + step] = term.astype(BF16).reshape(half, piece, step)
        for r in range(half):
            out_refs[r][...] = term_ref[places_ref[r]]

    stacked = jax.ShapeDtypeStruct((half, piece, width), BF16)
    out = jax.ShapeDtypeStruct((piece, width), BF16)
    got = call(
        kernel,
        [places],
        list(pieces) + [first, second],
        [stacked, jax.ShapeDtypeStruct((rows, rank), BF16)] + [out] * half,
        [stacked],
    )
    return got[0].reshape(rank, width), got[1], got[2:]


def routes(slots, devices):
    half = devices // 2
    me = lax.axis_index("dp")
    side, own = me // half, me % half
    k = jnp.arange(devices, dtype=I32)
    h = jnp.arange(half, dtype=I32)
    k_side = k // half
    need = jnp.any((slots[:, None] == k[None, :]) & (k_side[:, None] != k_side[None, :]), axis=0)
    before = need[None, :] & (k_side[None, :] == k_side[:, None]) & (k[None, :] < k[:, None])
    place = jnp.sum(before.astype(I32), axis=1)
    high = jnp.sum(jnp.where(need & (k_side == 1), 1, 0))
    low = jnp.sum(jnp.where(need & (k_side == 0), 1, 0))
    mine = need & (k_side == side)
    send = jnp.sum(jnp.where(mine[None, :] & (place[None, :] == h[:, None]), k % half, 0), axis=1)
    count = jnp.where(side == 0, low, high)
    places = own ^ h
    user_slot = jnp.sum(
        jnp.where(k[None, :] == (side * half + places)[:, None], slots[None, :], 0), axis=1
    )
    user_place = jnp.sum(jnp.where(user_slot[:, None] == k[None, :], place[None, :], 0), axis=1)
    local = user_slot // half == side
    return {
        "most": jnp.maximum(low, high),
        "places": places,
        "send": send ^ own,
        "fetch": jnp.where(local, (user_slot % half) ^ own, half + user_place),
        "to_cross": jnp.where(local, half, user_place),
        "to_local": jnp.where(local, user_slot % half, half),
        "to_arrived": jnp.where(h < count, send, half),
    }


def three_step(capacity, route, tokens, cotangent, table_down, up):
    devices = lax.axis_size("dp")
    half = devices // 2
    places = route["places"]
    pairs = [(i, (i + half) % devices) for i in range(devices)]

    def across(array):
        return lax.ppermute(array, "dp", pairs)

    def gather(table, arrived):
        return exchange(pick_pieces(route["fetch"], table, arrived))

    def collect(pieces, arrived):
        return exchange(
            sum_pieces(route["to_local"], route["to_arrived"], places, pieces, arrived)
        )

    arrived_down = across(pick_stacked(route["send"], table_down, capacity))
    table_up = exchange(split_pieces(places, up))
    arrived_up = across(pick_stacked(route["send"], table_up, capacity))
    got_down = gather(table_down, arrived_down)
    down, hidden, term_up = term_pieces(places, got_down, tokens, cotangent)
    pieces_up = exchange(term_up)
    got_up = gather(table_up, arrived_up)
    sums_up = across(sum_stacked(route["to_cross"], pieces_up, capacity))
    _, inner, term_down = term_pieces(places, got_up, cotangent, tokens)
    pieces_down = exchange(term_down)
    sums_down = across(sum_stacked(route["to_cross"], pieces_down, capacity))
    grad_up = collect(pieces_up, sums_up)
    grad_rows = dot("tr,rd->td", inner, down).astype(BF16)
    grad_down = collect(pieces_down, sums_down)
    return grad_rows, grad_down, grad_up


def exchange(pieces):
    devices = lax.axis_size("dp")
    half = len(pieces)
    got = list(pieces)
    for r in sorted(range(1, half), key=lambda r: (-bin(r).count("1"), -r)):
        got[r] = lax.ppermute(pieces[r], "dp", [(i, i ^ r) for i in range(devices)])
    return got


def shards(tokens, cotangent, segments, owner_map, down_t, up):
    devices = lax.axis_size("dp")
    slots = block_slots(segments, owner_map, 1, devices)
    if devices != 16:
        return two_step(slots, tokens, cotangent, down_t, up)
    half = devices // 2
    rank, width = down_t.shape[1:]
    shape = (half, rank // half, width)
    own = lax.axis_index("dp") % half
    table_down = exchange(split_pieces(own ^ jnp.arange(half, dtype=I32), down_t.reshape(shape)))
    route = routes(slots, devices)
    capacities = [3, 4, 5, half]
    branch = sum((route["most"] > c).astype(I32) for c in capacities[:-1])
    grad_rows, grad_down, grad_up = lax.switch(
        branch,
        [functools.partial(three_step, c) for c in capacities],
        route,
        tokens,
        cotangent,
        table_down,
        up.reshape(shape),
    )
    return (
        grad_rows,
        join_pieces(route["places"], grad_down).reshape(1, rank, width),
        join_pieces(route["places"], grad_up).reshape(1, rank, width),
    )


def solution(mesh):
    in_specs = (
        P(("groups", "dp"), None),
        P(("groups", "dp"), None),
        P("groups", None, None),
        P("groups"),
        P(("groups", "dp"), None, None),
        P(("groups", "dp"), None, None),
    )
    out_specs = (
        P(("groups", "dp"), None),
        P(("groups", "dp"), None, None),
        P(("groups", "dp"), None, None),
    )
    return jax.shard_map(shards, mesh=mesh, in_specs=in_specs, out_specs=out_specs, check_vma=False)
```

```python
import functools

import jax
import jax.numpy as jnp
from jax import lax
from jax.experimental import pallas as pl
from jax.experimental.pallas import tpu as pltpu
from jax.sharding import PartitionSpec as P

BLOCK = 128
F32 = jnp.float32
BF16 = jnp.bfloat16
I32 = jnp.int32
VMEM = pl.BlockSpec(memory_space=pltpu.VMEM)
SMEM = pl.BlockSpec(memory_space=pltpu.SMEM)


def block_slots(segments, owner_map, blocks, count_adapters):
    index = jnp.arange(blocks, dtype=I32)
    ids = segments[:, :, 0]
    starts = segments[:, :, 1]
    counts = segments[:, :, 2]
    inside = (index[None, None, :] >= starts[:, :, None]) & (
        index[None, None, :] < (starts + counts)[:, :, None]
    )
    adapter = jnp.sum(jnp.where(inside, ids[:, :, None], 0), axis=1)
    match = adapter[:, :, None] == jnp.arange(count_adapters, dtype=I32)[None, None, :]
    slots = jnp.sum(jnp.where(match, owner_map[None, None, :], 0), axis=2)
    return slots.reshape(-1)


def dot(spec, a, b):
    return jnp.einsum(spec, a, b, preferred_element_type=F32)


def two_step(slots, tokens, cotangent, down_t, up):
    devices = lax.axis_size("dp")
    rank, width = down_t.shape[1:]
    piece = 2 * rank // devices
    exchange = functools.partial(
        lax.all_to_all, axis_name="dp", split_axis=0, concat_axis=0, tiled=True
    )
    stack = jnp.concatenate([down_t[0], up[0]], axis=0).reshape(devices, piece, width)
    table = exchange(stack)
    mine = exchange(jnp.take(table, slots, axis=0, mode="clip")).reshape(2 * rank, width)
    down, up_ = mine[:rank], mine[rank:]
    hidden = dot("td,rd->tr", tokens, down).astype(BF16)
    inner = dot("td,rd->tr", cotangent, up_).astype(BF16)
    grad_rows = dot("tr,rd->td", inner, down).astype(BF16)
    terms = jnp.concatenate(
        [dot("tr,td->rd", inner, tokens), dot("tr,td->rd", hidden, cotangent)], axis=0
    ).astype(BF16)
    pieces = exchange(terms.reshape(devices, piece, width))
    onehot = (slots[None, :] == jnp.arange(devices, dtype=I32)[:, None]).astype(BF16)
    summed = dot("kb,bpd->kpd", onehot, pieces) * (1.0 / BLOCK)
    grads = exchange(summed.astype(BF16)).reshape(2, rank, width)
    return grad_rows, grads[:1], grads[1:]


def params(*shapes):
    size = 8 << 20
    for shape, width in shapes:
        extent = width
        for value in shape:
            extent *= value
        size += extent
    return pltpu.CompilerParams(vmem_limit_bytes=size)


def call(kernel, scalars, arrays, outs, scratch=()):
    sizes = [(a.shape, a.dtype.itemsize) for a in arrays]
    sizes += [(o.shape, o.dtype.itemsize) for o in outs]
    sizes += [(s.shape, s.dtype.itemsize) for s in scratch]
    return pl.pallas_call(
        kernel,
        out_shape=outs,
        in_specs=[SMEM] * len(scalars) + [VMEM] * len(arrays),
        out_specs=[VMEM] * len(outs),
        scratch_shapes=[pltpu.VMEM(s.shape, s.dtype) for s in scratch],
        compiler_params=params(*sizes),
    )(*scalars, *arrays)


def split_pieces(places, first, second):
    half = first.shape[0]

    def kernel(places_ref, first_ref, second_ref, *out_refs):
        for r in range(half):
            out_refs[r][0] = first_ref[places_ref[r]]
            out_refs[r][1] = second_ref[places_ref[r]]

    piece = jax.ShapeDtypeStruct((2,) + first.shape[1:], BF16)
    return call(kernel, [places], [first, second], [piece] * half)


def join_pieces(places, pieces):
    half = len(pieces)

    def kernel(places_ref, *refs):
        for r in range(half):
            refs[half][places_ref[r]] = refs[r][...]

    out = jax.ShapeDtypeStruct((half,) + pieces[0].shape, BF16)
    return call(kernel, [places], pieces, [out])[0]


def pick_crossing(index, table, count):
    half = len(table)
    shape = table[0].shape[1:]

    def kernel(index_ref, *refs):
        out_refs, all_ref = refs[half:-1], refs[-1]
        for r in range(half):
            all_ref[r] = refs[r][...]
        for j in range(count):
            for part in range(2):
                out_refs[part][j] = all_ref[index_ref[j], part]

    out = jax.ShapeDtypeStruct((count,) + shape, BF16)
    scratch = jax.ShapeDtypeStruct((half, 2) + shape, BF16)
    return call(kernel, [index], table, [out] * 2, [scratch])


def pick_pieces(index, places, table, part, arrived, terms=None):
    half = len(table)
    count = arrived.shape[0]
    shape = table[0].shape[1:]
    arrays = list(table) + [arrived] + ([] if terms is None else [terms])

    def kernel(index_ref, places_ref, *refs):
        out_refs, all_ref = refs[len(arrays) : -1], refs[-1]
        for r in range(half):
            all_ref[r] = refs[r][part]
        for j in range(count):
            all_ref[half + j] = refs[half][j]
        for r in range(half):
            if terms is None:
                out_refs[r][...] = all_ref[index_ref[r]]
            else:
                out_refs[r][0] = all_ref[index_ref[r]]
                out_refs[r][1] = refs[half + 1][places_ref[r]]

    out = jax.ShapeDtypeStruct(shape if terms is None else (2,) + shape, BF16)
    scratch = jax.ShapeDtypeStruct((half + count,) + shape, BF16)
    return call(kernel, [index, places], arrays, [out] * half, [scratch])


def lower(ref):
    return ref[1] if len(ref.shape) == 3 else ref[...]


def upper(ref):
    return ref[0] if len(ref.shape) == 3 else ref[...]


def sum_stacked(index, pieces, count):
    half = len(pieces)
    shape = pieces[0].shape[-2:]

    def kernel(index_ref, *refs):
        out_ref, total_ref = refs[half:]
        total_ref[...] = jnp.zeros_like(total_ref)
        for r in range(half):
            place = index_ref[r]
            total_ref[place] = total_ref[place] + lower(refs[r]).astype(F32)
        for k in range(count):
            out_ref[k] = total_ref[k].astype(BF16)

    out = jax.ShapeDtypeStruct((count,) + shape, BF16)
    scratch = jax.ShapeDtypeStruct((half + 1,) + shape, F32)
    return call(kernel, [index], pieces, [out], [scratch])[0]


def sum_pieces(index, arrived_index, places, pieces, arrived):
    half = len(pieces)
    count = arrived.shape[0]
    shape = pieces[0].shape[-2:]

    def kernel(index_ref, arrived_index_ref, places_ref, *refs):
        out_refs, total_ref = refs[half + 1 : -1], refs[-1]
        total_ref[...] = jnp.zeros_like(total_ref)
        for r in range(half):
            place = index_ref[r]
            total_ref[place] = total_ref[place] + lower(refs[r]).astype(F32)
        for j in range(count):
            place = arrived_index_ref[j]
            total_ref[place] = total_ref[place] + refs[half][j].astype(F32)
        for r in range(half):
            out_refs[r][...] = (total_ref[places_ref[r]] * (1.0 / BLOCK)).astype(BF16)

    out = jax.ShapeDtypeStruct(shape, BF16)
    scratch = jax.ShapeDtypeStruct((half + 1,) + shape, F32)
    return call(
        kernel, [index, arrived_index, places], list(pieces) + [arrived], [out] * half, [scratch]
    )


def term_pieces(places, pieces, first, second, whole):
    half = len(pieces)
    rows, width = first.shape
    piece = pieces[0].shape[-2]
    rank = half * piece
    step = max(s for s in (128, 256, 512, 640, 1024) if width % s == 0)

    def kernel(places_ref, *refs):
        first_ref, second_ref = refs[half : half + 2]
        if whole:
            adapter_ref, term_ref = refs[half + 2 :]
        else:
            projected_ref, out_refs = refs[half + 2], refs[half + 3 : -2]
            adapter_ref, term_ref = refs[-2:]
        for r in range(half):
            adapter_ref[places_ref[r]] = upper(refs[r])
        total = jnp.zeros((rows, rank), F32)
        for low in range(0, width, step):
            total += lax.dot_general(
                first_ref[:, low : low + step],
                adapter_ref[:, :, low : low + step].reshape(rank, step),
                (((1,), (1,)), ((), ())),
                preferred_element_type=F32,
            )
        if not whole:
            projected_ref[...] = total.astype(BF16)
        turned = total.T.astype(BF16)
        for low in range(0, width, step):
            term = jnp.dot(turned, second_ref[:, low : low + step], preferred_element_type=F32)
            term_ref[:, :, low : low + step] = term.astype(BF16).reshape(half, piece, step)
        if not whole:
            for r in range(half):
                out_refs[r][...] = term_ref[places_ref[r]]

    stacked = jax.ShapeDtypeStruct((half, piece, width), BF16)
    out = jax.ShapeDtypeStruct((piece, width), BF16)
    projected = jax.ShapeDtypeStruct((rows, rank), BF16)
    arrays = list(pieces) + [first, second]
    if whole:
        adapter, term = call(kernel, [places], arrays, [stacked, stacked])
        return adapter.reshape(rank, width), term
    got = call(kernel, [places], arrays, [projected] + [out] * half, [stacked, stacked])
    return got[0], got[1:]


def routes(slots, devices):
    half = devices // 2
    me = lax.axis_index("dp")
    side, own = me // half, me % half
    k = jnp.arange(devices, dtype=I32)
    h = jnp.arange(half, dtype=I32)
    k_side = k // half
    need = jnp.any((slots[:, None] == k[None, :]) & (k_side[:, None] != k_side[None, :]), axis=0)
    before = need[None, :] & (k_side[None, :] == k_side[:, None]) & (k[None, :] < k[:, None])
    place = jnp.sum(before.astype(I32), axis=1)
    high = jnp.sum(jnp.where(need & (k_side == 1), 1, 0))
    low = jnp.sum(jnp.where(need & (k_side == 0), 1, 0))
    mine = need & (k_side == side)
    send = jnp.sum(jnp.where(mine[None, :] & (place[None, :] == h[:, None]), k % half, 0), axis=1)
    count = jnp.where(side == 0, low, high)
    places = own ^ h
    user_slot = jnp.sum(
        jnp.where(k[None, :] == (side * half + places)[:, None], slots[None, :], 0), axis=1
    )
    user_place = jnp.sum(jnp.where(user_slot[:, None] == k[None, :], place[None, :], 0), axis=1)
    local = user_slot // half == side
    return {
        "most": jnp.maximum(low, high),
        "places": places,
        "send": send ^ own,
        "fetch": jnp.where(local, (user_slot % half) ^ own, half + user_place),
        "to_cross": jnp.where(local, half, user_place),
        "to_local": jnp.where(local, user_slot % half, half),
        "to_arrived": jnp.where(h < count, send, half),
    }


def three_step(capacity, route, tokens, cotangent, table):
    devices = lax.axis_size("dp")
    half = devices // 2
    places, fetch = route["places"], route["fetch"]
    pairs = [(i, (i + half) % devices) for i in range(devices)]

    def across(array):
        return lax.ppermute(array, "dp", pairs)

    def collect(pieces, arrived):
        return sum_pieces(route["to_local"], route["to_arrived"], places, pieces, arrived)

    arrived_down, arrived_up = map(across, pick_crossing(route["send"], table, capacity))
    got_down = exchange(pick_pieces(fetch, places, table, 0, arrived_down))
    down, term_up = term_pieces(places, got_down, tokens, cotangent, True)
    got_both = exchange(pick_pieces(fetch, places, table, 1, arrived_up, term_up))
    sums_up = across(sum_stacked(route["to_cross"], got_both, capacity))
    inner, term_down = term_pieces(places, got_both, cotangent, tokens, False)
    pieces_down = exchange(term_down)
    sums_down = across(sum_stacked(route["to_cross"], pieces_down, capacity))
    grad_up = exchange(collect(got_both, sums_up))
    grad_rows = dot("tr,rd->td", inner, down).astype(BF16)
    return grad_rows, collect(pieces_down, sums_down), grad_up


def exchange(pieces):
    devices = lax.axis_size("dp")
    half = len(pieces)
    got = list(pieces)
    for r in (6, 2, 4, 7, 3, 5, 1):
        got[r] = lax.ppermute(pieces[r], "dp", [(i, i ^ r) for i in range(devices)])
    return got


def shards(tokens, cotangent, segments, owner_map, down_t, up):
    devices = lax.axis_size("dp")
    slots = block_slots(segments, owner_map, 1, devices)
    if devices != 16:
        return two_step(slots, tokens, cotangent, down_t, up)
    half = devices // 2
    rank, width = down_t.shape[1:]
    shape = (half, rank // half, width)
    own = lax.axis_index("dp") % half
    places = own ^ jnp.arange(half, dtype=I32)
    table = exchange(split_pieces(places, down_t.reshape(shape), up.reshape(shape)))
    route = routes(slots, devices)
    capacities = [3, 4, 5, half]
    branch = sum((route["most"] > c).astype(I32) for c in capacities[:-1])
    grad_rows, grad_down, grad_up = lax.switch(
        branch,
        [functools.partial(three_step, c) for c in capacities],
        route,
        tokens,
        cotangent,
        table,
    )
    grad_down = exchange(grad_down)
    return (
        grad_rows,
        join_pieces(places, grad_down).reshape(1, rank, width),
        join_pieces(places, grad_up).reshape(1, rank, width),
    )


def solution(mesh):
    in_specs = (
        P(("groups", "dp"), None),
        P(("groups", "dp"), None),
        P("groups", None, None),
        P("groups"),
        P(("groups", "dp"), None, None),
        P(("groups", "dp"), None, None),
    )
    out_specs = (
        P(("groups", "dp"), None),
        P(("groups", "dp"), None, None),
        P(("groups", "dp"), None, None),
    )
    return jax.shard_map(shards, mesh=mesh, in_specs=in_specs, out_specs=out_specs, check_vma=False)
```

```python
import functools

import jax
import jax.numpy as jnp
from jax import lax
from jax.experimental import pallas as pl
from jax.experimental.pallas import tpu as pltpu
from jax.sharding import PartitionSpec as P

BLOCK = 128
F32 = jnp.float32
BF16 = jnp.bfloat16
I32 = jnp.int32
VMEM = pl.BlockSpec(memory_space=pltpu.VMEM)
SMEM = pl.BlockSpec(memory_space=pltpu.SMEM)


def block_slots(segments, owner_map, blocks, count_adapters):
    index = jnp.arange(blocks, dtype=I32)
    ids = segments[:, :, 0]
    starts = segments[:, :, 1]
    counts = segments[:, :, 2]
    inside = (index[None, None, :] >= starts[:, :, None]) & (
        index[None, None, :] < (starts + counts)[:, :, None]
    )
    adapter = jnp.sum(jnp.where(inside, ids[:, :, None], 0), axis=1)
    match = adapter[:, :, None] == jnp.arange(count_adapters, dtype=I32)[None, None, :]
    slots = jnp.sum(jnp.where(match, owner_map[None, None, :], 0), axis=2)
    return slots.reshape(-1)


def dot(spec, a, b):
    return jnp.einsum(spec, a, b, preferred_element_type=F32)


def two_step(slots, tokens, cotangent, down_t, up):
    devices = lax.axis_size("dp")
    rank, width = down_t.shape[1:]
    piece = 2 * rank // devices
    exchange = functools.partial(
        lax.all_to_all, axis_name="dp", split_axis=0, concat_axis=0, tiled=True
    )
    stack = jnp.concatenate([down_t[0], up[0]], axis=0).reshape(devices, piece, width)
    table = exchange(stack)
    mine = exchange(jnp.take(table, slots, axis=0, mode="clip")).reshape(2 * rank, width)
    down, up_ = mine[:rank], mine[rank:]
    hidden = dot("td,rd->tr", tokens, down).astype(BF16)
    inner = dot("td,rd->tr", cotangent, up_).astype(BF16)
    grad_rows = dot("tr,rd->td", inner, down).astype(BF16)
    terms = jnp.concatenate(
        [dot("tr,td->rd", inner, tokens), dot("tr,td->rd", hidden, cotangent)], axis=0
    ).astype(BF16)
    pieces = exchange(terms.reshape(devices, piece, width))
    onehot = (slots[None, :] == jnp.arange(devices, dtype=I32)[:, None]).astype(BF16)
    summed = dot("kb,bpd->kpd", onehot, pieces) * (1.0 / BLOCK)
    grads = exchange(summed.astype(BF16)).reshape(2, rank, width)
    return grad_rows, grads[:1], grads[1:]


def call(kernel, scalars, arrays, outs, scratch=(), after=()):
    size = 4 << 20
    for array in list(arrays) + list(outs) + list(scratch):
        extent = array.dtype.itemsize
        for value in array.shape:
            extent *= value
        size += extent
    return pl.pallas_call(
        kernel,
        out_shape=outs,
        in_specs=[SMEM] * len(scalars)
        + [VMEM] * len(arrays)
        + [pl.BlockSpec(memory_space=pl.ANY)] * len(after),
        out_specs=[VMEM] * len(outs),
        scratch_shapes=[pltpu.VMEM(s.shape, s.dtype) for s in scratch],
        compiler_params=pltpu.CompilerParams(vmem_limit_bytes=size),
    )(*scalars, *arrays, *after)


def stack_of(count, piece, dtype=BF16):
    return jax.ShapeDtypeStruct((count,) + piece, dtype)


def routes(segments, owner_map, devices):
    half = devices // 2
    entries = segments.shape[1]

    def kernel(segments_ref, owner_ref, out_ref, most_ref, slot_ref, need_ref, place_ref):
        side = lax.div(lax.axis_index("dp"), half)
        for d in range(devices):
            need_ref[d] = 0
            adapter = 0
            for e in range(entries):
                start = segments_ref[1, e, d]
                inside = (start <= 0) & (start + segments_ref[2, e, d] > 0)
                adapter += jnp.where(inside, segments_ref[0, e, d], 0)
            slot_ref[d] = owner_ref[adapter]
        for d in range(devices):
            slot = slot_ref[d]
            need_ref[slot] = jnp.where(lax.div(slot, half) != d // half, 1, need_ref[slot])
        for j in range(half):
            out_ref[SEND, j] = 0
            out_ref[ARRIVED, j] = half
        counts = []
        for s in range(2):
            count = jnp.int32(0)
            for k in range(half):
                needed = need_ref[s * half + k]
                place_ref[s * half + k] = count

                @pl.when((side == s) & (needed == 1))
                def _(count=count, k=k):
                    out_ref[SEND, count] = k
                    out_ref[ARRIVED, count] = k

                count += needed
            counts.append(count)
        most_ref[0] = jnp.maximum(counts[0], counts[1])
        for u in range(half):
            slot = slot_ref[side * half + u]
            local = lax.div(slot, half) == side
            place = place_ref[slot]
            own = lax.rem(slot, half)
            out_ref[FETCH, u] = jnp.where(local, own, half + place)
            out_ref[CROSS, u] = jnp.where(local, half, place)
            out_ref[LOCAL, u] = jnp.where(local, own, half)

    return pl.pallas_call(
        kernel,
        out_shape=[jax.ShapeDtypeStruct((5, half), I32), jax.ShapeDtypeStruct((1,), I32)],
        in_specs=[SMEM] * 2,
        out_specs=[SMEM] * 2,
        scratch_shapes=[pltpu.SMEM((devices,), I32)] * 3,
    )(jnp.transpose(segments, (2, 1, 0)), owner_map)


SEND, ARRIVED, FETCH, CROSS, LOCAL = range(5)


def pick_crossing(route, table, count, after=()):
    def kernel(route_ref, table_ref, *refs):
        for j in range(count):
            refs[-1][j] = table_ref[route_ref[SEND, j]]

    return call(kernel, [route], [table], [stack_of(count, table.shape[1:])], after=after)[0]


def pick_pieces(route, table, arrived, terms=None):
    half = table.shape[0]
    piece = table.shape[1:]

    def kernel(route_ref, table_ref, arrived_ref, *refs):
        out_ref = refs[-1]
        for u in range(half):
            target = out_ref.at[u] if terms is None else out_ref.at[u, 0]
            place = route_ref[FETCH, u]

            @pl.when(place < half)
            def _(place=place, target=target):
                target[...] = table_ref[place]

            @pl.when(place >= half)
            def _(place=place, target=target):
                target[...] = arrived_ref[place - half]

            if terms is not None:
                out_ref[u, 1] = refs[0][u]

    arrays = [table, arrived] + ([] if terms is None else [terms])
    out = stack_of(half, piece if terms is None else (2,) + piece)
    return call(kernel, [route], arrays, [out])[0]


def piece_of(ref, place, part):
    return ref[place] if part is None else ref[place, part]


def sum_crossing(route, pieces, part, count):
    half = pieces.shape[0]
    piece = pieces.shape[-2:]

    def kernel(route_ref, pieces_ref, out_ref, total_ref):
        total_ref[...] = jnp.zeros_like(total_ref)
        for u in range(half):
            place = route_ref[CROSS, u]

            @pl.when(place < half)
            def _(place=place, u=u):
                total_ref[place] = total_ref[place] + piece_of(pieces_ref, u, part).astype(F32)

        for k in range(count):
            out_ref[k] = total_ref[k].astype(BF16)

    return call(
        kernel, [route], [pieces], [stack_of(count, piece)], [stack_of(half, piece, F32)]
    )[0]


def sum_pieces(route, pieces, part, arrived):
    half = pieces.shape[0]
    count = arrived.shape[0]
    piece = pieces.shape[-2:]

    def kernel(route_ref, pieces_ref, arrived_ref, out_ref, total_ref):
        total_ref[...] = jnp.zeros_like(total_ref)
        for row, places, ref, which in (
            (LOCAL, half, pieces_ref, part),
            (ARRIVED, count, arrived_ref, None),
        ):
            for u in range(places):
                place = route_ref[row, u]

                @pl.when(place < half)
                def _(place=place, u=u, ref=ref, which=which):
                    total_ref[place] = total_ref[place] + piece_of(ref, u, which).astype(F32)

        for k in range(half):
            out_ref[k] = (total_ref[k] * (1.0 / BLOCK)).astype(BF16)

    return call(
        kernel, [route], [pieces, arrived], [stack_of(half, piece)], [stack_of(half, piece, F32)]
    )[0]


def term_pieces(pieces, first, second, after=()):
    half = pieces.shape[0]
    part = 0 if len(pieces.shape) == 4 else None
    rows, width = first.shape
    piece = pieces.shape[-2]
    rank = half * piece
    step = max(s for s in (128, 256, 512, 640, 1024) if width % s == 0)

    def kernel(pieces_ref, first_ref, second_ref, *refs):
        projected_ref, term_ref = refs[-2:]
        total = jnp.zeros((rows, rank), F32)
        for low in range(0, width, step):
            if part is None:
                adapter = pieces_ref[:, :, low : low + step]
            else:
                adapter = pieces_ref[:, part, :, low : low + step]
            total += lax.dot_general(
                first_ref[:, low : low + step],
                adapter.reshape(rank, step),
                (((1,), (1,)), ((), ())),
                preferred_element_type=F32,
            )
        projected_ref[...] = total.astype(BF16)
        turned = total.T.astype(BF16)
        for low in range(0, width, step):
            term = jnp.dot(turned, second_ref[:, low : low + step], preferred_element_type=F32)
            term_ref[:, :, low : low + step] = term.astype(BF16).reshape(half, piece, step)

    outs = [jax.ShapeDtypeStruct((rows, rank), BF16), stack_of(half, (piece, width))]
    return call(kernel, [], [pieces, first, second], outs, after=after)


def exchange(pieces):
    devices = lax.axis_size("dp")
    half = devices // 2
    groups = [list(range(half)), list(range(half, devices))]
    return lax.all_to_all(
        pieces, "dp", split_axis=0, concat_axis=0, tiled=True, axis_index_groups=groups
    )


def three_step(capacity, route, tokens, cotangent, table_down, up):
    devices = lax.axis_size("dp")
    half = devices // 2
    width = tokens.shape[1]
    pairs = [(i, (i + half) % devices) for i in range(devices)]

    def across(array):
        return lax.ppermute(array, "dp", pairs)

    arrived_down = across(pick_crossing(route, table_down, capacity))
    table_up = exchange(up)
    got_down = exchange(pick_pieces(route, table_down, arrived_down))
    arrived_up = across(pick_crossing(route, table_up, capacity, [arrived_down]))
    _, term_up = term_pieces(got_down, tokens, cotangent)
    got_both = exchange(pick_pieces(route, table_up, arrived_up, term_up))
    crossing_up = sum_crossing(route, got_both, 1, capacity)
    sums_up = across(crossing_up)
    inner, term_down = term_pieces(got_both, cotangent, tokens, [crossing_up])
    pieces_down = exchange(term_down)
    sums_down = across(sum_crossing(route, pieces_down, None, capacity))
    grad_up = exchange(sum_pieces(route, got_both, 1, sums_up))
    grad_rows = dot("tr,rd->td", inner, got_down.reshape(-1, width)).astype(BF16)
    return grad_rows, sum_pieces(route, pieces_down, None, sums_down), grad_up


def shards(tokens, cotangent, segments, owner_map, down_t, up):
    devices = lax.axis_size("dp")
    if devices != 16:
        slots = block_slots(segments, owner_map, 1, devices)
        return two_step(slots, tokens, cotangent, down_t, up)
    half = devices // 2
    rank, width = down_t.shape[1:]
    shape = (half, rank // half, width)
    table_down = exchange(down_t.reshape(shape))
    route, most = routes(segments, owner_map, devices)
    capacities = [3, 4, 5, half]
    branch = sum((most[0] > c).astype(I32) for c in capacities[:-1])
    grad_rows, sums_down, grad_up = lax.switch(
        branch,
        [functools.partial(three_step, c) for c in capacities],
        route,
        tokens,
        cotangent,
        table_down,
        up.reshape(shape),
    )
    grad_down = exchange(sums_down)
    return grad_rows, grad_down.reshape(1, rank, width), grad_up.reshape(1, rank, width)


def solution(mesh):
    in_specs = (
        P(("groups", "dp"), None),
        P(("groups", "dp"), None),
        P("groups", None, None),
        P("groups"),
        P(("groups", "dp"), None, None),
        P(("groups", "dp"), None, None),
    )
    out_specs = (
        P(("groups", "dp"), None),
        P(("groups", "dp"), None, None),
        P(("groups", "dp"), None, None),
    )
    return jax.shard_map(shards, mesh=mesh, in_specs=in_specs, out_specs=out_specs, check_vma=False)
```

```python
import functools

import jax
import jax.numpy as jnp
from jax import lax
from jax.experimental import pallas as pl
from jax.experimental.pallas import tpu as pltpu
from jax.sharding import PartitionSpec as P

BLOCK = 128
F32 = jnp.float32
BF16 = jnp.bfloat16
I32 = jnp.int32
VMEM = pl.BlockSpec(memory_space=pltpu.VMEM)
SMEM = pl.BlockSpec(memory_space=pltpu.SMEM)


def block_slots(segments, owner_map, blocks, count_adapters):
    index = jnp.arange(blocks, dtype=I32)
    ids = segments[:, :, 0]
    starts = segments[:, :, 1]
    counts = segments[:, :, 2]
    inside = (index[None, None, :] >= starts[:, :, None]) & (
        index[None, None, :] < (starts + counts)[:, :, None]
    )
    adapter = jnp.sum(jnp.where(inside, ids[:, :, None], 0), axis=1)
    match = adapter[:, :, None] == jnp.arange(count_adapters, dtype=I32)[None, None, :]
    slots = jnp.sum(jnp.where(match, owner_map[None, None, :], 0), axis=2)
    return slots.reshape(-1)


def dot(spec, a, b):
    return jnp.einsum(spec, a, b, preferred_element_type=F32)


def two_step(slots, tokens, cotangent, down_t, up):
    devices = lax.axis_size("dp")
    rank, width = down_t.shape[1:]
    piece = 2 * rank // devices
    exchange = functools.partial(
        lax.all_to_all, axis_name="dp", split_axis=0, concat_axis=0, tiled=True
    )
    stack = jnp.concatenate([down_t[0], up[0]], axis=0).reshape(devices, piece, width)
    table = exchange(stack)
    mine = exchange(jnp.take(table, slots, axis=0, mode="clip")).reshape(2 * rank, width)
    down, up_ = mine[:rank], mine[rank:]
    hidden = dot("td,rd->tr", tokens, down).astype(BF16)
    inner = dot("td,rd->tr", cotangent, up_).astype(BF16)
    grad_rows = dot("tr,rd->td", inner, down).astype(BF16)
    terms = jnp.concatenate(
        [dot("tr,td->rd", inner, tokens), dot("tr,td->rd", hidden, cotangent)], axis=0
    ).astype(BF16)
    pieces = exchange(terms.reshape(devices, piece, width))
    onehot = (slots[None, :] == jnp.arange(devices, dtype=I32)[:, None]).astype(BF16)
    summed = dot("kb,bpd->kpd", onehot, pieces) * (1.0 / BLOCK)
    grads = exchange(summed.astype(BF16)).reshape(2, rank, width)
    return grad_rows, grads[:1], grads[1:]


def call(kernel, scalars, arrays, outs, scratch=(), after=()):
    size = 4 << 20
    for array in list(arrays) + list(outs) + list(scratch):
        extent = array.dtype.itemsize
        for value in array.shape:
            extent *= value
        size += extent
    given = len(scalars) + len(arrays)
    return pl.pallas_call(
        lambda *refs: kernel(*refs[:given], *refs[given + len(after) :]),
        out_shape=outs,
        in_specs=[SMEM] * len(scalars)
        + [VMEM] * len(arrays)
        + [pl.BlockSpec(memory_space=pl.ANY)] * len(after),
        out_specs=[VMEM] * len(outs),
        scratch_shapes=[pltpu.VMEM(s.shape, s.dtype) for s in scratch],
        compiler_params=pltpu.CompilerParams(vmem_limit_bytes=size),
    )(*scalars, *arrays, *after)


def own_place(half):
    return lax.rem(lax.axis_index("dp"), half)


SEND, ARRIVED, FETCH, CROSS, LOCAL = range(5)


def routes(segments, owner_map, devices):
    half = devices // 2
    entries = segments.shape[1]

    def kernel(segments_ref, owner_ref, out_ref, most_ref, slot_ref, need_ref, place_ref):
        side = lax.div(lax.axis_index("dp"), half)
        own = own_place(half)
        for d in range(devices):
            need_ref[d] = 0
            adapter = 0
            for e in range(entries):
                start = segments_ref[1, e, d]
                inside = (start <= 0) & (start + segments_ref[2, e, d] > 0)
                adapter += jnp.where(inside, segments_ref[0, e, d], 0)
            slot_ref[d] = owner_ref[adapter]
        for d in range(devices):
            slot = slot_ref[d]
            need_ref[slot] = jnp.where(lax.div(slot, half) != d // half, 1, need_ref[slot])
        for j in range(half):
            out_ref[SEND, j] = 0
            out_ref[ARRIVED, j] = half
        counts = []
        for s in range(2):
            count = jnp.int32(0)
            for k in range(half):
                needed = need_ref[s * half + k]
                place_ref[s * half + k] = count

                @pl.when((side == s) & (needed == 1))
                def _(count=count, k=k):
                    out_ref[SEND, count] = own ^ k
                    out_ref[ARRIVED, count] = k

                count += needed
            counts.append(count)
        most_ref[0] = jnp.maximum(counts[0], counts[1])
        for u in range(half):
            slot = slot_ref[side * half + (own ^ u)]
            local = lax.div(slot, half) == side
            place = place_ref[slot]
            k = lax.rem(slot, half)
            out_ref[FETCH, u] = jnp.where(local, own ^ k, half + place)
            out_ref[CROSS, u] = jnp.where(local, half, place)
            out_ref[LOCAL, u] = jnp.where(local, k, half)

    return pl.pallas_call(
        kernel,
        out_shape=[jax.ShapeDtypeStruct((5, half), I32), jax.ShapeDtypeStruct((1,), I32)],
        in_specs=[SMEM] * 2,
        out_specs=[SMEM] * 2,
        scratch_shapes=[pltpu.SMEM((devices,), I32)] * 3,
    )(jnp.transpose(segments, (2, 1, 0)), owner_map)


def split_pieces(first, second):
    half = first.shape[0]

    def kernel(first_ref, second_ref, *out_refs):
        own = own_place(half)
        for r in range(half):
            out_refs[r][0] = first_ref[own ^ r]
            out_refs[r][1] = second_ref[own ^ r]

    piece = jax.ShapeDtypeStruct((2,) + first.shape[1:], BF16)
    return call(kernel, [], [first, second], [piece] * half)


def join_pieces(pieces):
    half = len(pieces)

    def kernel(*refs):
        own = own_place(half)
        for r in range(half):
            refs[half][own ^ r] = refs[r][...]

    out = jax.ShapeDtypeStruct((half,) + pieces[0].shape, BF16)
    return call(kernel, [], pieces, [out])[0]


def pick_crossing(route, table, part, count, after=()):
    half = len(table)
    shape = table[0].shape[1:]

    def kernel(route_ref, *refs):
        out_ref, all_ref = refs[half:]
        for r in range(half):
            all_ref[r] = refs[r][part]
        for j in range(count):
            out_ref[j] = all_ref[route_ref[SEND, j]]

    out = jax.ShapeDtypeStruct((count,) + shape, BF16)
    scratch = jax.ShapeDtypeStruct((half,) + shape, BF16)
    return call(kernel, [route], table, [out], [scratch], after)[0]


def pick_pieces(route, table, part, arrived, terms=None, after=()):
    half = len(table)
    count = arrived.shape[0]
    shape = table[0].shape[1:]
    arrays = list(table) + [arrived] + ([] if terms is None else [terms])

    def kernel(route_ref, *refs):
        out_refs, all_ref = refs[len(arrays) : -1], refs[-1]
        own = own_place(half)
        for r in range(half):
            all_ref[r] = refs[r][part]
        for j in range(count):
            all_ref[half + j] = refs[half][j]
        for r in range(half):
            if terms is None:
                out_refs[r][...] = all_ref[route_ref[FETCH, r]]
            else:
                out_refs[r][0] = all_ref[route_ref[FETCH, r]]
                out_refs[r][1] = refs[half + 1][own ^ r]

    out = jax.ShapeDtypeStruct(shape if terms is None else (2,) + shape, BF16)
    scratch = jax.ShapeDtypeStruct((half + count,) + shape, BF16)
    return call(kernel, [route], arrays, [out] * half, [scratch], after)


def lower(ref):
    return ref[1] if len(ref.shape) == 3 else ref[...]


def upper(ref):
    return ref[0] if len(ref.shape) == 3 else ref[...]


def sum_crossing(route, pieces, count, after=()):
    half = len(pieces)
    shape = pieces[0].shape[-2:]

    def kernel(route_ref, *refs):
        out_ref, total_ref = refs[half:]
        total_ref[...] = jnp.zeros_like(total_ref)
        for r in range(half):
            place = route_ref[CROSS, r]
            total_ref[place] = total_ref[place] + lower(refs[r]).astype(F32)
        for k in range(count):
            out_ref[k] = total_ref[k].astype(BF16)

    out = jax.ShapeDtypeStruct((count,) + shape, BF16)
    scratch = jax.ShapeDtypeStruct((half + 1,) + shape, F32)
    return call(kernel, [route], pieces, [out], [scratch], after)[0]


def sum_pieces(route, pieces, arrived, after=()):
    half = len(pieces)
    count = arrived.shape[0]
    shape = pieces[0].shape[-2:]

    def kernel(route_ref, *refs):
        out_refs, total_ref = refs[half + 1 : -1], refs[-1]
        own = own_place(half)
        total_ref[...] = jnp.zeros_like(total_ref)
        for r in range(half):
            place = route_ref[LOCAL, r]
            total_ref[place] = total_ref[place] + lower(refs[r]).astype(F32)
        for j in range(count):
            place = route_ref[ARRIVED, j]
            total_ref[place] = total_ref[place] + refs[half][j].astype(F32)
        for r in range(half):
            out_refs[r][...] = (total_ref[own ^ r] * (1.0 / BLOCK)).astype(BF16)

    out = jax.ShapeDtypeStruct(shape, BF16)
    scratch = jax.ShapeDtypeStruct((half + 1,) + shape, F32)
    arrays = list(pieces) + [arrived]
    return call(kernel, [route], arrays, [out] * half, [scratch], after)


def term_pieces(pieces, first, second, whole, after=()):
    half = len(pieces)
    rows, width = first.shape
    piece = pieces[0].shape[-2]
    rank = half * piece
    step = max(s for s in (128, 256, 512, 640, 1024) if width % s == 0)

    def kernel(*refs):
        own = own_place(half)
        first_ref, second_ref = refs[half : half + 2]
        if whole:
            adapter_ref, term_ref = refs[half + 2 :]
        else:
            projected_ref, out_refs = refs[half + 2], refs[half + 3 : -2]
            adapter_ref, term_ref = refs[-2:]
        for r in range(half):
            adapter_ref[own ^ r] = upper(refs[r])
        total = jnp.zeros((rows, rank), F32)
        for low in range(0, width, step):
            total += lax.dot_general(
                first_ref[:, low : low + step],
                adapter_ref[:, :, low : low + step].reshape(rank, step),
                (((1,), (1,)), ((), ())),
                preferred_element_type=F32,
            )
        if not whole:
            projected_ref[...] = total.astype(BF16)
        turned = total.T.astype(BF16)
        for low in range(0, width, step):
            term = jnp.dot(turned, second_ref[:, low : low + step], preferred_element_type=F32)
            term_ref[:, :, low : low + step] = term.astype(BF16).reshape(half, piece, step)
        if not whole:
            for r in range(half):
                out_refs[r][...] = term_ref[own ^ r]

    stacked = jax.ShapeDtypeStruct((half, piece, width), BF16)
    out = jax.ShapeDtypeStruct((piece, width), BF16)
    projected = jax.ShapeDtypeStruct((rows, rank), BF16)
    arrays = list(pieces) + [first, second]
    if whole:
        adapter, term = call(kernel, [], arrays, [stacked, stacked], after=after)
        return adapter.reshape(rank, width), term
    got = call(
        kernel, [], arrays, [projected] + [out] * half, [stacked, stacked], after
    )
    return got[0], got[1:]


def three_step(capacity, route, tokens, cotangent, table):
    devices = lax.axis_size("dp")
    half = devices // 2
    pairs = [(i, (i + half) % devices) for i in range(devices)]

    def across(array):
        return lax.ppermute(array, "dp", pairs)

    arrived_down = across(pick_crossing(route, table, 0, capacity))
    crossing_up = pick_crossing(route, table, 1, capacity, [arrived_down])
    arrived_up = across(crossing_up)
    got_down = exchange(pick_pieces(route, table, 0, arrived_down, after=[crossing_up]))
    down, term_up = term_pieces(got_down, tokens, cotangent, True)
    got_both = exchange(pick_pieces(route, table, 1, arrived_up, term_up))
    crossing_sums_up = sum_crossing(route, got_both, capacity)
    sums_up = across(crossing_sums_up)
    inner, term_down = term_pieces(got_both, cotangent, tokens, False, [crossing_sums_up])
    pieces_down = exchange(term_down)
    crossing_sums_down = sum_crossing(route, pieces_down, capacity, [sums_up])
    sums_down = across(crossing_sums_down)
    grad_up = exchange(sum_pieces(route, got_both, sums_up, [crossing_sums_down]))
    grad_rows = dot("tr,rd->td", inner, down).astype(BF16)
    return grad_rows, sum_pieces(route, pieces_down, sums_down), grad_up


def exchange(pieces):
    devices = lax.axis_size("dp")
    half = len(pieces)
    got = list(pieces)
    for r in (6, 2, 4, 7, 3, 5, 1):
        got[r] = lax.ppermute(pieces[r], "dp", [(i, i ^ r) for i in range(devices)])
    return got


def shards(tokens, cotangent, segments, owner_map, down_t, up):
    devices = lax.axis_size("dp")
    if devices != 16:
        slots = block_slots(segments, owner_map, 1, devices)
        return two_step(slots, tokens, cotangent, down_t, up)
    half = devices // 2
    rank, width = down_t.shape[1:]
    shape = (half, rank // half, width)
    table = exchange(split_pieces(down_t.reshape(shape), up.reshape(shape)))
    route, most = routes(segments, owner_map, devices)
    capacities = [3, 4, 5, half]
    branch = sum((most[0] > c).astype(I32) for c in capacities[:-1])
    grad_rows, grad_down, grad_up = lax.switch(
        branch,
        [functools.partial(three_step, c) for c in capacities],
        route,
        tokens,
        cotangent,
        table,
    )
    grad_down = exchange(grad_down)
    return (
        grad_rows,
        join_pieces(grad_down).reshape(1, rank, width),
        join_pieces(grad_up).reshape(1, rank, width),
    )


def solution(mesh):
    in_specs = (
        P(("groups", "dp"), None),
        P(("groups", "dp"), None),
        P("groups", None, None),
        P("groups"),
        P(("groups", "dp"), None, None),
        P(("groups", "dp"), None, None),
    )
    out_specs = (
        P(("groups", "dp"), None),
        P(("groups", "dp"), None, None),
        P(("groups", "dp"), None, None),
    )
    return jax.shard_map(shards, mesh=mesh, in_specs=in_specs, out_specs=out_specs, check_vma=False)
```

```python
import functools

import jax
import jax.numpy as jnp
from jax import lax
from jax.experimental import pallas as pl
from jax.experimental.pallas import tpu as pltpu
from jax.sharding import PartitionSpec as P

BLOCK = 128
F32 = jnp.float32
BF16 = jnp.bfloat16
I32 = jnp.int32
VMEM = pl.BlockSpec(memory_space=pltpu.VMEM)
SMEM = pl.BlockSpec(memory_space=pltpu.SMEM)


def block_slots(segments, owner_map, blocks, count_adapters):
    index = jnp.arange(blocks, dtype=I32)
    ids = segments[:, :, 0]
    starts = segments[:, :, 1]
    counts = segments[:, :, 2]
    inside = (index[None, None, :] >= starts[:, :, None]) & (
        index[None, None, :] < (starts + counts)[:, :, None]
    )
    adapter = jnp.sum(jnp.where(inside, ids[:, :, None], 0), axis=1)
    match = adapter[:, :, None] == jnp.arange(count_adapters, dtype=I32)[None, None, :]
    slots = jnp.sum(jnp.where(match, owner_map[None, None, :], 0), axis=2)
    return slots.reshape(-1)


def dot(spec, a, b):
    return jnp.einsum(spec, a, b, preferred_element_type=F32)


def two_step(slots, tokens, cotangent, down_t, up):
    devices = lax.axis_size("dp")
    rank, width = down_t.shape[1:]
    piece = 2 * rank // devices
    exchange = functools.partial(
        lax.all_to_all, axis_name="dp", split_axis=0, concat_axis=0, tiled=True
    )
    stack = jnp.concatenate([down_t[0], up[0]], axis=0).reshape(devices, piece, width)
    table = exchange(stack)
    mine = exchange(jnp.take(table, slots, axis=0, mode="clip")).reshape(2 * rank, width)
    down, up_ = mine[:rank], mine[rank:]
    hidden = dot("td,rd->tr", tokens, down).astype(BF16)
    inner = dot("td,rd->tr", cotangent, up_).astype(BF16)
    grad_rows = dot("tr,rd->td", inner, down).astype(BF16)
    terms = jnp.concatenate(
        [dot("tr,td->rd", inner, tokens), dot("tr,td->rd", hidden, cotangent)], axis=0
    ).astype(BF16)
    pieces = exchange(terms.reshape(devices, piece, width))
    onehot = (slots[None, :] == jnp.arange(devices, dtype=I32)[:, None]).astype(BF16)
    summed = dot("kb,bpd->kpd", onehot, pieces) * (1.0 / BLOCK)
    grads = exchange(summed.astype(BF16)).reshape(2, rank, width)
    return grad_rows, grads[:1], grads[1:]


def call(kernel, scalars, arrays, outs, scratch=(), after=()):
    size = 4 << 20
    for array in list(arrays) + list(outs) + list(scratch):
        extent = array.dtype.itemsize
        for value in array.shape:
            extent *= value
        size += extent
    given = len(scalars) + len(arrays)
    return pl.pallas_call(
        lambda *refs: kernel(*refs[:given], *refs[given + len(after) :]),
        out_shape=outs,
        in_specs=[SMEM] * len(scalars)
        + [VMEM] * len(arrays)
        + [pl.BlockSpec(memory_space=pl.ANY)] * len(after),
        out_specs=[VMEM] * len(outs),
        scratch_shapes=[pltpu.VMEM(s.shape, s.dtype) for s in scratch],
        compiler_params=pltpu.CompilerParams(vmem_limit_bytes=size),
    )(*scalars, *arrays, *after)


def own_place(half):
    return lax.rem(lax.axis_index("dp"), half)


SEND, ARRIVED, FETCH, CROSS, LOCAL = range(5)


def routes(segments, owner_map, devices):
    half = devices // 2
    entries = segments.shape[1]

    def kernel(segments_ref, owner_ref, out_ref, most_ref, slot_ref, need_ref, place_ref):
        side = lax.div(lax.axis_index("dp"), half)
        own = own_place(half)
        for d in range(devices):
            need_ref[d] = 0
            adapter = 0
            for e in range(entries):
                start = segments_ref[1, e, d]
                inside = (start <= 0) & (start + segments_ref[2, e, d] > 0)
                adapter += jnp.where(inside, segments_ref[0, e, d], 0)
            slot_ref[d] = owner_ref[adapter]
        for d in range(devices):
            slot = slot_ref[d]
            need_ref[slot] = jnp.where(lax.div(slot, half) != d // half, 1, need_ref[slot])
        for j in range(half):
            out_ref[SEND, j] = 0
            out_ref[ARRIVED, j] = half
        counts = []
        for s in range(2):
            count = jnp.int32(0)
            for k in range(half):
                needed = need_ref[s * half + k]
                place_ref[s * half + k] = count

                @pl.when((side == s) & (needed == 1))
                def _(count=count, k=k):
                    out_ref[SEND, count] = own ^ k
                    out_ref[ARRIVED, count] = k

                count += needed
            counts.append(count)
        most_ref[0] = jnp.maximum(counts[0], counts[1])
        for u in range(half):
            slot = slot_ref[side * half + (own ^ u)]
            local = lax.div(slot, half) == side
            place = place_ref[slot]
            k = lax.rem(slot, half)
            out_ref[FETCH, u] = jnp.where(local, own ^ k, half + place)
            out_ref[CROSS, u] = jnp.where(local, half, place)
            out_ref[LOCAL, u] = jnp.where(local, k, half)

    return pl.pallas_call(
        kernel,
        out_shape=[jax.ShapeDtypeStruct((5, half), I32), jax.ShapeDtypeStruct((1,), I32)],
        in_specs=[SMEM] * 2,
        out_specs=[SMEM] * 2,
        scratch_shapes=[pltpu.SMEM((devices,), I32)] * 3,
    )(jnp.transpose(segments, (2, 1, 0)), owner_map)


def split_pieces(stacked, after=()):
    half = stacked.shape[0]

    def kernel(stacked_ref, *out_refs):
        own = own_place(half)
        for r in range(half):
            out_refs[r][...] = stacked_ref[own ^ r]

    piece = jax.ShapeDtypeStruct(stacked.shape[1:], BF16)
    return call(kernel, [], [stacked], [piece] * half, after=after)


def join_pieces(pieces):
    half = len(pieces)

    def kernel(*refs):
        own = own_place(half)
        for r in range(half):
            refs[half][own ^ r] = refs[r][...]

    out = jax.ShapeDtypeStruct((half,) + pieces[0].shape, BF16)
    return call(kernel, [], pieces, [out])[0]


def pick_crossing(route, table, count, after=()):
    half = len(table)
    shape = table[0].shape

    def kernel(route_ref, *refs):
        out_ref, all_ref = refs[half:]
        for r in range(half):
            all_ref[r] = refs[r][...]
        for j in range(count):
            out_ref[j] = all_ref[route_ref[SEND, j]]

    out = jax.ShapeDtypeStruct((count,) + shape, BF16)
    scratch = jax.ShapeDtypeStruct((half,) + shape, BF16)
    return call(kernel, [route], table, [out], [scratch], after)[0]


def pick_pieces(route, table, arrived, terms=None, after=()):
    half = len(table)
    count = arrived.shape[0]
    shape = table[0].shape
    arrays = list(table) + [arrived] + ([] if terms is None else [terms])

    def kernel(route_ref, *refs):
        out_refs, all_ref = refs[len(arrays) : -1], refs[-1]
        own = own_place(half)
        for r in range(half):
            all_ref[r] = refs[r][...]
        for j in range(count):
            all_ref[half + j] = refs[half][j]
        for r in range(half):
            if terms is None:
                out_refs[r][...] = all_ref[route_ref[FETCH, r]]
            else:
                out_refs[r][0] = all_ref[route_ref[FETCH, r]]
                out_refs[r][1] = refs[half + 1][own ^ r]

    out = jax.ShapeDtypeStruct(shape if terms is None else (2,) + shape, BF16)
    scratch = jax.ShapeDtypeStruct((half + count,) + shape, BF16)
    return call(kernel, [route], arrays, [out] * half, [scratch], after)


def lower(ref):
    return ref[1] if len(ref.shape) == 3 else ref[...]


def upper(ref):
    return ref[0] if len(ref.shape) == 3 else ref[...]


def sum_crossing(route, pieces, count, after=()):
    half = len(pieces)
    shape = pieces[0].shape[-2:]

    def kernel(route_ref, *refs):
        out_ref, total_ref = refs[half:]
        total_ref[...] = jnp.zeros_like(total_ref)
        for r in range(half):
            place = route_ref[CROSS, r]
            total_ref[place] = total_ref[place] + lower(refs[r]).astype(F32)
        for k in range(count):
            out_ref[k] = total_ref[k].astype(BF16)

    out = jax.ShapeDtypeStruct((count,) + shape, BF16)
    scratch = jax.ShapeDtypeStruct((half + 1,) + shape, F32)
    return call(kernel, [route], pieces, [out], [scratch], after)[0]


def sum_pieces(route, pieces, arrived, after=()):
    half = len(pieces)
    count = arrived.shape[0]
    shape = pieces[0].shape[-2:]

    def kernel(route_ref, *refs):
        out_refs, total_ref = refs[half + 1 : -1], refs[-1]
        own = own_place(half)
        total_ref[...] = jnp.zeros_like(total_ref)
        for r in range(half):
            place = route_ref[LOCAL, r]
            total_ref[place] = total_ref[place] + lower(refs[r]).astype(F32)
        for j in range(count):
            place = route_ref[ARRIVED, j]
            total_ref[place] = total_ref[place] + refs[half][j].astype(F32)
        for r in range(half):
            out_refs[r][...] = (total_ref[own ^ r] * (1.0 / BLOCK)).astype(BF16)

    out = jax.ShapeDtypeStruct(shape, BF16)
    scratch = jax.ShapeDtypeStruct((half + 1,) + shape, F32)
    arrays = list(pieces) + [arrived]
    return call(kernel, [route], arrays, [out] * half, [scratch], after)


def term_pieces(pieces, first, second, whole, after=()):
    half = len(pieces)
    rows, width = first.shape
    piece = pieces[0].shape[-2]
    rank = half * piece
    step = max(s for s in (128, 256, 512, 640, 1024) if width % s == 0)

    def kernel(*refs):
        own = own_place(half)
        first_ref, second_ref = refs[half : half + 2]
        if whole:
            adapter_ref, term_ref = refs[half + 2 :]
        else:
            projected_ref, out_refs = refs[half + 2], refs[half + 3 : -2]
            adapter_ref, term_ref = refs[-2:]
        for r in range(half):
            adapter_ref[own ^ r] = upper(refs[r])
        total = jnp.zeros((rows, rank), F32)
        for low in range(0, width, step):
            total += lax.dot_general(
                first_ref[:, low : low + step],
                adapter_ref[:, :, low : low + step].reshape(rank, step),
                (((1,), (1,)), ((), ())),
                preferred_element_type=F32,
            )
        if not whole:
            projected_ref[...] = total.astype(BF16)
        turned = total.T.astype(BF16)
        for low in range(0, width, step):
            term = jnp.dot(turned, second_ref[:, low : low + step], preferred_element_type=F32)
            term_ref[:, :, low : low + step] = term.astype(BF16).reshape(half, piece, step)
        if not whole:
            for r in range(half):
                out_refs[r][...] = term_ref[own ^ r]

    stacked = jax.ShapeDtypeStruct((half, piece, width), BF16)
    out = jax.ShapeDtypeStruct((piece, width), BF16)
    projected = jax.ShapeDtypeStruct((rows, rank), BF16)
    arrays = list(pieces) + [first, second]
    if whole:
        adapter, term = call(kernel, [], arrays, [stacked, stacked], after=after)
        return adapter.reshape(rank, width), term
    got = call(
        kernel, [], arrays, [projected] + [out] * half, [stacked, stacked], after
    )
    return got[0], got[1:]


def three_step(capacity, route, tokens, cotangent, table_down, up):
    devices = lax.axis_size("dp")
    half = devices // 2
    pairs = [(i, (i + half) % devices) for i in range(devices)]

    def across(array):
        return lax.ppermute(array, "dp", pairs)

    crossing_down = pick_crossing(route, table_down, capacity)
    arrived_down = across(crossing_down)
    table_up = exchange(split_pieces(up, [crossing_down]))
    crossing_up = pick_crossing(route, table_up, capacity, [arrived_down])
    arrived_up = across(crossing_up)
    got_down = exchange(pick_pieces(route, table_down, arrived_down, after=[crossing_up]))
    down, term_up = term_pieces(got_down, tokens, cotangent, True)
    got_both = exchange(pick_pieces(route, table_up, arrived_up, term_up))
    crossing_sums_up = sum_crossing(route, got_both, capacity)
    sums_up = across(crossing_sums_up)
    inner, term_down = term_pieces(got_both, cotangent, tokens, False, [crossing_sums_up])
    pieces_down = exchange(term_down)
    crossing_sums_down = sum_crossing(route, pieces_down, capacity, [sums_up])
    sums_down = across(crossing_sums_down)
    grad_up = exchange(sum_pieces(route, got_both, sums_up, [crossing_sums_down]))
    grad_rows = dot("tr,rd->td", inner, down).astype(BF16)
    return grad_rows, sum_pieces(route, pieces_down, sums_down), grad_up


def exchange(pieces):
    devices = lax.axis_size("dp")
    half = len(pieces)
    got = list(pieces)
    for r in (6, 2, 4, 7, 3, 5, 1):
        got[r] = lax.ppermute(pieces[r], "dp", [(i, i ^ r) for i in range(devices)])
    return got


def shards(tokens, cotangent, segments, owner_map, down_t, up):
    devices = lax.axis_size("dp")
    if devices != 16:
        slots = block_slots(segments, owner_map, 1, devices)
        return two_step(slots, tokens, cotangent, down_t, up)
    half = devices // 2
    rank, width = down_t.shape[1:]
    shape = (half, rank // half, width)
    table_down = exchange(split_pieces(down_t.reshape(shape)))
    route, most = routes(segments, owner_map, devices)
    capacities = [3, 4, 5, half]
    branch = sum((most[0] > c).astype(I32) for c in capacities[:-1])
    grad_rows, grad_down, grad_up = lax.switch(
        branch,
        [functools.partial(three_step, c) for c in capacities],
        route,
        tokens,
        cotangent,
        table_down,
        up.reshape(shape),
    )
    grad_down = exchange(grad_down)
    return (
        grad_rows,
        join_pieces(grad_down).reshape(1, rank, width),
        join_pieces(grad_up).reshape(1, rank, width),
    )


def solution(mesh):
    in_specs = (
        P(("groups", "dp"), None),
        P(("groups", "dp"), None),
        P("groups", None, None),
        P("groups"),
        P(("groups", "dp"), None, None),
        P(("groups", "dp"), None, None),
    )
    out_specs = (
        P(("groups", "dp"), None),
        P(("groups", "dp"), None, None),
        P(("groups", "dp"), None, None),
    )
    return jax.shard_map(shards, mesh=mesh, in_specs=in_specs, out_specs=out_specs, check_vma=False)
```

```python
import functools

import jax
import jax.numpy as jnp
from jax import lax
from jax.experimental import pallas as pl
from jax.experimental.pallas import tpu as pltpu
from jax.sharding import PartitionSpec as P

BLOCK = 128
F32 = jnp.float32
BF16 = jnp.bfloat16
I32 = jnp.int32
VMEM = pl.BlockSpec(memory_space=pltpu.VMEM)
SMEM = pl.BlockSpec(memory_space=pltpu.SMEM)


def block_slots(segments, owner_map, blocks, count_adapters):
    index = jnp.arange(blocks, dtype=I32)
    ids = segments[:, :, 0]
    starts = segments[:, :, 1]
    counts = segments[:, :, 2]
    inside = (index[None, None, :] >= starts[:, :, None]) & (
        index[None, None, :] < (starts + counts)[:, :, None]
    )
    adapter = jnp.sum(jnp.where(inside, ids[:, :, None], 0), axis=1)
    match = adapter[:, :, None] == jnp.arange(count_adapters, dtype=I32)[None, None, :]
    slots = jnp.sum(jnp.where(match, owner_map[None, None, :], 0), axis=2)
    return slots.reshape(-1)


def dot(spec, a, b):
    return jnp.einsum(spec, a, b, preferred_element_type=F32)


def two_step(slots, tokens, cotangent, down_t, up):
    devices = lax.axis_size("dp")
    rank, width = down_t.shape[1:]
    piece = 2 * rank // devices
    exchange = functools.partial(
        lax.all_to_all, axis_name="dp", split_axis=0, concat_axis=0, tiled=True
    )
    stack = jnp.concatenate([down_t[0], up[0]], axis=0).reshape(devices, piece, width)
    table = exchange(stack)
    mine = exchange(jnp.take(table, slots, axis=0, mode="clip")).reshape(2 * rank, width)
    down, up_ = mine[:rank], mine[rank:]
    hidden = dot("td,rd->tr", tokens, down).astype(BF16)
    inner = dot("td,rd->tr", cotangent, up_).astype(BF16)
    grad_rows = dot("tr,rd->td", inner, down).astype(BF16)
    terms = jnp.concatenate(
        [dot("tr,td->rd", inner, tokens), dot("tr,td->rd", hidden, cotangent)], axis=0
    ).astype(BF16)
    pieces = exchange(terms.reshape(devices, piece, width))
    onehot = (slots[None, :] == jnp.arange(devices, dtype=I32)[:, None]).astype(BF16)
    summed = dot("kb,bpd->kpd", onehot, pieces) * (1.0 / BLOCK)
    grads = exchange(summed.astype(BF16)).reshape(2, rank, width)
    return grad_rows, grads[:1], grads[1:]


STEPS = ((0, 0), (2, 4), (4, 2), (6, 6), (3, 5), (5, 3), (7, 7), (1, 1))


def call(kernel, scalars, arrays, outs, scratch=(), after=()):
    size = 4 << 20
    for array in list(arrays) + list(outs) + list(scratch):
        extent = array.dtype.itemsize
        for value in array.shape:
            extent *= value
        size += extent
    given = len(scalars) + len(arrays)
    return pl.pallas_call(
        lambda *refs: kernel(*refs[:given], *refs[given + len(after) :]),
        out_shape=outs,
        in_specs=[SMEM] * len(scalars)
        + [VMEM] * len(arrays)
        + [pl.BlockSpec(memory_space=pl.ANY)] * len(after),
        out_specs=[VMEM] * len(outs),
        scratch_shapes=[pltpu.VMEM(s.shape, s.dtype) for s in scratch],
        compiler_params=pltpu.CompilerParams(vmem_limit_bytes=size),
    )(*scalars, *arrays, *after)


def partners(sending):
    own = lax.rem(lax.axis_index("dp"), len(STEPS))
    places = []
    for a, b in STEPS:
        if a % 2 and not sending:
            a, b = b, a
        places.append(own ^ jnp.where(own % 2 == 1, b, a) if a != b else own ^ a)
    return places


SEND, ARRIVED, FETCH, CROSS, LOCAL = range(5)


def routes(segments, owner_map, devices):
    half = devices // 2
    entries = segments.shape[1]

    def kernel(segments_ref, owner_ref, out_ref, most_ref, slot_ref, need_ref, place_ref):
        side = lax.div(lax.axis_index("dp"), half)
        for d in range(devices):
            need_ref[d] = 0
            adapter = 0
            for e in range(entries):
                start = segments_ref[1, e, d]
                inside = (start <= 0) & (start + segments_ref[2, e, d] > 0)
                adapter += jnp.where(inside, segments_ref[0, e, d], 0)
            slot_ref[d] = owner_ref[adapter]
        for d in range(devices):
            slot = slot_ref[d]
            need_ref[slot] = jnp.where(lax.div(slot, half) != d // half, 1, need_ref[slot])
        for j in range(half):
            out_ref[SEND, j] = 0
            out_ref[ARRIVED, j] = half
        counts = []
        for s in range(2):
            count = jnp.int32(0)
            for k in range(half):
                needed = need_ref[s * half + k]
                place_ref[s * half + k] = count

                @pl.when((side == s) & (needed == 1))
                def _(count=count, k=k):
                    out_ref[SEND, count] = k
                    out_ref[ARRIVED, count] = k

                count += needed
            counts.append(count)
        most_ref[0] = jnp.maximum(counts[0], counts[1])
        for u in range(half):
            slot = slot_ref[side * half + u]
            local = lax.div(slot, half) == side
            place = place_ref[slot]
            k = lax.rem(slot, half)
            out_ref[FETCH, u] = jnp.where(local, k, half + place)
            out_ref[CROSS, u] = jnp.where(local, half, place)
            out_ref[LOCAL, u] = jnp.where(local, k, half)

    return pl.pallas_call(
        kernel,
        out_shape=[jax.ShapeDtypeStruct((5, half), I32), jax.ShapeDtypeStruct((1,), I32)],
        in_specs=[SMEM] * 2,
        out_specs=[SMEM] * 2,
        scratch_shapes=[pltpu.SMEM((devices,), I32)] * 3,
    )(jnp.transpose(segments, (2, 1, 0)), owner_map)


def split_pieces(stacked, after=()):
    half = stacked.shape[0]

    def kernel(stacked_ref, *out_refs):
        for ref, p in zip(out_refs, partners(True)):
            ref[...] = stacked_ref[p]

    piece = jax.ShapeDtypeStruct(stacked.shape[1:], BF16)
    return call(kernel, [], [stacked], [piece] * half, after=after)


def join_pieces(pieces):
    half = len(pieces)

    def kernel(*refs):
        for ref, p in zip(refs, partners(False)):
            refs[half][p] = ref[...]

    out = jax.ShapeDtypeStruct((half,) + pieces[0].shape, BF16)
    return call(kernel, [], pieces, [out])[0]


def pick_crossing(route, table, count, after=()):
    half = len(table)
    shape = table[0].shape

    def kernel(route_ref, *refs):
        out_ref, all_ref = refs[half:]
        for ref, p in zip(refs, partners(False)):
            all_ref[p] = ref[...]
        for j in range(count):
            out_ref[j] = all_ref[route_ref[SEND, j]]

    out = jax.ShapeDtypeStruct((count,) + shape, BF16)
    scratch = jax.ShapeDtypeStruct((half,) + shape, BF16)
    return call(kernel, [route], table, [out], [scratch], after)[0]


def pick_pieces(route, table, arrived, terms=None, after=()):
    half = len(table)
    count = arrived.shape[0]
    shape = table[0].shape
    arrays = list(table) + [arrived] + ([] if terms is None else [terms])

    def kernel(route_ref, *refs):
        out_refs, all_ref = refs[len(arrays) : -1], refs[-1]
        for ref, p in zip(refs[:half], partners(False)):
            all_ref[p] = ref[...]
        for j in range(count):
            all_ref[half + j] = refs[half][j]
        for ref, p in zip(out_refs, partners(True)):
            if terms is None:
                ref[...] = all_ref[route_ref[FETCH, p]]
            else:
                ref[0] = all_ref[route_ref[FETCH, p]]
                ref[1] = refs[half + 1][p]

    out = jax.ShapeDtypeStruct(shape if terms is None else (2,) + shape, BF16)
    scratch = jax.ShapeDtypeStruct((half + count,) + shape, BF16)
    return call(kernel, [route], arrays, [out] * half, [scratch], after)


def lower(ref):
    return ref[1] if len(ref.shape) == 3 else ref[...]


def upper(ref):
    return ref[0] if len(ref.shape) == 3 else ref[...]


def sum_crossing(route, pieces, count, after=()):
    half = len(pieces)
    shape = pieces[0].shape[-2:]

    def kernel(route_ref, *refs):
        out_ref, total_ref = refs[half:]
        total_ref[...] = jnp.zeros_like(total_ref)
        for ref, p in zip(refs[:half], partners(False)):
            place = route_ref[CROSS, p]
            total_ref[place] = total_ref[place] + lower(ref).astype(F32)
        for k in range(count):
            out_ref[k] = total_ref[k].astype(BF16)

    out = jax.ShapeDtypeStruct((count,) + shape, BF16)
    scratch = jax.ShapeDtypeStruct((half + 1,) + shape, F32)
    return call(kernel, [route], pieces, [out], [scratch], after)[0]


def sum_pieces(route, pieces, arrived, after=()):
    half = len(pieces)
    count = arrived.shape[0]
    shape = pieces[0].shape[-2:]

    def kernel(route_ref, *refs):
        out_refs, total_ref = refs[half + 1 : -1], refs[-1]
        total_ref[...] = jnp.zeros_like(total_ref)
        for ref, p in zip(refs[:half], partners(False)):
            place = route_ref[LOCAL, p]
            total_ref[place] = total_ref[place] + lower(ref).astype(F32)
        for j in range(count):
            place = route_ref[ARRIVED, j]
            total_ref[place] = total_ref[place] + refs[half][j].astype(F32)
        for ref, p in zip(out_refs, partners(True)):
            ref[...] = (total_ref[p] * (1.0 / BLOCK)).astype(BF16)

    out = jax.ShapeDtypeStruct(shape, BF16)
    scratch = jax.ShapeDtypeStruct((half + 1,) + shape, F32)
    arrays = list(pieces) + [arrived]
    return call(kernel, [route], arrays, [out] * half, [scratch], after)


def term_pieces(pieces, first, second, whole, after=()):
    half = len(pieces)
    rows, width = first.shape
    piece = pieces[0].shape[-2]
    rank = half * piece
    step = max(s for s in (128, 256, 512, 640, 1024) if width % s == 0)

    def kernel(*refs):
        first_ref, second_ref = refs[half : half + 2]
        if whole:
            adapter_ref, term_ref = refs[half + 2 :]
        else:
            projected_ref, out_refs = refs[half + 2], refs[half + 3 : -2]
            adapter_ref, term_ref = refs[-2:]
        for ref, p in zip(refs[:half], partners(False)):
            adapter_ref[p] = upper(ref)
        total = jnp.zeros((rows, rank), F32)
        for low in range(0, width, step):
            total += lax.dot_general(
                first_ref[:, low : low + step],
                adapter_ref[:, :, low : low + step].reshape(rank, step),
                (((1,), (1,)), ((), ())),
                preferred_element_type=F32,
            )
        if not whole:
            projected_ref[...] = total.astype(BF16)
        turned = total.T.astype(BF16)
        for low in range(0, width, step):
            term = jnp.dot(turned, second_ref[:, low : low + step], preferred_element_type=F32)
            term_ref[:, :, low : low + step] = term.astype(BF16).reshape(half, piece, step)
        if not whole:
            for ref, p in zip(out_refs, partners(True)):
                ref[...] = term_ref[p]

    stacked = jax.ShapeDtypeStruct((half, piece, width), BF16)
    out = jax.ShapeDtypeStruct((piece, width), BF16)
    projected = jax.ShapeDtypeStruct((rows, rank), BF16)
    arrays = list(pieces) + [first, second]
    if whole:
        adapter, term = call(kernel, [], arrays, [stacked, stacked], after=after)
        return adapter.reshape(rank, width), term
    got = call(
        kernel, [], arrays, [projected] + [out] * half, [stacked, stacked], after
    )
    return got[0], got[1:]


def three_step(capacity, route, tokens, cotangent, table_down, up):
    devices = lax.axis_size("dp")
    half = devices // 2
    pairs = [(i, (i + half) % devices) for i in range(devices)]

    def across(array):
        return lax.ppermute(array, "dp", pairs)

    crossing_down = pick_crossing(route, table_down, capacity)
    arrived_down = across(crossing_down)
    table_up = exchange(split_pieces(up, [crossing_down]))
    crossing_up = pick_crossing(route, table_up, capacity, [arrived_down])
    arrived_up = across(crossing_up)
    got_down = exchange(pick_pieces(route, table_down, arrived_down, after=[crossing_up]))
    down, term_up = term_pieces(got_down, tokens, cotangent, True)
    got_both = exchange(pick_pieces(route, table_up, arrived_up, term_up))
    crossing_sums_up = sum_crossing(route, got_both, capacity)
    sums_up = across(crossing_sums_up)
    inner, term_down = term_pieces(got_both, cotangent, tokens, False, [crossing_sums_up])
    pieces_down = exchange(term_down)
    crossing_sums_down = sum_crossing(route, pieces_down, capacity, [sums_up])
    sums_down = across(crossing_sums_down)
    grad_up = exchange(sum_pieces(route, got_both, sums_up, [crossing_sums_down]))
    grad_rows = dot("tr,rd->td", inner, down).astype(BF16)
    return grad_rows, sum_pieces(route, pieces_down, sums_down), grad_up


def exchange(pieces):
    devices = lax.axis_size("dp")
    got = [pieces[0]]
    for piece, step in zip(pieces[1:], STEPS[1:]):
        got.append(lax.ppermute(piece, "dp", [(i, i ^ step[i % 2]) for i in range(devices)]))
    return got


def shards(tokens, cotangent, segments, owner_map, down_t, up):
    devices = lax.axis_size("dp")
    if devices != 2 * len(STEPS):
        slots = block_slots(segments, owner_map, 1, devices)
        return two_step(slots, tokens, cotangent, down_t, up)
    half = devices // 2
    rank, width = down_t.shape[1:]
    shape = (half, rank // half, width)
    table_down = exchange(split_pieces(down_t.reshape(shape)))
    route, most = routes(segments, owner_map, devices)
    capacities = [3, 4, 5, half]
    branch = sum((most[0] > c).astype(I32) for c in capacities[:-1])
    grad_rows, grad_down, grad_up = lax.switch(
        branch,
        [functools.partial(three_step, c) for c in capacities],
        route,
        tokens,
        cotangent,
        table_down,
        up.reshape(shape),
    )
    grad_down = exchange(grad_down)
    return (
        grad_rows,
        join_pieces(grad_down).reshape(1, rank, width),
        join_pieces(grad_up).reshape(1, rank, width),
    )


def solution(mesh):
    in_specs = (
        P(("groups", "dp"), None),
        P(("groups", "dp"), None),
        P("groups", None, None),
        P("groups"),
        P(("groups", "dp"), None, None),
        P(("groups", "dp"), None, None),
    )
    out_specs = (
        P(("groups", "dp"), None),
        P(("groups", "dp"), None, None),
        P(("groups", "dp"), None, None),
    )
    return jax.shard_map(shards, mesh=mesh, in_specs=in_specs, out_specs=out_specs, check_vma=False)
```

```python
import functools

import jax
import jax.numpy as jnp
from jax import lax
from jax.experimental import pallas as pl
from jax.experimental.pallas import tpu as pltpu
from jax.sharding import PartitionSpec as P

BLOCK = 128
F32 = jnp.float32
BF16 = jnp.bfloat16
I32 = jnp.int32
VMEM = pl.BlockSpec(memory_space=pltpu.VMEM)
SMEM = pl.BlockSpec(memory_space=pltpu.SMEM)


def block_slots(segments, owner_map, blocks, count_adapters):
    index = jnp.arange(blocks, dtype=I32)
    ids = segments[:, :, 0]
    starts = segments[:, :, 1]
    counts = segments[:, :, 2]
    inside = (index[None, None, :] >= starts[:, :, None]) & (
        index[None, None, :] < (starts + counts)[:, :, None]
    )
    adapter = jnp.sum(jnp.where(inside, ids[:, :, None], 0), axis=1)
    match = adapter[:, :, None] == jnp.arange(count_adapters, dtype=I32)[None, None, :]
    slots = jnp.sum(jnp.where(match, owner_map[None, None, :], 0), axis=2)
    return slots.reshape(-1)


def dot(spec, a, b):
    return jnp.einsum(spec, a, b, preferred_element_type=F32)


def two_step(slots, tokens, cotangent, down_t, up):
    devices = lax.axis_size("dp")
    rank, width = down_t.shape[1:]
    piece = 2 * rank // devices
    exchange = functools.partial(
        lax.all_to_all, axis_name="dp", split_axis=0, concat_axis=0, tiled=True
    )
    stack = jnp.concatenate([down_t[0], up[0]], axis=0).reshape(devices, piece, width)
    table = exchange(stack)
    mine = exchange(jnp.take(table, slots, axis=0, mode="clip")).reshape(2 * rank, width)
    down, up_ = mine[:rank], mine[rank:]
    hidden = dot("td,rd->tr", tokens, down).astype(BF16)
    inner = dot("td,rd->tr", cotangent, up_).astype(BF16)
    grad_rows = dot("tr,rd->td", inner, down).astype(BF16)
    terms = jnp.concatenate(
        [dot("tr,td->rd", inner, tokens), dot("tr,td->rd", hidden, cotangent)], axis=0
    ).astype(BF16)
    pieces = exchange(terms.reshape(devices, piece, width))
    onehot = (slots[None, :] == jnp.arange(devices, dtype=I32)[:, None]).astype(BF16)
    summed = dot("kb,bpd->kpd", onehot, pieces) * (1.0 / BLOCK)
    grads = exchange(summed.astype(BF16)).reshape(2, rank, width)
    return grad_rows, grads[:1], grads[1:]


STEPS = ((0, 0), (2, 4), (4, 2), (6, 6), (3, 5), (5, 3), (7, 7), (1, 1))


def partner(index, step):
    a, b = step
    if a == b:
        return index ^ a
    second = index if a % 2 == 0 else index ^ (index // 2) ^ (index // 4)
    return index ^ (a + (second % 2) * (b - a))


def partners():
    own = lax.rem(lax.axis_index("dp"), len(STEPS))
    return [partner(own, step) for step in STEPS]


def call(kernel, scalars, arrays, outs, scratch=(), after=()):
    size = 4 << 20
    for array in list(arrays) + list(outs) + list(scratch):
        extent = array.dtype.itemsize
        for value in array.shape:
            extent *= value
        size += extent
    given = len(scalars) + len(arrays)
    return pl.pallas_call(
        lambda *refs: kernel(*refs[:given], *refs[given + len(after) :]),
        out_shape=outs,
        in_specs=[SMEM] * len(scalars)
        + [VMEM] * len(arrays)
        + [pl.BlockSpec(memory_space=pl.ANY)] * len(after),
        out_specs=[VMEM] * len(outs),
        scratch_shapes=[pltpu.VMEM(s.shape, s.dtype) for s in scratch],
        compiler_params=pltpu.CompilerParams(vmem_limit_bytes=size),
    )(*scalars, *arrays, *after)


SEND, ARRIVED, FETCH, CROSS, LOCAL = range(5)


def routes(segments, owner_map, devices, capacities):
    half = devices // 2
    entries = segments.shape[1]

    def kernel(segments_ref, owner_ref, out_ref, branch_ref, slot_ref, need_ref, place_ref):
        side = lax.div(lax.axis_index("dp"), half)
        for d in range(devices):
            need_ref[d] = 0
            adapter = 0
            for e in range(entries):
                start = segments_ref[1, e, d]
                inside = (start <= 0) & (start + segments_ref[2, e, d] > 0)
                adapter += jnp.where(inside, segments_ref[0, e, d], 0)
            slot_ref[d] = owner_ref[adapter]
        for d in range(devices):
            slot = slot_ref[d]
            need_ref[slot] = jnp.where(lax.div(slot, half) != d // half, 1, need_ref[slot])
        for j in range(half):
            out_ref[SEND, j] = 0
            out_ref[ARRIVED, j] = half
        counts = []
        for s in range(2):
            count = jnp.int32(0)
            for k in range(half):
                needed = need_ref[s * half + k]
                place_ref[s * half + k] = count

                @pl.when((side == s) & (needed == 1))
                def _(count=count, k=k):
                    out_ref[SEND, count] = k
                    out_ref[ARRIVED, count] = k

                count += needed
            counts.append(count)
        most = jnp.maximum(counts[0], counts[1])
        branch = jnp.int32(0)
        for capacity in capacities[:-1]:
            branch += jnp.where(most > capacity, 1, 0)
        branch_ref[0] = branch
        for u in range(half):
            slot = slot_ref[side * half + u]
            local = lax.div(slot, half) == side
            place = place_ref[slot]
            k = lax.rem(slot, half)
            out_ref[FETCH, u] = jnp.where(local, k, half + place)
            out_ref[CROSS, u] = jnp.where(local, half, place)
            out_ref[LOCAL, u] = jnp.where(local, k, half)

    return pl.pallas_call(
        kernel,
        out_shape=[jax.ShapeDtypeStruct((5, half), I32), jax.ShapeDtypeStruct((1,), I32)],
        in_specs=[SMEM] * 2,
        out_specs=[SMEM] * 2,
        scratch_shapes=[pltpu.SMEM((devices,), I32)] * 3,
    )(jnp.transpose(segments, (2, 1, 0)), owner_map)


def split_pieces(stacked, after=()):
    half = stacked.shape[0]

    def kernel(stacked_ref, *out_refs):
        for ref, p in zip(out_refs, partners()):
            ref[...] = stacked_ref[p]

    piece = jax.ShapeDtypeStruct(stacked.shape[1:], BF16)
    return call(kernel, [], [stacked], [piece] * half, after=after)


def join_pieces(pieces):
    half = len(pieces)

    def kernel(*refs):
        for ref, p in zip(refs, partners()):
            refs[half][p] = ref[...]

    out = jax.ShapeDtypeStruct((half,) + pieces[0].shape, BF16)
    return call(kernel, [], pieces, [out])[0]


def pick_crossing(route, table, count, after=()):
    half = len(table)
    shape = table[0].shape

    def kernel(route_ref, *refs):
        out_ref, all_ref = refs[half:]
        for ref, p in zip(refs, partners()):
            all_ref[p] = ref[...]
        for j in range(count):
            out_ref[j] = all_ref[route_ref[SEND, j]]

    out = jax.ShapeDtypeStruct((count,) + shape, BF16)
    scratch = jax.ShapeDtypeStruct((half,) + shape, BF16)
    return call(kernel, [route], table, [out], [scratch], after)[0]


def pick_pieces(route, table, arrived, terms=None, after=()):
    half = len(table)
    count = arrived.shape[0]
    shape = table[0].shape
    arrays = list(table) + [arrived] + ([] if terms is None else [terms])

    def kernel(route_ref, *refs):
        out_refs, all_ref = refs[len(arrays) : -1], refs[-1]
        for ref, p in zip(refs[:half], partners()):
            all_ref[p] = ref[...]
        for j in range(count):
            all_ref[half + j] = refs[half][j]
        for ref, p in zip(out_refs, partners()):
            if terms is None:
                ref[...] = all_ref[route_ref[FETCH, p]]
            else:
                ref[0] = all_ref[route_ref[FETCH, p]]
                ref[1] = refs[half + 1][p]

    out = jax.ShapeDtypeStruct(shape if terms is None else (2,) + shape, BF16)
    scratch = jax.ShapeDtypeStruct((half + count,) + shape, BF16)
    return call(kernel, [route], arrays, [out] * half, [scratch], after)


def lower(ref):
    return ref[1] if len(ref.shape) == 3 else ref[...]


def upper(ref):
    return ref[0] if len(ref.shape) == 3 else ref[...]


def sum_crossing(route, pieces, count, after=()):
    half = len(pieces)
    shape = pieces[0].shape[-2:]

    def kernel(route_ref, *refs):
        out_ref, total_ref = refs[half:]
        total_ref[...] = jnp.zeros_like(total_ref)
        for ref, p in zip(refs[:half], partners()):
            place = route_ref[CROSS, p]
            total_ref[place] = total_ref[place] + lower(ref).astype(F32)
        for k in range(count):
            out_ref[k] = total_ref[k].astype(BF16)

    out = jax.ShapeDtypeStruct((count,) + shape, BF16)
    scratch = jax.ShapeDtypeStruct((half + 1,) + shape, F32)
    return call(kernel, [route], pieces, [out], [scratch], after)[0]


def sum_pieces(route, pieces, arrived, after=()):
    half = len(pieces)
    count = arrived.shape[0]
    shape = pieces[0].shape[-2:]

    def kernel(route_ref, *refs):
        out_refs, total_ref = refs[half + 1 : -1], refs[-1]
        total_ref[...] = jnp.zeros_like(total_ref)
        for ref, p in zip(refs[:half], partners()):
            place = route_ref[LOCAL, p]
            total_ref[place] = total_ref[place] + lower(ref).astype(F32)
        for j in range(count):
            place = route_ref[ARRIVED, j]
            total_ref[place] = total_ref[place] + refs[half][j].astype(F32)
        for ref, p in zip(out_refs, partners()):
            ref[...] = (total_ref[p] * (1.0 / BLOCK)).astype(BF16)

    out = jax.ShapeDtypeStruct(shape, BF16)
    scratch = jax.ShapeDtypeStruct((half + 1,) + shape, F32)
    arrays = list(pieces) + [arrived]
    return call(kernel, [route], arrays, [out] * half, [scratch], after)


def term_pieces(pieces, first, second, whole, after=()):
    half = len(pieces)
    rows, width = first.shape
    piece = pieces[0].shape[-2]
    rank = half * piece
    step = max(s for s in (128, 256, 512, 640, 1024) if width % s == 0)

    def kernel(*refs):
        first_ref, second_ref = refs[half : half + 2]
        if whole:
            adapter_ref, term_ref = refs[half + 2 :]
        else:
            projected_ref, out_refs = refs[half + 2], refs[half + 3 : -2]
            adapter_ref, term_ref = refs[-2:]
        for ref, p in zip(refs[:half], partners()):
            adapter_ref[p] = upper(ref)
        total = jnp.zeros((rows, rank), F32)
        for low in range(0, width, step):
            total += lax.dot_general(
                first_ref[:, low : low + step],
                adapter_ref[:, :, low : low + step].reshape(rank, step),
                (((1,), (1,)), ((), ())),
                preferred_element_type=F32,
            )
        if not whole:
            projected_ref[...] = total.astype(BF16)
        turned = total.T.astype(BF16)
        for low in range(0, width, step):
            term = jnp.dot(turned, second_ref[:, low : low + step], preferred_element_type=F32)
            term_ref[:, :, low : low + step] = term.astype(BF16).reshape(half, piece, step)
        if not whole:
            for ref, p in zip(out_refs, partners()):
                ref[...] = term_ref[p]

    stacked = jax.ShapeDtypeStruct((half, piece, width), BF16)
    out = jax.ShapeDtypeStruct((piece, width), BF16)
    projected = jax.ShapeDtypeStruct((rows, rank), BF16)
    arrays = list(pieces) + [first, second]
    if whole:
        adapter, term = call(kernel, [], arrays, [stacked, stacked], after=after)
        return adapter.reshape(rank, width), term
    got = call(
        kernel, [], arrays, [projected] + [out] * half, [stacked, stacked], after
    )
    return got[0], got[1:]


def three_step(capacity, route, tokens, cotangent, table_down, up):
    devices = lax.axis_size("dp")
    half = devices // 2
    pairs = [(i, (i + half) % devices) for i in range(devices)]

    def across(array):
        return lax.ppermute(array, "dp", pairs)

    crossing_down = pick_crossing(route, table_down, capacity)
    arrived_down = across(crossing_down)
    table_up = exchange(split_pieces(up, [crossing_down]))
    crossing_up = pick_crossing(route, table_up, capacity, [arrived_down])
    arrived_up = across(crossing_up)
    got_down = exchange(pick_pieces(route, table_down, arrived_down, after=[crossing_up]))
    down, term_up = term_pieces(got_down, tokens, cotangent, True)
    got_both = exchange(pick_pieces(route, table_up, arrived_up, term_up))
    crossing_sums_up = sum_crossing(route, got_both, capacity)
    sums_up = across(crossing_sums_up)
    inner, term_down = term_pieces(got_both, cotangent, tokens, False, [crossing_sums_up])
    pieces_down = exchange(term_down)
    crossing_sums_down = sum_crossing(route, pieces_down, capacity, [sums_up])
    sums_down = across(crossing_sums_down)
    grad_up = exchange(sum_pieces(route, got_both, sums_up, [crossing_sums_down]))
    grad_rows = dot("tr,rd->td", inner, down).astype(BF16)
    return grad_rows, sum_pieces(route, pieces_down, sums_down), grad_up


def exchange(pieces):
    devices = lax.axis_size("dp")
    got = [pieces[0]]
    for piece, step in zip(pieces[1:], STEPS[1:]):
        got.append(lax.ppermute(piece, "dp", [(i, partner(i, step)) for i in range(devices)]))
    return got


def shards(tokens, cotangent, segments, owner_map, down_t, up):
    devices = lax.axis_size("dp")
    if devices != 2 * len(STEPS):
        slots = block_slots(segments, owner_map, 1, devices)
        return two_step(slots, tokens, cotangent, down_t, up)
    half = devices // 2
    rank, width = down_t.shape[1:]
    shape = (half, rank // half, width)
    capacities = [3, 4, 5, half]
    route, branch = routes(segments, owner_map, devices, capacities)
    table_down = exchange(split_pieces(down_t.reshape(shape), [route]))
    grad_rows, grad_down, grad_up = lax.switch(
        branch[0],
        [functools.partial(three_step, c) for c in capacities],
        route,
        tokens,
        cotangent,
        table_down,
        up.reshape(shape),
    )
    grad_down = exchange(grad_down)
    return (
        grad_rows,
        join_pieces(grad_down).reshape(1, rank, width),
        join_pieces(grad_up).reshape(1, rank, width),
    )


def solution(mesh):
    in_specs = (
        P(("groups", "dp"), None),
        P(("groups", "dp"), None),
        P("groups", None, None),
        P("groups"),
        P(("groups", "dp"), None, None),
        P(("groups", "dp"), None, None),
    )
    out_specs = (
        P(("groups", "dp"), None),
        P(("groups", "dp"), None, None),
        P(("groups", "dp"), None, None),
    )
    return jax.shard_map(shards, mesh=mesh, in_specs=in_specs, out_specs=out_specs, check_vma=False)
```

```python
import functools

import jax
import jax.numpy as jnp
from jax import lax
from jax.experimental import pallas as pl
from jax.experimental.pallas import tpu as pltpu
from jax.sharding import PartitionSpec as P

BLOCK = 128
F32 = jnp.float32
BF16 = jnp.bfloat16
I32 = jnp.int32
VMEM = pl.BlockSpec(memory_space=pltpu.VMEM)
SMEM = pl.BlockSpec(memory_space=pltpu.SMEM)


def block_slots(segments, owner_map, blocks, count_adapters):
    index = jnp.arange(blocks, dtype=I32)
    ids = segments[:, :, 0]
    starts = segments[:, :, 1]
    counts = segments[:, :, 2]
    inside = (index[None, None, :] >= starts[:, :, None]) & (
        index[None, None, :] < (starts + counts)[:, :, None]
    )
    adapter = jnp.sum(jnp.where(inside, ids[:, :, None], 0), axis=1)
    match = adapter[:, :, None] == jnp.arange(count_adapters, dtype=I32)[None, None, :]
    slots = jnp.sum(jnp.where(match, owner_map[None, None, :], 0), axis=2)
    return slots.reshape(-1)


def dot(spec, a, b):
    return jnp.einsum(spec, a, b, preferred_element_type=F32)


def two_step(slots, tokens, cotangent, down_t, up):
    devices = lax.axis_size("dp")
    rank, width = down_t.shape[1:]
    piece = 2 * rank // devices
    exchange = functools.partial(
        lax.all_to_all, axis_name="dp", split_axis=0, concat_axis=0, tiled=True
    )
    stack = jnp.concatenate([down_t[0], up[0]], axis=0).reshape(devices, piece, width)
    table = exchange(stack)
    mine = exchange(jnp.take(table, slots, axis=0, mode="clip")).reshape(2 * rank, width)
    down, up_ = mine[:rank], mine[rank:]
    hidden = dot("td,rd->tr", tokens, down).astype(BF16)
    inner = dot("td,rd->tr", cotangent, up_).astype(BF16)
    grad_rows = dot("tr,rd->td", inner, down).astype(BF16)
    terms = jnp.concatenate(
        [dot("tr,td->rd", inner, tokens), dot("tr,td->rd", hidden, cotangent)], axis=0
    ).astype(BF16)
    pieces = exchange(terms.reshape(devices, piece, width))
    onehot = (slots[None, :] == jnp.arange(devices, dtype=I32)[:, None]).astype(BF16)
    summed = dot("kb,bpd->kpd", onehot, pieces) * (1.0 / BLOCK)
    grads = exchange(summed.astype(BF16)).reshape(2, rank, width)
    return grad_rows, grads[:1], grads[1:]


STEPS = ((0, 0), (1, 1), (2, 4), (4, 2), (6, 6), (3, 5), (5, 3), (7, 7))


def partners(sending):
    own = lax.rem(lax.axis_index("dp"), len(STEPS))
    places = []
    for a, b in STEPS:
        if a % 2 and not sending:
            a, b = b, a
        places.append(own ^ jnp.where(own % 2 == 1, b, a) if a != b else own ^ a)
    return places


def call(kernel, scalars, arrays, outs, scratch=(), after=()):
    size = 4 << 20
    for array in list(arrays) + list(outs) + list(scratch):
        extent = array.dtype.itemsize
        for value in array.shape:
            extent *= value
        size += extent
    given = len(scalars) + len(arrays)
    return pl.pallas_call(
        lambda *refs: kernel(*refs[:given], *refs[given + len(after) :]),
        out_shape=outs,
        in_specs=[SMEM] * len(scalars)
        + [VMEM] * len(arrays)
        + [pl.BlockSpec(memory_space=pl.ANY)] * len(after),
        out_specs=[VMEM] * len(outs),
        scratch_shapes=[pltpu.VMEM(s.shape, s.dtype) for s in scratch],
        compiler_params=pltpu.CompilerParams(vmem_limit_bytes=size),
    )(*scalars, *arrays, *after)


SEND, ARRIVED, FETCH, CROSS, LOCAL = range(5)


def routes(segments, owner_map, devices, capacities):
    half = devices // 2
    entries = segments.shape[1]

    def kernel(segments_ref, owner_ref, out_ref, branch_ref, slot_ref, need_ref, place_ref):
        side = lax.div(lax.axis_index("dp"), half)
        for d in range(devices):
            need_ref[d] = 0
            adapter = 0
            for e in range(entries):
                start = segments_ref[1, e, d]
                inside = (start <= 0) & (start + segments_ref[2, e, d] > 0)
                adapter += jnp.where(inside, segments_ref[0, e, d], 0)
            slot_ref[d] = owner_ref[adapter]
        for d in range(devices):
            slot = slot_ref[d]
            need_ref[slot] = jnp.where(lax.div(slot, half) != d // half, 1, need_ref[slot])
        for j in range(half):
            out_ref[SEND, j] = 0
            out_ref[ARRIVED, j] = half
        counts = []
        for s in range(2):
            count = jnp.int32(0)
            for k in range(half):
                needed = need_ref[s * half + k]
                place_ref[s * half + k] = count

                @pl.when((side == s) & (needed == 1))
                def _(count=count, k=k):
                    out_ref[SEND, count] = k
                    out_ref[ARRIVED, count] = k

                count += needed
            counts.append(count)
        most = jnp.maximum(counts[0], counts[1])
        branch = jnp.int32(0)
        for capacity in capacities[:-1]:
            branch += jnp.where(most > capacity, 1, 0)
        branch_ref[0] = branch
        for u in range(half):
            slot = slot_ref[side * half + u]
            local = lax.div(slot, half) == side
            place = place_ref[slot]
            k = lax.rem(slot, half)
            out_ref[FETCH, u] = jnp.where(local, k, half + place)
            out_ref[CROSS, u] = jnp.where(local, half, place)
            out_ref[LOCAL, u] = jnp.where(local, k, half)

    return pl.pallas_call(
        kernel,
        out_shape=[jax.ShapeDtypeStruct((5, half), I32), jax.ShapeDtypeStruct((1,), I32)],
        in_specs=[SMEM] * 2,
        out_specs=[SMEM] * 2,
        scratch_shapes=[pltpu.SMEM((devices,), I32)] * 3,
    )(jnp.transpose(segments, (2, 1, 0)), owner_map)


def split_pieces(stacked, after=()):
    half = stacked.shape[0]

    def kernel(stacked_ref, *out_refs):
        for ref, p in zip(out_refs, partners(True)):
            ref[...] = stacked_ref[p]

    piece = jax.ShapeDtypeStruct(stacked.shape[1:], BF16)
    return call(kernel, [], [stacked], [piece] * half, after=after)


def join_pieces(pieces):
    half = len(pieces)

    def kernel(*refs):
        for ref, p in zip(refs, partners(False)):
            refs[half][p] = ref[...]

    out = jax.ShapeDtypeStruct((half,) + pieces[0].shape, BF16)
    return call(kernel, [], pieces, [out])[0]


def pick_crossing(route, table, count, after=()):
    half = len(table)
    shape = table[0].shape

    def kernel(route_ref, *refs):
        out_ref, all_ref = refs[half:]
        for ref, p in zip(refs, partners(False)):
            all_ref[p] = ref[...]
        for j in range(count):
            out_ref[j] = all_ref[route_ref[SEND, j]]

    out = jax.ShapeDtypeStruct((count,) + shape, BF16)
    scratch = jax.ShapeDtypeStruct((half,) + shape, BF16)
    return call(kernel, [route], table, [out], [scratch], after)[0]


def pick_pieces(route, table, arrived, terms=None, after=()):
    half = len(table)
    count = arrived.shape[0]
    shape = table[0].shape
    arrays = list(table) + [arrived] + ([] if terms is None else [terms])

    def kernel(route_ref, *refs):
        out_refs, all_ref = refs[len(arrays) : -1], refs[-1]
        for ref, p in zip(refs[:half], partners(False)):
            all_ref[p] = ref[...]
        for j in range(count):
            all_ref[half + j] = refs[half][j]
        for ref, p in zip(out_refs, partners(True)):
            if terms is None:
                ref[...] = all_ref[route_ref[FETCH, p]]
            else:
                ref[0] = all_ref[route_ref[FETCH, p]]
                ref[1] = refs[half + 1][p]

    out = jax.ShapeDtypeStruct(shape if terms is None else (2,) + shape, BF16)
    scratch = jax.ShapeDtypeStruct((half + count,) + shape, BF16)
    return call(kernel, [route], arrays, [out] * half, [scratch], after)


def lower(ref):
    return ref[1] if len(ref.shape) == 3 else ref[...]


def upper(ref):
    return ref[0] if len(ref.shape) == 3 else ref[...]


def sum_crossing(route, pieces, count, after=()):
    half = len(pieces)
    shape = pieces[0].shape[-2:]

    def kernel(route_ref, *refs):
        out_ref, total_ref = refs[half:]
        total_ref[...] = jnp.zeros_like(total_ref)
        for ref, p in zip(refs[:half], partners(False)):
            place = route_ref[CROSS, p]
            total_ref[place] = total_ref[place] + lower(ref).astype(F32)
        for k in range(count):
            out_ref[k] = total_ref[k].astype(BF16)

    out = jax.ShapeDtypeStruct((count,) + shape, BF16)
    scratch = jax.ShapeDtypeStruct((half + 1,) + shape, F32)
    return call(kernel, [route], pieces, [out], [scratch], after)[0]


def sum_pieces(route, pieces, arrived, after=()):
    half = len(pieces)
    count = arrived.shape[0]
    shape = pieces[0].shape[-2:]

    def kernel(route_ref, *refs):
        out_refs, total_ref = refs[half + 1 : -1], refs[-1]
        total_ref[...] = jnp.zeros_like(total_ref)
        for ref, p in zip(refs[:half], partners(False)):
            place = route_ref[LOCAL, p]
            total_ref[place] = total_ref[place] + lower(ref).astype(F32)
        for j in range(count):
            place = route_ref[ARRIVED, j]
            total_ref[place] = total_ref[place] + refs[half][j].astype(F32)
        for ref, p in zip(out_refs, partners(True)):
            ref[...] = (total_ref[p] * (1.0 / BLOCK)).astype(BF16)

    out = jax.ShapeDtypeStruct(shape, BF16)
    scratch = jax.ShapeDtypeStruct((half + 1,) + shape, F32)
    arrays = list(pieces) + [arrived]
    return call(kernel, [route], arrays, [out] * half, [scratch], after)


def term_pieces(pieces, first, second, whole, after=()):
    half = len(pieces)
    rows, width = first.shape
    piece = pieces[0].shape[-2]
    rank = half * piece
    step = max(s for s in (128, 256, 512, 640, 1024) if width % s == 0)

    def kernel(*refs):
        first_ref, second_ref = refs[half : half + 2]
        if whole:
            adapter_ref, term_ref = refs[half + 2 :]
        else:
            projected_ref, out_refs = refs[half + 2], refs[half + 3 : -2]
            adapter_ref, term_ref = refs[-2:]
        for ref, p in zip(refs[:half], partners(False)):
            adapter_ref[p] = upper(ref)
        total = jnp.zeros((rows, rank), F32)
        for low in range(0, width, step):
            total += lax.dot_general(
                first_ref[:, low : low + step],
                adapter_ref[:, :, low : low + step].reshape(rank, step),
                (((1,), (1,)), ((), ())),
                preferred_element_type=F32,
            )
        if not whole:
            projected_ref[...] = total.astype(BF16)
        turned = total.T.astype(BF16)
        for low in range(0, width, step):
            term = jnp.dot(turned, second_ref[:, low : low + step], preferred_element_type=F32)
            term_ref[:, :, low : low + step] = term.astype(BF16).reshape(half, piece, step)
        if not whole:
            for ref, p in zip(out_refs, partners(True)):
                ref[...] = term_ref[p]

    stacked = jax.ShapeDtypeStruct((half, piece, width), BF16)
    out = jax.ShapeDtypeStruct((piece, width), BF16)
    projected = jax.ShapeDtypeStruct((rows, rank), BF16)
    arrays = list(pieces) + [first, second]
    if whole:
        adapter, term = call(kernel, [], arrays, [stacked, stacked], after=after)
        return adapter.reshape(rank, width), term
    got = call(
        kernel, [], arrays, [projected] + [out] * half, [stacked, stacked], after
    )
    return got[0], got[1:]


def three_step(capacity, route, tokens, cotangent, table_down, up):
    devices = lax.axis_size("dp")
    half = devices // 2
    pairs = [(i, (i + half) % devices) for i in range(devices)]

    def across(array):
        return lax.ppermute(array, "dp", pairs)

    crossing_down = pick_crossing(route, table_down, capacity)
    arrived_down = across(crossing_down)
    table_up = exchange(split_pieces(up, [crossing_down]))
    crossing_up = pick_crossing(route, table_up, capacity, [arrived_down])
    arrived_up = across(crossing_up)
    got_down = exchange(pick_pieces(route, table_down, arrived_down, after=[crossing_up]))
    down, term_up = term_pieces(got_down, tokens, cotangent, True)
    got_both = exchange(pick_pieces(route, table_up, arrived_up, term_up))
    crossing_sums_up = sum_crossing(route, got_both, capacity)
    sums_up = across(crossing_sums_up)
    inner, term_down = term_pieces(got_both, cotangent, tokens, False, [crossing_sums_up])
    pieces_down = exchange(term_down)
    crossing_sums_down = sum_crossing(route, pieces_down, capacity, [sums_up])
    sums_down = across(crossing_sums_down)
    grad_up = exchange(sum_pieces(route, got_both, sums_up, [crossing_sums_down]))
    grad_rows = dot("tr,rd->td", inner, down).astype(BF16)
    return grad_rows, sum_pieces(route, pieces_down, sums_down), grad_up


def exchange(pieces):
    devices = lax.axis_size("dp")
    got = [pieces[0]]
    for piece, step in zip(pieces[1:], STEPS[1:]):
        got.append(lax.ppermute(piece, "dp", [(i, i ^ step[i % 2]) for i in range(devices)]))
    return got


def shards(tokens, cotangent, segments, owner_map, down_t, up):
    devices = lax.axis_size("dp")
    if devices != 2 * len(STEPS):
        slots = block_slots(segments, owner_map, 1, devices)
        return two_step(slots, tokens, cotangent, down_t, up)
    half = devices // 2
    rank, width = down_t.shape[1:]
    shape = (half, rank // half, width)
    capacities = [3, 4, 5, half]
    route, branch = routes(segments, owner_map, devices, capacities)
    table_down = exchange(split_pieces(down_t.reshape(shape)))
    grad_rows, grad_down, grad_up = lax.switch(
        branch[0],
        [functools.partial(three_step, c) for c in capacities],
        route,
        tokens,
        cotangent,
        table_down,
        up.reshape(shape),
    )
    grad_down = exchange(grad_down)
    return (
        grad_rows,
        join_pieces(grad_down).reshape(1, rank, width),
        join_pieces(grad_up).reshape(1, rank, width),
    )


def solution(mesh):
    in_specs = (
        P(("groups", "dp"), None),
        P(("groups", "dp"), None),
        P("groups", None, None),
        P("groups"),
        P(("groups", "dp"), None, None),
        P(("groups", "dp"), None, None),
    )
    out_specs = (
        P(("groups", "dp"), None),
        P(("groups", "dp"), None, None),
        P(("groups", "dp"), None, None),
    )
    return jax.shard_map(shards, mesh=mesh, in_specs=in_specs, out_specs=out_specs, check_vma=False)
```

```python
import functools

import jax
import jax.numpy as jnp
from jax import lax
from jax.experimental import pallas as pl
from jax.experimental.pallas import tpu as pltpu
from jax.sharding import PartitionSpec as P

BLOCK = 128
F32 = jnp.float32
BF16 = jnp.bfloat16
I32 = jnp.int32
VMEM = pl.BlockSpec(memory_space=pltpu.VMEM)
SMEM = pl.BlockSpec(memory_space=pltpu.SMEM)


def block_slots(segments, owner_map, blocks, count_adapters):
    index = jnp.arange(blocks, dtype=I32)
    ids = segments[:, :, 0]
    starts = segments[:, :, 1]
    counts = segments[:, :, 2]
    inside = (index[None, None, :] >= starts[:, :, None]) & (
        index[None, None, :] < (starts + counts)[:, :, None]
    )
    adapter = jnp.sum(jnp.where(inside, ids[:, :, None], 0), axis=1)
    match = adapter[:, :, None] == jnp.arange(count_adapters, dtype=I32)[None, None, :]
    slots = jnp.sum(jnp.where(match, owner_map[None, None, :], 0), axis=2)
    return slots.reshape(-1)


def dot(spec, a, b):
    return jnp.einsum(spec, a, b, preferred_element_type=F32)


def two_step(slots, tokens, cotangent, down_t, up):
    devices = lax.axis_size("dp")
    rank, width = down_t.shape[1:]
    piece = 2 * rank // devices
    exchange = functools.partial(
        lax.all_to_all, axis_name="dp", split_axis=0, concat_axis=0, tiled=True
    )
    stack = jnp.concatenate([down_t[0], up[0]], axis=0).reshape(devices, piece, width)
    table = exchange(stack)
    mine = exchange(jnp.take(table, slots, axis=0, mode="clip")).reshape(2 * rank, width)
    down, up_ = mine[:rank], mine[rank:]
    hidden = dot("td,rd->tr", tokens, down).astype(BF16)
    inner = dot("td,rd->tr", cotangent, up_).astype(BF16)
    grad_rows = dot("tr,rd->td", inner, down).astype(BF16)
    terms = jnp.concatenate(
        [dot("tr,td->rd", inner, tokens), dot("tr,td->rd", hidden, cotangent)], axis=0
    ).astype(BF16)
    pieces = exchange(terms.reshape(devices, piece, width))
    onehot = (slots[None, :] == jnp.arange(devices, dtype=I32)[:, None]).astype(BF16)
    summed = dot("kb,bpd->kpd", onehot, pieces) * (1.0 / BLOCK)
    grads = exchange(summed.astype(BF16)).reshape(2, rank, width)
    return grad_rows, grads[:1], grads[1:]


STEPS = ((0, 0), (2, 4), (4, 2), (6, 6), (3, 5), (5, 3), (7, 7), (1, 1))


def partners(sending):
    own = lax.rem(lax.axis_index("dp"), len(STEPS))
    places = []
    for a, b in STEPS:
        if a % 2 and not sending:
            a, b = b, a
        places.append(own ^ jnp.where(own % 2 == 1, b, a) if a != b else own ^ a)
    return places


def call(kernel, scalars, arrays, outs, scratch=(), after=()):
    size = 4 << 20
    for array in list(arrays) + list(outs) + list(scratch):
        extent = array.dtype.itemsize
        for value in array.shape:
            extent *= value
        size += extent
    given = len(scalars) + len(arrays)
    return pl.pallas_call(
        lambda *refs: kernel(*refs[:given], *refs[given + len(after) :]),
        out_shape=outs,
        in_specs=[SMEM] * len(scalars)
        + [VMEM] * len(arrays)
        + [pl.BlockSpec(memory_space=pl.ANY)] * len(after),
        out_specs=[VMEM] * len(outs),
        scratch_shapes=[pltpu.VMEM(s.shape, s.dtype) for s in scratch],
        compiler_params=pltpu.CompilerParams(vmem_limit_bytes=size),
    )(*scalars, *arrays, *after)


SEND, ARRIVED, FETCH, CROSS, LOCAL = range(5)


def routes(segments, owner_map, devices, capacities):
    half = devices // 2
    entries = segments.shape[1]

    def kernel(segments_ref, owner_ref, out_ref, branch_ref, slot_ref, need_ref, place_ref):
        side = lax.div(lax.axis_index("dp"), half)
        for d in range(devices):
            need_ref[d] = 0
            adapter = 0
            for e in range(entries):
                start = segments_ref[1, e, d]
                inside = (start <= 0) & (start + segments_ref[2, e, d] > 0)
                adapter += jnp.where(inside, segments_ref[0, e, d], 0)
            slot_ref[d] = owner_ref[adapter]
        for d in range(devices):
            slot = slot_ref[d]
            need_ref[slot] = jnp.where(lax.div(slot, half) != d // half, 1, need_ref[slot])
        for j in range(half):
            out_ref[SEND, j] = 0
            out_ref[ARRIVED, j] = half
        counts = []
        for s in range(2):
            count = jnp.int32(0)
            for k in range(half):
                needed = need_ref[s * half + k]
                place_ref[s * half + k] = count

                @pl.when((side == s) & (needed == 1))
                def _(count=count, k=k):
                    out_ref[SEND, count] = k
                    out_ref[ARRIVED, count] = k

                count += needed
            counts.append(count)
        most = jnp.maximum(counts[0], counts[1])
        branch = jnp.int32(0)
        for capacity in capacities[:-1]:
            branch += jnp.where(most > capacity, 1, 0)
        branch_ref[0] = branch
        for u in range(half):
            slot = slot_ref[side * half + u]
            local = lax.div(slot, half) == side
            place = place_ref[slot]
            k = lax.rem(slot, half)
            out_ref[FETCH, u] = jnp.where(local, k, half + place)
            out_ref[CROSS, u] = jnp.where(local, half, place)
            out_ref[LOCAL, u] = jnp.where(local, k, half)

    return pl.pallas_call(
        kernel,
        out_shape=[jax.ShapeDtypeStruct((5, half), I32), jax.ShapeDtypeStruct((1,), I32)],
        in_specs=[SMEM] * 2,
        out_specs=[SMEM] * 2,
        scratch_shapes=[pltpu.SMEM((devices,), I32)] * 3,
    )(jnp.transpose(segments, (2, 1, 0)), owner_map)


def split_pieces(stacked, after=()):
    half = stacked.shape[0]

    def kernel(stacked_ref, *out_refs):
        for ref, p in zip(out_refs, partners(True)):
            ref[...] = stacked_ref[p]

    piece = jax.ShapeDtypeStruct(stacked.shape[1:], BF16)
    return call(kernel, [], [stacked], [piece] * half, after=after)


def join_pieces(pieces):
    half = len(pieces)

    def kernel(*refs):
        for ref, p in zip(refs, partners(False)):
            refs[half][p] = ref[...]

    out = jax.ShapeDtypeStruct((half,) + pieces[0].shape, BF16)
    return call(kernel, [], pieces, [out])[0]


def pick_crossing(route, table, count, after=()):
    half = len(table)
    shape = table[0].shape

    def kernel(route_ref, *refs):
        out_ref, all_ref = refs[half:]
        for ref, p in zip(refs, partners(False)):
            all_ref[p] = ref[...]
        for j in range(count):
            out_ref[j] = all_ref[route_ref[SEND, j]]

    out = jax.ShapeDtypeStruct((count,) + shape, BF16)
    scratch = jax.ShapeDtypeStruct((half,) + shape, BF16)
    return call(kernel, [route], table, [out], [scratch], after)[0]


def pick_pieces(route, table, arrived, terms=None, after=()):
    half = len(table)
    count = arrived.shape[0]
    shape = table[0].shape
    arrays = list(table) + [arrived] + ([] if terms is None else [terms])

    def kernel(route_ref, *refs):
        out_refs, all_ref = refs[len(arrays) : -1], refs[-1]
        for ref, p in zip(refs[:half], partners(False)):
            all_ref[p] = ref[...]
        for j in range(count):
            all_ref[half + j] = refs[half][j]
        for ref, p in zip(out_refs, partners(True)):
            if terms is None:
                ref[...] = all_ref[route_ref[FETCH, p]]
            else:
                ref[0] = all_ref[route_ref[FETCH, p]]
                ref[1] = refs[half + 1][p]

    out = jax.ShapeDtypeStruct(shape if terms is None else (2,) + shape, BF16)
    scratch = jax.ShapeDtypeStruct((half + count,) + shape, BF16)
    return call(kernel, [route], arrays, [out] * half, [scratch], after)


def lower(ref):
    return ref[1] if len(ref.shape) == 3 else ref[...]


def upper(ref):
    return ref[0] if len(ref.shape) == 3 else ref[...]


def sum_crossing(route, pieces, count, after=()):
    half = len(pieces)
    shape = pieces[0].shape[-2:]

    def kernel(route_ref, *refs):
        out_ref, total_ref = refs[half:]
        total_ref[...] = jnp.zeros_like(total_ref)
        for ref, p in zip(refs[:half], partners(False)):
            place = route_ref[CROSS, p]
            total_ref[place] = total_ref[place] + lower(ref).astype(F32)
        for k in range(count):
            out_ref[k] = total_ref[k].astype(BF16)

    out = jax.ShapeDtypeStruct((count,) + shape, BF16)
    scratch = jax.ShapeDtypeStruct((half + 1,) + shape, F32)
    return call(kernel, [route], pieces, [out], [scratch], after)[0]


def sum_pieces(route, pieces, arrived, after=()):
    half = len(pieces)
    count = arrived.shape[0]
    shape = pieces[0].shape[-2:]

    def kernel(route_ref, *refs):
        out_refs, total_ref = refs[half + 1 : -1], refs[-1]
        total_ref[...] = jnp.zeros_like(total_ref)
        for ref, p in zip(refs[:half], partners(False)):
            place = route_ref[LOCAL, p]
            total_ref[place] = total_ref[place] + lower(ref).astype(F32)
        for j in range(count):
            place = route_ref[ARRIVED, j]
            total_ref[place] = total_ref[place] + refs[half][j].astype(F32)
        for ref, p in zip(out_refs, partners(True)):
            ref[...] = (total_ref[p] * (1.0 / BLOCK)).astype(BF16)

    out = jax.ShapeDtypeStruct(shape, BF16)
    scratch = jax.ShapeDtypeStruct((half + 1,) + shape, F32)
    arrays = list(pieces) + [arrived]
    return call(kernel, [route], arrays, [out] * half, [scratch], after)


def term_pieces(pieces, first, second, whole, after=()):
    half = len(pieces)
    rows, width = first.shape
    piece = pieces[0].shape[-2]
    rank = half * piece
    step = max(s for s in (128, 256, 512, 640, 1024) if width % s == 0)

    def kernel(*refs):
        first_ref, second_ref = refs[half : half + 2]
        if whole:
            adapter_ref, term_ref = refs[half + 2 :]
        else:
            projected_ref, out_refs = refs[half + 2], refs[half + 3 : -2]
            adapter_ref, term_ref = refs[-2:]
        for ref, p in zip(refs[:half], partners(False)):
            adapter_ref[p] = upper(ref)
        total = jnp.zeros((rows, rank), F32)
        for low in range(0, width, step):
            total += lax.dot_general(
                first_ref[:, low : low + step],
                adapter_ref[:, :, low : low + step].reshape(rank, step),
                (((1,), (1,)), ((), ())),
                preferred_element_type=F32,
            )
        if not whole:
            projected_ref[...] = total.astype(BF16)
        turned = total.T.astype(BF16)
        for low in range(0, width, step):
            term = jnp.dot(turned, second_ref[:, low : low + step], preferred_element_type=F32)
            term_ref[:, :, low : low + step] = term.astype(BF16).reshape(half, piece, step)
        if not whole:
            for ref, p in zip(out_refs, partners(True)):
                ref[...] = term_ref[p]

    stacked = jax.ShapeDtypeStruct((half, piece, width), BF16)
    out = jax.ShapeDtypeStruct((piece, width), BF16)
    projected = jax.ShapeDtypeStruct((rows, rank), BF16)
    arrays = list(pieces) + [first, second]
    if whole:
        adapter, term = call(kernel, [], arrays, [stacked, stacked], after=after)
        return adapter.reshape(rank, width), term
    got = call(
        kernel, [], arrays, [projected] + [out] * half, [stacked, stacked], after
    )
    return got[0], got[1:]


def three_step(capacity, route, tokens, cotangent, table_down, up):
    devices = lax.axis_size("dp")
    half = devices // 2
    pairs = [(i, (i + half) % devices) for i in range(devices)]

    def across(array):
        return lax.ppermute(array, "dp", pairs)

    crossing_down = pick_crossing(route, table_down, capacity)
    arrived_down = across(crossing_down)
    table_up = exchange(split_pieces(up, [crossing_down]))
    crossing_up = pick_crossing(route, table_up, capacity, [arrived_down])
    arrived_up = across(crossing_up)
    got_down = exchange(pick_pieces(route, table_down, arrived_down, after=[crossing_up]))
    down, term_up = term_pieces(got_down, tokens, cotangent, True)
    got_both = exchange(pick_pieces(route, table_up, arrived_up, term_up))
    crossing_sums_up = sum_crossing(route, got_both, capacity)
    sums_up = across(crossing_sums_up)
    inner, term_down = term_pieces(got_both, cotangent, tokens, False, [crossing_sums_up])
    pieces_down = exchange(term_down)
    crossing_sums_down = sum_crossing(route, pieces_down, capacity, [sums_up])
    sums_down = across(crossing_sums_down)
    grad_up = exchange(sum_pieces(route, got_both, sums_up, [crossing_sums_down]))
    grad_rows = dot("tr,rd->td", inner, down).astype(BF16)
    return grad_rows, sum_pieces(route, pieces_down, sums_down), grad_up


def exchange(pieces):
    devices = lax.axis_size("dp")
    got = [pieces[0]]
    for piece, step in zip(pieces[1:], STEPS[1:]):
        got.append(lax.ppermute(piece, "dp", [(i, i ^ step[i % 2]) for i in range(devices)]))
    return got


def shards(tokens, cotangent, segments, owner_map, down_t, up):
    devices = lax.axis_size("dp")
    if devices != 2 * len(STEPS):
        slots = block_slots(segments, owner_map, 1, devices)
        return two_step(slots, tokens, cotangent, down_t, up)
    half = devices // 2
    rank, width = down_t.shape[1:]
    shape = (half, rank // half, width)
    capacities = [3, 4, 5, half]
    route, branch = routes(segments, owner_map, devices, capacities)
    table_down = exchange(split_pieces(down_t.reshape(shape)))
    grad_rows, grad_down, grad_up = lax.switch(
        branch[0],
        [functools.partial(three_step, c) for c in capacities],
        route,
        tokens,
        cotangent,
        table_down,
        up.reshape(shape),
    )
    grad_down = exchange(grad_down)
    return (
        grad_rows,
        join_pieces(grad_down).reshape(1, rank, width),
        join_pieces(grad_up).reshape(1, rank, width),
    )


def solution(mesh):
    in_specs = (
        P(("groups", "dp"), None),
        P(("groups", "dp"), None),
        P("groups", None, None),
        P("groups"),
        P(("groups", "dp"), None, None),
        P(("groups", "dp"), None, None),
    )
    out_specs = (
        P(("groups", "dp"), None),
        P(("groups", "dp"), None, None),
        P(("groups", "dp"), None, None),
    )
    return jax.shard_map(shards, mesh=mesh, in_specs=in_specs, out_specs=out_specs, check_vma=False)
```

```python
import functools

import jax
import jax.numpy as jnp
from jax import lax
from jax.experimental import pallas as pl
from jax.experimental.pallas import tpu as pltpu
from jax.sharding import PartitionSpec as P

BLOCK = 128
F32 = jnp.float32
BF16 = jnp.bfloat16
I32 = jnp.int32
VMEM = pl.BlockSpec(memory_space=pltpu.VMEM)
SMEM = pl.BlockSpec(memory_space=pltpu.SMEM)


def block_slots(segments, owner_map, blocks, count_adapters):
    index = jnp.arange(blocks, dtype=I32)
    ids = segments[:, :, 0]
    starts = segments[:, :, 1]
    counts = segments[:, :, 2]
    inside = (index[None, None, :] >= starts[:, :, None]) & (
        index[None, None, :] < (starts + counts)[:, :, None]
    )
    adapter = jnp.sum(jnp.where(inside, ids[:, :, None], 0), axis=1)
    match = adapter[:, :, None] == jnp.arange(count_adapters, dtype=I32)[None, None, :]
    slots = jnp.sum(jnp.where(match, owner_map[None, None, :], 0), axis=2)
    return slots.reshape(-1)


def dot(spec, a, b):
    return jnp.einsum(spec, a, b, preferred_element_type=F32)


def two_step(slots, tokens, cotangent, down_t, up):
    devices = lax.axis_size("dp")
    rank, width = down_t.shape[1:]
    piece = 2 * rank // devices
    exchange = functools.partial(
        lax.all_to_all, axis_name="dp", split_axis=0, concat_axis=0, tiled=True
    )
    stack = jnp.concatenate([down_t[0], up[0]], axis=0).reshape(devices, piece, width)
    table = exchange(stack)
    mine = exchange(jnp.take(table, slots, axis=0, mode="clip")).reshape(2 * rank, width)
    down, up_ = mine[:rank], mine[rank:]
    hidden = dot("td,rd->tr", tokens, down).astype(BF16)
    inner = dot("td,rd->tr", cotangent, up_).astype(BF16)
    grad_rows = dot("tr,rd->td", inner, down).astype(BF16)
    terms = jnp.concatenate(
        [dot("tr,td->rd", inner, tokens), dot("tr,td->rd", hidden, cotangent)], axis=0
    ).astype(BF16)
    pieces = exchange(terms.reshape(devices, piece, width))
    onehot = (slots[None, :] == jnp.arange(devices, dtype=I32)[:, None]).astype(BF16)
    summed = dot("kb,bpd->kpd", onehot, pieces) * (1.0 / BLOCK)
    grads = exchange(summed.astype(BF16)).reshape(2, rank, width)
    return grad_rows, grads[:1], grads[1:]


ALONE = ((0, 0), (2, 4), (4, 2), (6, 6), (3, 5), (5, 3), (7, 7), (1, 1))
BESIDE = ((0, 0), (4, 4), (6, 6), (5, 5), (7, 7), (2, 2), (3, 3), (1, 1))


def partners(steps, sending):
    own = lax.rem(lax.axis_index("dp"), len(steps))
    places = []
    for a, b in steps:
        if a % 2 and not sending:
            a, b = b, a
        places.append(own ^ jnp.where(own % 2 == 1, b, a) if a != b else own ^ a)
    return places


def call(kernel, scalars, arrays, outs, scratch=(), after=()):
    size = 4 << 20
    for array in list(arrays) + list(outs) + list(scratch):
        extent = array.dtype.itemsize
        for value in array.shape:
            extent *= value
        size += extent
    given = len(scalars) + len(arrays)
    return pl.pallas_call(
        lambda *refs: kernel(*refs[:given], *refs[given + len(after) :]),
        out_shape=outs,
        in_specs=[SMEM] * len(scalars)
        + [VMEM] * len(arrays)
        + [pl.BlockSpec(memory_space=pl.ANY)] * len(after),
        out_specs=[VMEM] * len(outs),
        scratch_shapes=[pltpu.VMEM(s.shape, s.dtype) for s in scratch],
        compiler_params=pltpu.CompilerParams(vmem_limit_bytes=size),
    )(*scalars, *arrays, *after)


SEND, ARRIVED, FETCH, CROSS, LOCAL = range(5)


def routes(segments, owner_map, devices, capacities):
    half = devices // 2
    entries = segments.shape[1]

    def kernel(segments_ref, owner_ref, out_ref, branch_ref, slot_ref, need_ref, place_ref):
        side = lax.div(lax.axis_index("dp"), half)
        for d in range(devices):
            need_ref[d] = 0
            adapter = 0
            for e in range(entries):
                start = segments_ref[1, e, d]
                inside = (start <= 0) & (start + segments_ref[2, e, d] > 0)
                adapter += jnp.where(inside, segments_ref[0, e, d], 0)
            slot_ref[d] = owner_ref[adapter]
        for d in range(devices):
            slot = slot_ref[d]
            need_ref[slot] = jnp.where(lax.div(slot, half) != d // half, 1, need_ref[slot])
        for j in range(half):
            out_ref[SEND, j] = 0
            out_ref[ARRIVED, j] = half
        counts = []
        for s in range(2):
            count = jnp.int32(0)
            for k in range(half):
                needed = need_ref[s * half + k]
                place_ref[s * half + k] = count

                @pl.when((side == s) & (needed == 1))
                def _(count=count, k=k):
                    out_ref[SEND, count] = k
                    out_ref[ARRIVED, count] = k

                count += needed
            counts.append(count)
        most = jnp.maximum(counts[0], counts[1])
        branch = jnp.int32(0)
        for capacity in capacities[:-1]:
            branch += jnp.where(most > capacity, 1, 0)
        branch_ref[0] = branch
        for u in range(half):
            slot = slot_ref[side * half + u]
            local = lax.div(slot, half) == side
            place = place_ref[slot]
            k = lax.rem(slot, half)
            out_ref[FETCH, u] = jnp.where(local, k, half + place)
            out_ref[CROSS, u] = jnp.where(local, half, place)
            out_ref[LOCAL, u] = jnp.where(local, k, half)

    return pl.pallas_call(
        kernel,
        out_shape=[jax.ShapeDtypeStruct((5, half), I32), jax.ShapeDtypeStruct((1,), I32)],
        in_specs=[SMEM] * 2,
        out_specs=[SMEM] * 2,
        scratch_shapes=[pltpu.SMEM((devices,), I32)] * 3,
    )(jnp.transpose(segments, (2, 1, 0)), owner_map)


def split_pieces(stacked, target, after=()):
    half = stacked.shape[0]

    def kernel(stacked_ref, *out_refs):
        for ref, p in zip(out_refs, partners(target, True)):
            ref[...] = stacked_ref[p]

    piece = jax.ShapeDtypeStruct(stacked.shape[1:], BF16)
    return call(kernel, [], [stacked], [piece] * half, after=after)


def join_pieces(pieces, source):
    half = len(pieces)

    def kernel(*refs):
        for ref, p in zip(refs, partners(source, False)):
            refs[half][p] = ref[...]

    out = jax.ShapeDtypeStruct((half,) + pieces[0].shape, BF16)
    return call(kernel, [], pieces, [out])[0]


def pick_crossing(route, table, source, count, after=()):
    half = len(table)
    shape = table[0].shape

    def kernel(route_ref, *refs):
        out_ref, all_ref = refs[half:]
        for ref, p in zip(refs, partners(source, False)):
            all_ref[p] = ref[...]
        for j in range(count):
            out_ref[j] = all_ref[route_ref[SEND, j]]

    out = jax.ShapeDtypeStruct((count,) + shape, BF16)
    scratch = jax.ShapeDtypeStruct((half,) + shape, BF16)
    return call(kernel, [route], table, [out], [scratch], after)[0]


def pick_pieces(route, table, source, target, arrived, terms=None, after=()):
    half = len(table)
    count = arrived.shape[0]
    shape = table[0].shape
    arrays = list(table) + [arrived] + ([] if terms is None else [terms])

    def kernel(route_ref, *refs):
        out_refs, all_ref = refs[len(arrays) : -1], refs[-1]
        for ref, p in zip(refs[:half], partners(source, False)):
            all_ref[p] = ref[...]
        for j in range(count):
            all_ref[half + j] = refs[half][j]
        for ref, p in zip(out_refs, partners(target, True)):
            if terms is None:
                ref[...] = all_ref[route_ref[FETCH, p]]
            else:
                ref[0] = all_ref[route_ref[FETCH, p]]
                ref[1] = refs[half + 1][p]

    out = jax.ShapeDtypeStruct(shape if terms is None else (2,) + shape, BF16)
    scratch = jax.ShapeDtypeStruct((half + count,) + shape, BF16)
    return call(kernel, [route], arrays, [out] * half, [scratch], after)


def lower(ref):
    return ref[1] if len(ref.shape) == 3 else ref[...]


def upper(ref):
    return ref[0] if len(ref.shape) == 3 else ref[...]


def sum_crossing(route, pieces, source, count, after=()):
    half = len(pieces)
    shape = pieces[0].shape[-2:]

    def kernel(route_ref, *refs):
        out_ref, total_ref = refs[half:]
        total_ref[...] = jnp.zeros_like(total_ref)
        for ref, p in zip(refs[:half], partners(source, False)):
            place = route_ref[CROSS, p]
            total_ref[place] = total_ref[place] + lower(ref).astype(F32)
        for k in range(count):
            out_ref[k] = total_ref[k].astype(BF16)

    out = jax.ShapeDtypeStruct((count,) + shape, BF16)
    scratch = jax.ShapeDtypeStruct((half + 1,) + shape, F32)
    return call(kernel, [route], pieces, [out], [scratch], after)[0]


def sum_pieces(route, pieces, source, target, arrived, after=()):
    half = len(pieces)
    count = arrived.shape[0]
    shape = pieces[0].shape[-2:]

    def kernel(route_ref, *refs):
        out_refs, total_ref = refs[half + 1 : -1], refs[-1]
        total_ref[...] = jnp.zeros_like(total_ref)
        for ref, p in zip(refs[:half], partners(source, False)):
            place = route_ref[LOCAL, p]
            total_ref[place] = total_ref[place] + lower(ref).astype(F32)
        for j in range(count):
            place = route_ref[ARRIVED, j]
            total_ref[place] = total_ref[place] + refs[half][j].astype(F32)
        for ref, p in zip(out_refs, partners(target, True)):
            ref[...] = (total_ref[p] * (1.0 / BLOCK)).astype(BF16)

    out = jax.ShapeDtypeStruct(shape, BF16)
    scratch = jax.ShapeDtypeStruct((half + 1,) + shape, F32)
    arrays = list(pieces) + [arrived]
    return call(kernel, [route], arrays, [out] * half, [scratch], after)


def term_pieces(pieces, source, target, first, second, after=()):
    half = len(pieces)
    rows, width = first.shape
    piece = pieces[0].shape[-2]
    rank = half * piece
    step = max(s for s in (128, 256, 512, 640, 1024) if width % s == 0)

    def kernel(*refs):
        first_ref, second_ref = refs[half : half + 2]
        if target is None:
            adapter_ref, term_ref = refs[half + 2 :]
        else:
            projected_ref, out_refs = refs[half + 2], refs[half + 3 : -2]
            adapter_ref, term_ref = refs[-2:]
        for ref, p in zip(refs[:half], partners(source, False)):
            adapter_ref[p] = upper(ref)
        total = jnp.zeros((rows, rank), F32)
        for low in range(0, width, step):
            total += lax.dot_general(
                first_ref[:, low : low + step],
                adapter_ref[:, :, low : low + step].reshape(rank, step),
                (((1,), (1,)), ((), ())),
                preferred_element_type=F32,
            )
        if target is not None:
            projected_ref[...] = total.astype(BF16)
        turned = total.T.astype(BF16)
        for low in range(0, width, step):
            term = jnp.dot(turned, second_ref[:, low : low + step], preferred_element_type=F32)
            term_ref[:, :, low : low + step] = term.astype(BF16).reshape(half, piece, step)
        if target is not None:
            for ref, p in zip(out_refs, partners(target, True)):
                ref[...] = term_ref[p]

    stacked = jax.ShapeDtypeStruct((half, piece, width), BF16)
    out = jax.ShapeDtypeStruct((piece, width), BF16)
    projected = jax.ShapeDtypeStruct((rows, rank), BF16)
    arrays = list(pieces) + [first, second]
    if target is None:
        adapter, term = call(kernel, [], arrays, [stacked, stacked], after=after)
        return adapter.reshape(rank, width), term
    got = call(
        kernel, [], arrays, [projected] + [out] * half, [stacked, stacked], after
    )
    return got[0], got[1:]


def three_step(capacity, route, tokens, cotangent, table_down, up):
    devices = lax.axis_size("dp")
    half = devices // 2
    pairs = [(i, (i + half) % devices) for i in range(devices)]

    def across(array):
        return lax.ppermute(array, "dp", pairs)

    crossing_down = pick_crossing(route, table_down, ALONE, capacity)
    arrived_down = across(crossing_down)
    table_up = exchange(split_pieces(up, BESIDE, [crossing_down]), BESIDE)
    crossing_up = pick_crossing(route, table_up, BESIDE, capacity, [arrived_down])
    arrived_up = across(crossing_up)
    got_down = exchange(
        pick_pieces(route, table_down, ALONE, BESIDE, arrived_down, after=[crossing_up]), BESIDE
    )
    down, term_up = term_pieces(got_down, BESIDE, None, tokens, cotangent)
    got_both = exchange(
        pick_pieces(route, table_up, BESIDE, ALONE, arrived_up, term_up), ALONE
    )
    crossing_sums_up = sum_crossing(route, got_both, ALONE, capacity)
    sums_up = across(crossing_sums_up)
    inner, term_down = term_pieces(
        got_both, ALONE, BESIDE, cotangent, tokens, [crossing_sums_up]
    )
    pieces_down = exchange(term_down, BESIDE)
    crossing_sums_down = sum_crossing(route, pieces_down, BESIDE, capacity, [sums_up])
    sums_down = across(crossing_sums_down)
    grad_up = exchange(
        sum_pieces(route, got_both, ALONE, BESIDE, sums_up, [crossing_sums_down]), BESIDE
    )
    grad_rows = dot("tr,rd->td", inner, down).astype(BF16)
    return grad_rows, sum_pieces(route, pieces_down, BESIDE, ALONE, sums_down), grad_up


def exchange(pieces, steps):
    devices = lax.axis_size("dp")
    got = [pieces[0]]
    for piece, step in zip(pieces[1:], steps[1:]):
        got.append(lax.ppermute(piece, "dp", [(i, i ^ step[i % 2]) for i in range(devices)]))
    return got


def shards(tokens, cotangent, segments, owner_map, down_t, up):
    devices = lax.axis_size("dp")
    if devices != 2 * len(ALONE):
        slots = block_slots(segments, owner_map, 1, devices)
        return two_step(slots, tokens, cotangent, down_t, up)
    half = devices // 2
    rank, width = down_t.shape[1:]
    shape = (half, rank // half, width)
    capacities = [3, 4, 5, half]
    route, branch = routes(segments, owner_map, devices, capacities)
    table_down = exchange(split_pieces(down_t.reshape(shape), ALONE), ALONE)
    grad_rows, grad_down, grad_up = lax.switch(
        branch[0],
        [functools.partial(three_step, c) for c in capacities],
        route,
        tokens,
        cotangent,
        table_down,
        up.reshape(shape),
    )
    grad_down = exchange(grad_down, ALONE)
    return (
        grad_rows,
        join_pieces(grad_down, ALONE).reshape(1, rank, width),
        join_pieces(grad_up, BESIDE).reshape(1, rank, width),
    )


def solution(mesh):
    in_specs = (
        P(("groups", "dp"), None),
        P(("groups", "dp"), None),
        P("groups", None, None),
        P("groups"),
        P(("groups", "dp"), None, None),
        P(("groups", "dp"), None, None),
    )
    out_specs = (
        P(("groups", "dp"), None),
        P(("groups", "dp"), None, None),
        P(("groups", "dp"), None, None),
    )
    return jax.shard_map(shards, mesh=mesh, in_specs=in_specs, out_specs=out_specs, check_vma=False)
```

```python
import functools

import jax
import jax.numpy as jnp
from jax import lax
from jax.experimental import pallas as pl
from jax.experimental.pallas import tpu as pltpu
from jax.sharding import PartitionSpec as P

BLOCK = 128
F32 = jnp.float32
BF16 = jnp.bfloat16
I32 = jnp.int32
VMEM = pl.BlockSpec(memory_space=pltpu.VMEM)
SMEM = pl.BlockSpec(memory_space=pltpu.SMEM)


def block_slots(segments, owner_map, blocks, count_adapters):
    index = jnp.arange(blocks, dtype=I32)
    ids = segments[:, :, 0]
    starts = segments[:, :, 1]
    counts = segments[:, :, 2]
    inside = (index[None, None, :] >= starts[:, :, None]) & (
        index[None, None, :] < (starts + counts)[:, :, None]
    )
    adapter = jnp.sum(jnp.where(inside, ids[:, :, None], 0), axis=1)
    match = adapter[:, :, None] == jnp.arange(count_adapters, dtype=I32)[None, None, :]
    slots = jnp.sum(jnp.where(match, owner_map[None, None, :], 0), axis=2)
    return slots.reshape(-1)


def dot(spec, a, b):
    return jnp.einsum(spec, a, b, preferred_element_type=F32)


def two_step(slots, tokens, cotangent, down_t, up):
    devices = lax.axis_size("dp")
    rank, width = down_t.shape[1:]
    piece = 2 * rank // devices
    exchange = functools.partial(
        lax.all_to_all, axis_name="dp", split_axis=0, concat_axis=0, tiled=True
    )
    stack = jnp.concatenate([down_t[0], up[0]], axis=0).reshape(devices, piece, width)
    table = exchange(stack)
    mine = exchange(jnp.take(table, slots, axis=0, mode="clip")).reshape(2 * rank, width)
    down, up_ = mine[:rank], mine[rank:]
    hidden = dot("td,rd->tr", tokens, down).astype(BF16)
    inner = dot("td,rd->tr", cotangent, up_).astype(BF16)
    grad_rows = dot("tr,rd->td", inner, down).astype(BF16)
    terms = jnp.concatenate(
        [dot("tr,td->rd", inner, tokens), dot("tr,td->rd", hidden, cotangent)], axis=0
    ).astype(BF16)
    pieces = exchange(terms.reshape(devices, piece, width))
    onehot = (slots[None, :] == jnp.arange(devices, dtype=I32)[:, None]).astype(BF16)
    summed = dot("kb,bpd->kpd", onehot, pieces) * (1.0 / BLOCK)
    grads = exchange(summed.astype(BF16)).reshape(2, rank, width)
    return grad_rows, grads[:1], grads[1:]


STEPS = ((0, 0), (6, 6), (2, 4), (4, 2), (7, 7), (3, 5), (5, 3), (1, 1))


def partners(sending):
    own = lax.rem(lax.axis_index("dp"), len(STEPS))
    places = []
    for a, b in STEPS:
        if a % 2 and not sending:
            a, b = b, a
        places.append(own ^ jnp.where(own % 2 == 1, b, a) if a != b else own ^ a)
    return places


def call(kernel, scalars, arrays, outs, scratch=(), after=()):
    size = 4 << 20
    for array in list(arrays) + list(outs) + list(scratch):
        extent = array.dtype.itemsize
        for value in array.shape:
            extent *= value
        size += extent
    given = len(scalars) + len(arrays)
    return pl.pallas_call(
        lambda *refs: kernel(*refs[:given], *refs[given + len(after) :]),
        out_shape=outs,
        in_specs=[SMEM] * len(scalars)
        + [VMEM] * len(arrays)
        + [pl.BlockSpec(memory_space=pl.ANY)] * len(after),
        out_specs=[VMEM] * len(outs),
        scratch_shapes=[pltpu.VMEM(s.shape, s.dtype) for s in scratch],
        compiler_params=pltpu.CompilerParams(vmem_limit_bytes=size),
    )(*scalars, *arrays, *after)


SEND, ARRIVED, FETCH, CROSS, LOCAL = range(5)


def routes(segments, owner_map, devices, capacities):
    half = devices // 2
    entries = segments.shape[1]

    def kernel(segments_ref, owner_ref, out_ref, branch_ref, slot_ref, need_ref, place_ref):
        side = lax.div(lax.axis_index("dp"), half)
        for d in range(devices):
            need_ref[d] = 0
            adapter = 0
            for e in range(entries):
                start = segments_ref[1, e, d]
                inside = (start <= 0) & (start + segments_ref[2, e, d] > 0)
                adapter += jnp.where(inside, segments_ref[0, e, d], 0)
            slot_ref[d] = owner_ref[adapter]
        for d in range(devices):
            slot = slot_ref[d]
            need_ref[slot] = jnp.where(lax.div(slot, half) != d // half, 1, need_ref[slot])
        for j in range(half):
            out_ref[SEND, j] = 0
            out_ref[ARRIVED, j] = half
        counts = []
        for s in range(2):
            count = jnp.int32(0)
            for k in range(half):
                needed = need_ref[s * half + k]
                place_ref[s * half + k] = count

                @pl.when((side == s) & (needed == 1))
                def _(count=count, k=k):
                    out_ref[SEND, count] = k
                    out_ref[ARRIVED, count] = k

                count += needed
            counts.append(count)
        most = jnp.maximum(counts[0], counts[1])
        branch = jnp.int32(0)
        for capacity in capacities[:-1]:
            branch += jnp.where(most > capacity, 1, 0)
        branch_ref[0] = branch
        for u in range(half):
            slot = slot_ref[side * half + u]
            local = lax.div(slot, half) == side
            place = place_ref[slot]
            k = lax.rem(slot, half)
            out_ref[FETCH, u] = jnp.where(local, k, half + place)
            out_ref[CROSS, u] = jnp.where(local, half, place)
            out_ref[LOCAL, u] = jnp.where(local, k, half)

    return pl.pallas_call(
        kernel,
        out_shape=[jax.ShapeDtypeStruct((5, half), I32), jax.ShapeDtypeStruct((1,), I32)],
        in_specs=[SMEM] * 2,
        out_specs=[SMEM] * 2,
        scratch_shapes=[pltpu.SMEM((devices,), I32)] * 3,
    )(jnp.transpose(segments, (2, 1, 0)), owner_map)


def split_pieces(stacked, after=()):
    half = stacked.shape[0]

    def kernel(stacked_ref, *out_refs):
        for ref, p in zip(out_refs, partners(True)):
            ref[...] = stacked_ref[p]

    piece = jax.ShapeDtypeStruct(stacked.shape[1:], BF16)
    return call(kernel, [], [stacked], [piece] * half, after=after)


def join_pieces(pieces):
    half = len(pieces)

    def kernel(*refs):
        for ref, p in zip(refs, partners(False)):
            refs[half][p] = ref[...]

    out = jax.ShapeDtypeStruct((half,) + pieces[0].shape, BF16)
    return call(kernel, [], pieces, [out])[0]


def pick_crossing(route, table, count, after=()):
    half = len(table)
    shape = table[0].shape

    def kernel(route_ref, *refs):
        out_ref, all_ref = refs[half:]
        for ref, p in zip(refs, partners(False)):
            all_ref[p] = ref[...]
        for j in range(count):
            out_ref[j] = all_ref[route_ref[SEND, j]]

    out = jax.ShapeDtypeStruct((count,) + shape, BF16)
    scratch = jax.ShapeDtypeStruct((half,) + shape, BF16)
    return call(kernel, [route], table, [out], [scratch], after)[0]


def pick_pieces(route, table, arrived, terms=None, after=()):
    half = len(table)
    count = arrived.shape[0]
    shape = table[0].shape
    arrays = list(table) + [arrived] + ([] if terms is None else [terms])

    def kernel(route_ref, *refs):
        out_refs, all_ref = refs[len(arrays) : -1], refs[-1]
        for ref, p in zip(refs[:half], partners(False)):
            all_ref[p] = ref[...]
        for j in range(count):
            all_ref[half + j] = refs[half][j]
        for ref, p in zip(out_refs, partners(True)):
            if terms is None:
                ref[...] = all_ref[route_ref[FETCH, p]]
            else:
                ref[0] = all_ref[route_ref[FETCH, p]]
                ref[1] = refs[half + 1][p]

    out = jax.ShapeDtypeStruct(shape if terms is None else (2,) + shape, BF16)
    scratch = jax.ShapeDtypeStruct((half + count,) + shape, BF16)
    return call(kernel, [route], arrays, [out] * half, [scratch], after)


def lower(ref):
    return ref[1] if len(ref.shape) == 3 else ref[...]


def upper(ref):
    return ref[0] if len(ref.shape) == 3 else ref[...]


def sum_crossing(route, pieces, count, after=()):
    half = len(pieces)
    shape = pieces[0].shape[-2:]

    def kernel(route_ref, *refs):
        out_ref, total_ref = refs[half:]
        total_ref[...] = jnp.zeros_like(total_ref)
        for ref, p in zip(refs[:half], partners(False)):
            place = route_ref[CROSS, p]
            total_ref[place] = total_ref[place] + lower(ref).astype(F32)
        for k in range(count):
            out_ref[k] = total_ref[k].astype(BF16)

    out = jax.ShapeDtypeStruct((count,) + shape, BF16)
    scratch = jax.ShapeDtypeStruct((half + 1,) + shape, F32)
    return call(kernel, [route], pieces, [out], [scratch], after)[0]


def sum_pieces(route, pieces, arrived, after=()):
    half = len(pieces)
    count = arrived.shape[0]
    shape = pieces[0].shape[-2:]

    def kernel(route_ref, *refs):
        out_refs, total_ref = refs[half + 1 : -1], refs[-1]
        total_ref[...] = jnp.zeros_like(total_ref)
        for ref, p in zip(refs[:half], partners(False)):
            place = route_ref[LOCAL, p]
            total_ref[place] = total_ref[place] + lower(ref).astype(F32)
        for j in range(count):
            place = route_ref[ARRIVED, j]
            total_ref[place] = total_ref[place] + refs[half][j].astype(F32)
        for ref, p in zip(out_refs, partners(True)):
            ref[...] = (total_ref[p] * (1.0 / BLOCK)).astype(BF16)

    out = jax.ShapeDtypeStruct(shape, BF16)
    scratch = jax.ShapeDtypeStruct((half + 1,) + shape, F32)
    arrays = list(pieces) + [arrived]
    return call(kernel, [route], arrays, [out] * half, [scratch], after)


def term_pieces(pieces, first, second, whole, after=()):
    half = len(pieces)
    rows, width = first.shape
    piece = pieces[0].shape[-2]
    rank = half * piece
    step = max(s for s in (128, 256, 512, 640, 1024) if width % s == 0)

    def kernel(*refs):
        first_ref, second_ref = refs[half : half + 2]
        if whole:
            adapter_ref, term_ref = refs[half + 2 :]
        else:
            projected_ref, out_refs = refs[half + 2], refs[half + 3 : -2]
            adapter_ref, term_ref = refs[-2:]
        for ref, p in zip(refs[:half], partners(False)):
            adapter_ref[p] = upper(ref)
        total = jnp.zeros((rows, rank), F32)
        for low in range(0, width, step):
            total += lax.dot_general(
                first_ref[:, low : low + step],
                adapter_ref[:, :, low : low + step].reshape(rank, step),
                (((1,), (1,)), ((), ())),
                preferred_element_type=F32,
            )
        if not whole:
            projected_ref[...] = total.astype(BF16)
        turned = total.T.astype(BF16)
        for low in range(0, width, step):
            term = jnp.dot(turned, second_ref[:, low : low + step], preferred_element_type=F32)
            term_ref[:, :, low : low + step] = term.astype(BF16).reshape(half, piece, step)
        if not whole:
            for ref, p in zip(out_refs, partners(True)):
                ref[...] = term_ref[p]

    stacked = jax.ShapeDtypeStruct((half, piece, width), BF16)
    out = jax.ShapeDtypeStruct((piece, width), BF16)
    projected = jax.ShapeDtypeStruct((rows, rank), BF16)
    arrays = list(pieces) + [first, second]
    if whole:
        adapter, term = call(kernel, [], arrays, [stacked, stacked], after=after)
        return adapter.reshape(rank, width), term
    got = call(
        kernel, [], arrays, [projected] + [out] * half, [stacked, stacked], after
    )
    return got[0], got[1:]


def three_step(capacity, route, tokens, cotangent, table_down, up):
    devices = lax.axis_size("dp")
    half = devices // 2
    pairs = [(i, (i + half) % devices) for i in range(devices)]

    def across(array):
        return lax.ppermute(array, "dp", pairs)

    crossing_down = pick_crossing(route, table_down, capacity)
    arrived_down = across(crossing_down)
    table_up = exchange(split_pieces(up, [crossing_down]))
    crossing_up = pick_crossing(route, table_up, capacity, [arrived_down])
    arrived_up = across(crossing_up)
    got_down = exchange(pick_pieces(route, table_down, arrived_down, after=[crossing_up]))
    down, term_up = term_pieces(got_down, tokens, cotangent, True)
    got_both = exchange(pick_pieces(route, table_up, arrived_up, term_up))
    crossing_sums_up = sum_crossing(route, got_both, capacity)
    sums_up = across(crossing_sums_up)
    inner, term_down = term_pieces(got_both, cotangent, tokens, False, [crossing_sums_up])
    pieces_down = exchange(term_down)
    crossing_sums_down = sum_crossing(route, pieces_down, capacity, [sums_up])
    sums_down = across(crossing_sums_down)
    grad_up = exchange(sum_pieces(route, got_both, sums_up, [crossing_sums_down]))
    grad_rows = dot("tr,rd->td", inner, down).astype(BF16)
    return grad_rows, sum_pieces(route, pieces_down, sums_down), grad_up


def exchange(pieces):
    devices = lax.axis_size("dp")
    got = [pieces[0]]
    for piece, step in zip(pieces[1:], STEPS[1:]):
        got.append(lax.ppermute(piece, "dp", [(i, i ^ step[i % 2]) for i in range(devices)]))
    return got


def shards(tokens, cotangent, segments, owner_map, down_t, up):
    devices = lax.axis_size("dp")
    if devices != 2 * len(STEPS):
        slots = block_slots(segments, owner_map, 1, devices)
        return two_step(slots, tokens, cotangent, down_t, up)
    half = devices // 2
    rank, width = down_t.shape[1:]
    shape = (half, rank // half, width)
    capacities = [3, 4, 5, half]
    route, branch = routes(segments, owner_map, devices, capacities)
    table_down = exchange(split_pieces(down_t.reshape(shape)))
    grad_rows, grad_down, grad_up = lax.switch(
        branch[0],
        [functools.partial(three_step, c) for c in capacities],
        route,
        tokens,
        cotangent,
        table_down,
        up.reshape(shape),
    )
    grad_down = exchange(grad_down)
    return (
        grad_rows,
        join_pieces(grad_down).reshape(1, rank, width),
        join_pieces(grad_up).reshape(1, rank, width),
    )


def solution(mesh):
    in_specs = (
        P(("groups", "dp"), None),
        P(("groups", "dp"), None),
        P("groups", None, None),
        P("groups"),
        P(("groups", "dp"), None, None),
        P(("groups", "dp"), None, None),
    )
    out_specs = (
        P(("groups", "dp"), None),
        P(("groups", "dp"), None, None),
        P(("groups", "dp"), None, None),
    )
    return jax.shard_map(shards, mesh=mesh, in_specs=in_specs, out_specs=out_specs, check_vma=False)
```

```python
import functools

import jax
import jax.numpy as jnp
from jax import lax
from jax.experimental import pallas as pl
from jax.experimental.pallas import tpu as pltpu
from jax.sharding import PartitionSpec as P

BLOCK = 128
F32 = jnp.float32
BF16 = jnp.bfloat16
I32 = jnp.int32
VMEM = pl.BlockSpec(memory_space=pltpu.VMEM)
SMEM = pl.BlockSpec(memory_space=pltpu.SMEM)


def block_slots(segments, owner_map, blocks, count_adapters):
    index = jnp.arange(blocks, dtype=I32)
    ids = segments[:, :, 0]
    starts = segments[:, :, 1]
    counts = segments[:, :, 2]
    inside = (index[None, None, :] >= starts[:, :, None]) & (
        index[None, None, :] < (starts + counts)[:, :, None]
    )
    adapter = jnp.sum(jnp.where(inside, ids[:, :, None], 0), axis=1)
    match = adapter[:, :, None] == jnp.arange(count_adapters, dtype=I32)[None, None, :]
    slots = jnp.sum(jnp.where(match, owner_map[None, None, :], 0), axis=2)
    return slots.reshape(-1)


def dot(spec, a, b):
    return jnp.einsum(spec, a, b, preferred_element_type=F32)


def two_step(slots, tokens, cotangent, down_t, up):
    devices = lax.axis_size("dp")
    rank, width = down_t.shape[1:]
    piece = 2 * rank // devices
    exchange = functools.partial(
        lax.all_to_all, axis_name="dp", split_axis=0, concat_axis=0, tiled=True
    )
    stack = jnp.concatenate([down_t[0], up[0]], axis=0).reshape(devices, piece, width)
    table = exchange(stack)
    mine = exchange(jnp.take(table, slots, axis=0, mode="clip")).reshape(2 * rank, width)
    down, up_ = mine[:rank], mine[rank:]
    hidden = dot("td,rd->tr", tokens, down).astype(BF16)
    inner = dot("td,rd->tr", cotangent, up_).astype(BF16)
    grad_rows = dot("tr,rd->td", inner, down).astype(BF16)
    terms = jnp.concatenate(
        [dot("tr,td->rd", inner, tokens), dot("tr,td->rd", hidden, cotangent)], axis=0
    ).astype(BF16)
    pieces = exchange(terms.reshape(devices, piece, width))
    onehot = (slots[None, :] == jnp.arange(devices, dtype=I32)[:, None]).astype(BF16)
    summed = dot("kb,bpd->kpd", onehot, pieces) * (1.0 / BLOCK)
    grads = exchange(summed.astype(BF16)).reshape(2, rank, width)
    return grad_rows, grads[:1], grads[1:]


STEPS = ((0, 0), (6, 6), (7, 7), (2, 4), (4, 2), (3, 5), (5, 3), (1, 1))


def partners(sending):
    own = lax.rem(lax.axis_index("dp"), len(STEPS))
    places = []
    for a, b in STEPS:
        if a % 2 and not sending:
            a, b = b, a
        places.append(own ^ jnp.where(own % 2 == 1, b, a) if a != b else own ^ a)
    return places


def call(kernel, scalars, arrays, outs, scratch=(), after=()):
    size = 4 << 20
    for array in list(arrays) + list(outs) + list(scratch):
        extent = array.dtype.itemsize
        for value in array.shape:
            extent *= value
        size += extent
    given = len(scalars) + len(arrays)
    return pl.pallas_call(
        lambda *refs: kernel(*refs[:given], *refs[given + len(after) :]),
        out_shape=outs,
        in_specs=[SMEM] * len(scalars)
        + [VMEM] * len(arrays)
        + [pl.BlockSpec(memory_space=pl.ANY)] * len(after),
        out_specs=[VMEM] * len(outs),
        scratch_shapes=[pltpu.VMEM(s.shape, s.dtype) for s in scratch],
        compiler_params=pltpu.CompilerParams(vmem_limit_bytes=size),
    )(*scalars, *arrays, *after)


SEND, ARRIVED, FETCH, CROSS, LOCAL = range(5)


def routes(segments, owner_map, devices, capacities):
    half = devices // 2
    entries = segments.shape[1]

    def kernel(segments_ref, owner_ref, out_ref, branch_ref, slot_ref, need_ref, place_ref):
        side = lax.div(lax.axis_index("dp"), half)
        for d in range(devices):
            need_ref[d] = 0
            adapter = 0
            for e in range(entries):
                start = segments_ref[1, e, d]
                inside = (start <= 0) & (start + segments_ref[2, e, d] > 0)
                adapter += jnp.where(inside, segments_ref[0, e, d], 0)
            slot_ref[d] = owner_ref[adapter]
        for d in range(devices):
            slot = slot_ref[d]
            need_ref[slot] = jnp.where(lax.div(slot, half) != d // half, 1, need_ref[slot])
        for j in range(half):
            out_ref[SEND, j] = 0
            out_ref[ARRIVED, j] = half
        counts = []
        for s in range(2):
            count = jnp.int32(0)
            for k in range(half):
                needed = need_ref[s * half + k]
                place_ref[s * half + k] = count

                @pl.when((side == s) & (needed == 1))
                def _(count=count, k=k):
                    out_ref[SEND, count] = k
                    out_ref[ARRIVED, count] = k

                count += needed
            counts.append(count)
        most = jnp.maximum(counts[0], counts[1])
        branch = jnp.int32(0)
        for capacity in capacities[:-1]:
            branch += jnp.where(most > capacity, 1, 0)
        branch_ref[0] = branch
        for u in range(half):
            slot = slot_ref[side * half + u]
            local = lax.div(slot, half) == side
            place = place_ref[slot]
            k = lax.rem(slot, half)
            out_ref[FETCH, u] = jnp.where(local, k, half + place)
            out_ref[CROSS, u] = jnp.where(local, half, place)
            out_ref[LOCAL, u] = jnp.where(local, k, half)

    return pl.pallas_call(
        kernel,
        out_shape=[jax.ShapeDtypeStruct((5, half), I32), jax.ShapeDtypeStruct((1,), I32)],
        in_specs=[SMEM] * 2,
        out_specs=[SMEM] * 2,
        scratch_shapes=[pltpu.SMEM((devices,), I32)] * 3,
    )(jnp.transpose(segments, (2, 1, 0)), owner_map)


def split_pieces(stacked, after=()):
    half = stacked.shape[0]

    def kernel(stacked_ref, *out_refs):
        for ref, p in zip(out_refs, partners(True)):
            ref[...] = stacked_ref[p]

    piece = jax.ShapeDtypeStruct(stacked.shape[1:], BF16)
    return call(kernel, [], [stacked], [piece] * half, after=after)


def join_pieces(pieces):
    half = len(pieces)

    def kernel(*refs):
        for ref, p in zip(refs, partners(False)):
            refs[half][p] = ref[...]

    out = jax.ShapeDtypeStruct((half,) + pieces[0].shape, BF16)
    return call(kernel, [], pieces, [out])[0]


def pick_crossing(route, table, count, after=()):
    half = len(table)
    shape = table[0].shape

    def kernel(route_ref, *refs):
        out_ref, all_ref = refs[half:]
        for ref, p in zip(refs, partners(False)):
            all_ref[p] = ref[...]
        for j in range(count):
            out_ref[j] = all_ref[route_ref[SEND, j]]

    out = jax.ShapeDtypeStruct((count,) + shape, BF16)
    scratch = jax.ShapeDtypeStruct((half,) + shape, BF16)
    return call(kernel, [route], table, [out], [scratch], after)[0]


def pick_pieces(route, table, arrived, terms=None, after=()):
    half = len(table)
    count = arrived.shape[0]
    shape = table[0].shape
    arrays = list(table) + [arrived] + ([] if terms is None else [terms])

    def kernel(route_ref, *refs):
        out_refs, all_ref = refs[len(arrays) : -1], refs[-1]
        for ref, p in zip(refs[:half], partners(False)):
            all_ref[p] = ref[...]
        for j in range(count):
            all_ref[half + j] = refs[half][j]
        for ref, p in zip(out_refs, partners(True)):
            if terms is None:
                ref[...] = all_ref[route_ref[FETCH, p]]
            else:
                ref[0] = all_ref[route_ref[FETCH, p]]
                ref[1] = refs[half + 1][p]

    out = jax.ShapeDtypeStruct(shape if terms is None else (2,) + shape, BF16)
    scratch = jax.ShapeDtypeStruct((half + count,) + shape, BF16)
    return call(kernel, [route], arrays, [out] * half, [scratch], after)


def lower(ref):
    return ref[1] if len(ref.shape) == 3 else ref[...]


def upper(ref):
    return ref[0] if len(ref.shape) == 3 else ref[...]


def sum_crossing(route, pieces, count, after=()):
    half = len(pieces)
    shape = pieces[0].shape[-2:]

    def kernel(route_ref, *refs):
        out_ref, total_ref = refs[half:]
        total_ref[...] = jnp.zeros_like(total_ref)
        for ref, p in zip(refs[:half], partners(False)):
            place = route_ref[CROSS, p]
            total_ref[place] = total_ref[place] + lower(ref).astype(F32)
        for k in range(count):
            out_ref[k] = total_ref[k].astype(BF16)

    out = jax.ShapeDtypeStruct((count,) + shape, BF16)
    scratch = jax.ShapeDtypeStruct((half + 1,) + shape, F32)
    return call(kernel, [route], pieces, [out], [scratch], after)[0]


def sum_pieces(route, pieces, arrived, after=()):
    half = len(pieces)
    count = arrived.shape[0]
    shape = pieces[0].shape[-2:]

    def kernel(route_ref, *refs):
        out_refs, total_ref = refs[half + 1 : -1], refs[-1]
        total_ref[...] = jnp.zeros_like(total_ref)
        for ref, p in zip(refs[:half], partners(False)):
            place = route_ref[LOCAL, p]
            total_ref[place] = total_ref[place] + lower(ref).astype(F32)
        for j in range(count):
            place = route_ref[ARRIVED, j]
            total_ref[place] = total_ref[place] + refs[half][j].astype(F32)
        for ref, p in zip(out_refs, partners(True)):
            ref[...] = (total_ref[p] * (1.0 / BLOCK)).astype(BF16)

    out = jax.ShapeDtypeStruct(shape, BF16)
    scratch = jax.ShapeDtypeStruct((half + 1,) + shape, F32)
    arrays = list(pieces) + [arrived]
    return call(kernel, [route], arrays, [out] * half, [scratch], after)


def term_pieces(pieces, first, second, whole, after=()):
    half = len(pieces)
    rows, width = first.shape
    piece = pieces[0].shape[-2]
    rank = half * piece
    step = max(s for s in (128, 256, 512, 640, 1024) if width % s == 0)

    def kernel(*refs):
        first_ref, second_ref = refs[half : half + 2]
        if whole:
            adapter_ref, term_ref = refs[half + 2 :]
        else:
            projected_ref, out_refs = refs[half + 2], refs[half + 3 : -2]
            adapter_ref, term_ref = refs[-2:]
        for ref, p in zip(refs[:half], partners(False)):
            adapter_ref[p] = upper(ref)
        total = jnp.zeros((rows, rank), F32)
        for low in range(0, width, step):
            total += lax.dot_general(
                first_ref[:, low : low + step],
                adapter_ref[:, :, low : low + step].reshape(rank, step),
                (((1,), (1,)), ((), ())),
                preferred_element_type=F32,
            )
        if not whole:
            projected_ref[...] = total.astype(BF16)
        turned = total.T.astype(BF16)
        for low in range(0, width, step):
            term = jnp.dot(turned, second_ref[:, low : low + step], preferred_element_type=F32)
            term_ref[:, :, low : low + step] = term.astype(BF16).reshape(half, piece, step)
        if not whole:
            for ref, p in zip(out_refs, partners(True)):
                ref[...] = term_ref[p]

    stacked = jax.ShapeDtypeStruct((half, piece, width), BF16)
    out = jax.ShapeDtypeStruct((piece, width), BF16)
    projected = jax.ShapeDtypeStruct((rows, rank), BF16)
    arrays = list(pieces) + [first, second]
    if whole:
        adapter, term = call(kernel, [], arrays, [stacked, stacked], after=after)
        return adapter.reshape(rank, width), term
    got = call(
        kernel, [], arrays, [projected] + [out] * half, [stacked, stacked], after
    )
    return got[0], got[1:]


def three_step(capacity, route, tokens, cotangent, table_down, up):
    devices = lax.axis_size("dp")
    half = devices // 2
    pairs = [(i, (i + half) % devices) for i in range(devices)]

    def across(array):
        return lax.ppermute(array, "dp", pairs)

    crossing_down = pick_crossing(route, table_down, capacity)
    arrived_down = across(crossing_down)
    table_up = exchange(split_pieces(up, [crossing_down]))
    crossing_up = pick_crossing(route, table_up, capacity, [arrived_down])
    arrived_up = across(crossing_up)
    got_down = exchange(pick_pieces(route, table_down, arrived_down, after=[crossing_up]))
    down, term_up = term_pieces(got_down, tokens, cotangent, True)
    got_both = exchange(pick_pieces(route, table_up, arrived_up, term_up))
    crossing_sums_up = sum_crossing(route, got_both, capacity)
    sums_up = across(crossing_sums_up)
    inner, term_down = term_pieces(got_both, cotangent, tokens, False, [crossing_sums_up])
    pieces_down = exchange(term_down)
    crossing_sums_down = sum_crossing(route, pieces_down, capacity, [sums_up])
    sums_down = across(crossing_sums_down)
    grad_up = exchange(sum_pieces(route, got_both, sums_up, [crossing_sums_down]))
    grad_rows = dot("tr,rd->td", inner, down).astype(BF16)
    return grad_rows, sum_pieces(route, pieces_down, sums_down), grad_up


def exchange(pieces):
    devices = lax.axis_size("dp")
    got = [pieces[0]]
    for piece, step in zip(pieces[1:], STEPS[1:]):
        got.append(lax.ppermute(piece, "dp", [(i, i ^ step[i % 2]) for i in range(devices)]))
    return got


def shards(tokens, cotangent, segments, owner_map, down_t, up):
    devices = lax.axis_size("dp")
    if devices != 2 * len(STEPS):
        slots = block_slots(segments, owner_map, 1, devices)
        return two_step(slots, tokens, cotangent, down_t, up)
    half = devices // 2
    rank, width = down_t.shape[1:]
    shape = (half, rank // half, width)
    capacities = [3, 4, 5, half]
    route, branch = routes(segments, owner_map, devices, capacities)
    table_down = exchange(split_pieces(down_t.reshape(shape)))
    grad_rows, grad_down, grad_up = lax.switch(
        branch[0],
        [functools.partial(three_step, c) for c in capacities],
        route,
        tokens,
        cotangent,
        table_down,
        up.reshape(shape),
    )
    grad_down = exchange(grad_down)
    return (
        grad_rows,
        join_pieces(grad_down).reshape(1, rank, width),
        join_pieces(grad_up).reshape(1, rank, width),
    )


def solution(mesh):
    in_specs = (
        P(("groups", "dp"), None),
        P(("groups", "dp"), None),
        P("groups", None, None),
        P("groups"),
        P(("groups", "dp"), None, None),
        P(("groups", "dp"), None, None),
    )
    out_specs = (
        P(("groups", "dp"), None),
        P(("groups", "dp"), None, None),
        P(("groups", "dp"), None, None),
    )
    return jax.shard_map(shards, mesh=mesh, in_specs=in_specs, out_specs=out_specs, check_vma=False)
```

```python
import functools

import jax
import jax.numpy as jnp
from jax import lax
from jax.experimental import pallas as pl
from jax.experimental.pallas import tpu as pltpu
from jax.sharding import PartitionSpec as P

BLOCK = 128
F32 = jnp.float32
BF16 = jnp.bfloat16
I32 = jnp.int32
VMEM = pl.BlockSpec(memory_space=pltpu.VMEM)
SMEM = pl.BlockSpec(memory_space=pltpu.SMEM)


def block_slots(segments, owner_map, blocks, count_adapters):
    index = jnp.arange(blocks, dtype=I32)
    ids = segments[:, :, 0]
    starts = segments[:, :, 1]
    counts = segments[:, :, 2]
    inside = (index[None, None, :] >= starts[:, :, None]) & (
        index[None, None, :] < (starts + counts)[:, :, None]
    )
    adapter = jnp.sum(jnp.where(inside, ids[:, :, None], 0), axis=1)
    match = adapter[:, :, None] == jnp.arange(count_adapters, dtype=I32)[None, None, :]
    slots = jnp.sum(jnp.where(match, owner_map[None, None, :], 0), axis=2)
    return slots.reshape(-1)


def dot(spec, a, b):
    return jnp.einsum(spec, a, b, preferred_element_type=F32)


def two_step(slots, tokens, cotangent, down_t, up):
    devices = lax.axis_size("dp")
    rank, width = down_t.shape[1:]
    piece = 2 * rank // devices
    exchange = functools.partial(
        lax.all_to_all, axis_name="dp", split_axis=0, concat_axis=0, tiled=True
    )
    stack = jnp.concatenate([down_t[0], up[0]], axis=0).reshape(devices, piece, width)
    table = exchange(stack)
    mine = exchange(jnp.take(table, slots, axis=0, mode="clip")).reshape(2 * rank, width)
    down, up_ = mine[:rank], mine[rank:]
    hidden = dot("td,rd->tr", tokens, down).astype(BF16)
    inner = dot("td,rd->tr", cotangent, up_).astype(BF16)
    grad_rows = dot("tr,rd->td", inner, down).astype(BF16)
    terms = jnp.concatenate(
        [dot("tr,td->rd", inner, tokens), dot("tr,td->rd", hidden, cotangent)], axis=0
    ).astype(BF16)
    pieces = exchange(terms.reshape(devices, piece, width))
    onehot = (slots[None, :] == jnp.arange(devices, dtype=I32)[:, None]).astype(BF16)
    summed = dot("kb,bpd->kpd", onehot, pieces) * (1.0 / BLOCK)
    grads = exchange(summed.astype(BF16)).reshape(2, rank, width)
    return grad_rows, grads[:1], grads[1:]


STEPS = ((0, 0), (6, 6), (2, 4), (4, 2), (7, 7), (3, 5), (5, 3), (1, 1))


def partners(sending):
    own = lax.rem(lax.axis_index("dp"), len(STEPS))
    places = []
    for a, b in STEPS:
        if a % 2 and not sending:
            a, b = b, a
        places.append(own ^ jnp.where(own % 2 == 1, b, a) if a != b else own ^ a)
    return places


def call(kernel, scalars, arrays, outs, scratch=(), after=()):
    size = 4 << 20
    for array in list(arrays) + list(outs) + list(scratch):
        extent = array.dtype.itemsize
        for value in array.shape:
            extent *= value
        size += extent
    given = len(scalars) + len(arrays)
    return pl.pallas_call(
        lambda *refs: kernel(*refs[:given], *refs[given + len(after) :]),
        out_shape=outs,
        in_specs=[SMEM] * len(scalars)
        + [VMEM] * len(arrays)
        + [pl.BlockSpec(memory_space=pl.ANY)] * len(after),
        out_specs=[VMEM] * len(outs),
        scratch_shapes=[pltpu.VMEM(s.shape, s.dtype) for s in scratch],
        compiler_params=pltpu.CompilerParams(vmem_limit_bytes=size),
    )(*scalars, *arrays, *after)


SEND, ARRIVED, FETCH, CROSS, LOCAL = range(5)


def routes(segments, owner_map, devices, capacities):
    half = devices // 2
    entries = segments.shape[1]

    def kernel(segments_ref, owner_ref, out_ref, branch_ref, slot_ref, need_ref, place_ref):
        side = lax.div(lax.axis_index("dp"), half)
        for d in range(devices):
            need_ref[d] = 0
            adapter = 0
            for e in range(entries):
                start = segments_ref[1, e, d]
                inside = (start <= 0) & (start + segments_ref[2, e, d] > 0)
                adapter += jnp.where(inside, segments_ref[0, e, d], 0)
            slot_ref[d] = owner_ref[adapter]
        for d in range(devices):
            slot = slot_ref[d]
            need_ref[slot] = jnp.where(lax.div(slot, half) != d // half, 1, need_ref[slot])
        for j in range(half):
            out_ref[SEND, j] = 0
            out_ref[ARRIVED, j] = half
        counts = []
        for s in range(2):
            count = jnp.int32(0)
            for k in range(half):
                needed = need_ref[s * half + k]
                place_ref[s * half + k] = count

                @pl.when((side == s) & (needed == 1))
                def _(count=count, k=k):
                    out_ref[SEND, count] = k
                    out_ref[ARRIVED, count] = k

                count += needed
            counts.append(count)
        most = jnp.maximum(counts[0], counts[1])
        branch = jnp.int32(0)
        for capacity in capacities[:-1]:
            branch += jnp.where(most > capacity, 1, 0)
        branch_ref[0] = branch
        for u in range(half):
            slot = slot_ref[side * half + u]
            local = lax.div(slot, half) == side
            place = place_ref[slot]
            k = lax.rem(slot, half)
            out_ref[FETCH, u] = jnp.where(local, k, half + place)
            out_ref[CROSS, u] = jnp.where(local, half, place)
            out_ref[LOCAL, u] = jnp.where(local, k, half)

    return pl.pallas_call(
        kernel,
        out_shape=[jax.ShapeDtypeStruct((5, half), I32), jax.ShapeDtypeStruct((1,), I32)],
        in_specs=[SMEM] * 2,
        out_specs=[SMEM] * 2,
        scratch_shapes=[pltpu.SMEM((devices,), I32)] * 3,
    )(jnp.transpose(segments, (2, 1, 0)), owner_map)


def split_pieces(stacked, after=()):
    half = stacked.shape[0]

    def kernel(stacked_ref, *out_refs):
        for ref, p in zip(out_refs, partners(True)):
            ref[...] = stacked_ref[p]

    piece = jax.ShapeDtypeStruct(stacked.shape[1:], BF16)
    return call(kernel, [], [stacked], [piece] * half, after=after)


def join_pieces(pieces):
    half = len(pieces)

    def kernel(*refs):
        for ref, p in zip(refs, partners(False)):
            refs[half][p] = ref[...]

    out = jax.ShapeDtypeStruct((half,) + pieces[0].shape, BF16)
    return call(kernel, [], pieces, [out])[0]


def pick_crossing(route, table, count, after=()):
    half = len(table)
    shape = table[0].shape

    def kernel(route_ref, *refs):
        out_ref, all_ref = refs[half:]
        for ref, p in zip(refs, partners(False)):
            all_ref[p] = ref[...]
        for j in range(count):
            out_ref[j] = all_ref[route_ref[SEND, j]]

    out = jax.ShapeDtypeStruct((count,) + shape, BF16)
    scratch = jax.ShapeDtypeStruct((half,) + shape, BF16)
    return call(kernel, [route], table, [out], [scratch], after)[0]


def pick_pieces(route, table, arrived, terms=None, after=()):
    half = len(table)
    count = arrived.shape[0]
    shape = table[0].shape
    arrays = list(table) + [arrived] + ([] if terms is None else [terms])

    def kernel(route_ref, *refs):
        out_refs, all_ref = refs[len(arrays) : -1], refs[-1]
        for ref, p in zip(refs[:half], partners(False)):
            all_ref[p] = ref[...]
        for j in range(count):
            all_ref[half + j] = refs[half][j]
        for ref, p in zip(out_refs, partners(True)):
            if terms is None:
                ref[...] = all_ref[route_ref[FETCH, p]]
            else:
                ref[0] = all_ref[route_ref[FETCH, p]]
                ref[1] = refs[half + 1][p]

    out = jax.ShapeDtypeStruct(shape if terms is None else (2,) + shape, BF16)
    scratch = jax.ShapeDtypeStruct((half + count,) + shape, BF16)
    return call(kernel, [route], arrays, [out] * half, [scratch], after)


def lower(ref):
    return ref[1] if len(ref.shape) == 3 else ref[...]


def upper(ref):
    return ref[0] if len(ref.shape) == 3 else ref[...]


def sum_crossing(route, pieces, count, after=()):
    half = len(pieces)
    shape = pieces[0].shape[-2:]

    def kernel(route_ref, *refs):
        out_ref, total_ref = refs[half:]
        total_ref[...] = jnp.zeros_like(total_ref)
        for ref, p in zip(refs[:half], partners(False)):
            place = route_ref[CROSS, p]
            total_ref[place] = total_ref[place] + lower(ref).astype(F32)
        for k in range(count):
            out_ref[k] = total_ref[k].astype(BF16)

    out = jax.ShapeDtypeStruct((count,) + shape, BF16)
    scratch = jax.ShapeDtypeStruct((half + 1,) + shape, F32)
    return call(kernel, [route], pieces, [out], [scratch], after)[0]


def sum_pieces(route, pieces, arrived, after=()):
    half = len(pieces)
    count = arrived.shape[0]
    shape = pieces[0].shape[-2:]

    def kernel(route_ref, *refs):
        out_refs, total_ref = refs[half + 1 : -1], refs[-1]
        total_ref[...] = jnp.zeros_like(total_ref)
        for ref, p in zip(refs[:half], partners(False)):
            place = route_ref[LOCAL, p]
            total_ref[place] = total_ref[place] + lower(ref).astype(F32)
        for j in range(count):
            place = route_ref[ARRIVED, j]
            total_ref[place] = total_ref[place] + refs[half][j].astype(F32)
        for ref, p in zip(out_refs, partners(True)):
            ref[...] = (total_ref[p] * (1.0 / BLOCK)).astype(BF16)

    out = jax.ShapeDtypeStruct(shape, BF16)
    scratch = jax.ShapeDtypeStruct((half + 1,) + shape, F32)
    arrays = list(pieces) + [arrived]
    return call(kernel, [route], arrays, [out] * half, [scratch], after)


def term_pieces(pieces, first, second, whole, after=()):
    half = len(pieces)
    rows, width = first.shape
    piece = pieces[0].shape[-2]
    rank = half * piece
    step = max(s for s in (128, 256, 512, 640, 1024) if width % s == 0)

    def kernel(*refs):
        first_ref, second_ref = refs[half : half + 2]
        if whole:
            adapter_ref, term_ref = refs[half + 2 :]
        else:
            projected_ref, out_refs = refs[half + 2], refs[half + 3 : -2]
            adapter_ref, term_ref = refs[-2:]
        for ref, p in zip(refs[:half], partners(False)):
            adapter_ref[p] = upper(ref)
        total = jnp.zeros((rows, rank), F32)
        for low in range(0, width, step):
            total += lax.dot_general(
                first_ref[:, low : low + step],
                adapter_ref[:, :, low : low + step].reshape(rank, step),
                (((1,), (1,)), ((), ())),
                preferred_element_type=F32,
            )
        if not whole:
            projected_ref[...] = total.astype(BF16)
        turned = total.T.astype(BF16)
        for low in range(0, width, step):
            term = jnp.dot(turned, second_ref[:, low : low + step], preferred_element_type=F32)
            term_ref[:, :, low : low + step] = term.astype(BF16).reshape(half, piece, step)
        if not whole:
            for ref, p in zip(out_refs, partners(True)):
                ref[...] = term_ref[p]

    stacked = jax.ShapeDtypeStruct((half, piece, width), BF16)
    out = jax.ShapeDtypeStruct((piece, width), BF16)
    projected = jax.ShapeDtypeStruct((rows, rank), BF16)
    arrays = list(pieces) + [first, second]
    if whole:
        adapter, term = call(kernel, [], arrays, [stacked, stacked], after=after)
        return adapter.reshape(rank, width), term
    got = call(
        kernel, [], arrays, [projected] + [out] * half, [stacked, stacked], after
    )
    return got[0], got[1:]


def three_step(capacity, route, tokens, cotangent, table_down, up):
    devices = lax.axis_size("dp")
    half = devices // 2
    pairs = [(i, (i + half) % devices) for i in range(devices)]

    def across(array):
        return lax.ppermute(array, "dp", pairs)

    crossing_down = pick_crossing(route, table_down, capacity)
    arrived_down = across(crossing_down)
    table_up = exchange(split_pieces(up, [crossing_down]))
    crossing_up = pick_crossing(route, table_up, capacity, [arrived_down])
    arrived_up = across(crossing_up)
    got_down = exchange(pick_pieces(route, table_down, arrived_down))
    down, term_up = term_pieces(got_down, tokens, cotangent, True)
    got_both = exchange(pick_pieces(route, table_up, arrived_up, term_up))
    crossing_sums_up = sum_crossing(route, got_both, capacity)
    sums_up = across(crossing_sums_up)
    inner, term_down = term_pieces(got_both, cotangent, tokens, False, [crossing_sums_up])
    pieces_down = exchange(term_down)
    crossing_sums_down = sum_crossing(route, pieces_down, capacity, [sums_up])
    sums_down = across(crossing_sums_down)
    grad_up = exchange(sum_pieces(route, got_both, sums_up, [crossing_sums_down]))
    grad_rows = dot("tr,rd->td", inner, down).astype(BF16)
    return grad_rows, sum_pieces(route, pieces_down, sums_down), grad_up


def exchange(pieces):
    devices = lax.axis_size("dp")
    got = [pieces[0]]
    for piece, step in zip(pieces[1:], STEPS[1:]):
        got.append(lax.ppermute(piece, "dp", [(i, i ^ step[i % 2]) for i in range(devices)]))
    return got


def shards(tokens, cotangent, segments, owner_map, down_t, up):
    devices = lax.axis_size("dp")
    if devices != 2 * len(STEPS):
        slots = block_slots(segments, owner_map, 1, devices)
        return two_step(slots, tokens, cotangent, down_t, up)
    half = devices // 2
    rank, width = down_t.shape[1:]
    shape = (half, rank // half, width)
    capacities = [3, 4, 5, half]
    route, branch = routes(segments, owner_map, devices, capacities)
    table_down = exchange(split_pieces(down_t.reshape(shape)))
    grad_rows, grad_down, grad_up = lax.switch(
        branch[0],
        [functools.partial(three_step, c) for c in capacities],
        route,
        tokens,
        cotangent,
        table_down,
        up.reshape(shape),
    )
    grad_down = exchange(grad_down)
    return (
        grad_rows,
        join_pieces(grad_down).reshape(1, rank, width),
        join_pieces(grad_up).reshape(1, rank, width),
    )


def solution(mesh):
    in_specs = (
        P(("groups", "dp"), None),
        P(("groups", "dp"), None),
        P("groups", None, None),
        P("groups"),
        P(("groups", "dp"), None, None),
        P(("groups", "dp"), None, None),
    )
    out_specs = (
        P(("groups", "dp"), None),
        P(("groups", "dp"), None, None),
        P(("groups", "dp"), None, None),
    )
    return jax.shard_map(shards, mesh=mesh, in_specs=in_specs, out_specs=out_specs, check_vma=False)
```

```python
import functools

import jax
import jax.numpy as jnp
from jax import lax
from jax.experimental import pallas as pl
from jax.experimental.pallas import tpu as pltpu
from jax.sharding import PartitionSpec as P

BLOCK = 128
F32 = jnp.float32
BF16 = jnp.bfloat16
I32 = jnp.int32
VMEM = pl.BlockSpec(memory_space=pltpu.VMEM)
SMEM = pl.BlockSpec(memory_space=pltpu.SMEM)


def block_slots(segments, owner_map, blocks, count_adapters):
    index = jnp.arange(blocks, dtype=I32)
    ids = segments[:, :, 0]
    starts = segments[:, :, 1]
    counts = segments[:, :, 2]
    inside = (index[None, None, :] >= starts[:, :, None]) & (
        index[None, None, :] < (starts + counts)[:, :, None]
    )
    adapter = jnp.sum(jnp.where(inside, ids[:, :, None], 0), axis=1)
    match = adapter[:, :, None] == jnp.arange(count_adapters, dtype=I32)[None, None, :]
    slots = jnp.sum(jnp.where(match, owner_map[None, None, :], 0), axis=2)
    return slots.reshape(-1)


def dot(spec, a, b):
    return jnp.einsum(spec, a, b, preferred_element_type=F32)


def two_step(slots, tokens, cotangent, down_t, up):
    devices = lax.axis_size("dp")
    rank, width = down_t.shape[1:]
    piece = 2 * rank // devices
    exchange = functools.partial(
        lax.all_to_all, axis_name="dp", split_axis=0, concat_axis=0, tiled=True
    )
    stack = jnp.concatenate([down_t[0], up[0]], axis=0).reshape(devices, piece, width)
    table = exchange(stack)
    mine = exchange(jnp.take(table, slots, axis=0, mode="clip")).reshape(2 * rank, width)
    down, up_ = mine[:rank], mine[rank:]
    hidden = dot("td,rd->tr", tokens, down).astype(BF16)
    inner = dot("td,rd->tr", cotangent, up_).astype(BF16)
    grad_rows = dot("tr,rd->td", inner, down).astype(BF16)
    terms = jnp.concatenate(
        [dot("tr,td->rd", inner, tokens), dot("tr,td->rd", hidden, cotangent)], axis=0
    ).astype(BF16)
    pieces = exchange(terms.reshape(devices, piece, width))
    onehot = (slots[None, :] == jnp.arange(devices, dtype=I32)[:, None]).astype(BF16)
    summed = dot("kb,bpd->kpd", onehot, pieces) * (1.0 / BLOCK)
    grads = exchange(summed.astype(BF16)).reshape(2, rank, width)
    return grad_rows, grads[:1], grads[1:]


STEPS = ((0, 0), (6, 6), (2, 4), (4, 2), (7, 7), (3, 5), (5, 3), (1, 1))


def partners(sending):
    own = lax.rem(lax.axis_index("dp"), len(STEPS))
    places = []
    for a, b in STEPS:
        if a % 2 and not sending:
            a, b = b, a
        places.append(own ^ jnp.where(own % 2 == 1, b, a) if a != b else own ^ a)
    return places


def call(kernel, scalars, arrays, outs, scratch=(), after=()):
    size = 4 << 20
    for array in list(arrays) + list(outs) + list(scratch):
        extent = array.dtype.itemsize
        for value in array.shape:
            extent *= value
        size += extent
    given = len(scalars) + len(arrays)
    return pl.pallas_call(
        lambda *refs: kernel(*refs[:given], *refs[given + len(after) :]),
        out_shape=outs,
        in_specs=[SMEM] * len(scalars)
        + [VMEM] * len(arrays)
        + [pl.BlockSpec(memory_space=pl.ANY)] * len(after),
        out_specs=[VMEM] * len(outs),
        scratch_shapes=[pltpu.VMEM(s.shape, s.dtype) for s in scratch],
        compiler_params=pltpu.CompilerParams(vmem_limit_bytes=size),
    )(*scalars, *arrays, *after)


SEND, ARRIVED, FETCH, CROSS, LOCAL = range(5)


def routes(segments, owner_map, devices, capacities):
    half = devices // 2
    entries = segments.shape[1]

    def kernel(segments_ref, owner_ref, out_ref, branch_ref, slot_ref, need_ref, place_ref):
        side = lax.div(lax.axis_index("dp"), half)
        for d in range(devices):
            need_ref[d] = 0
            adapter = 0
            for e in range(entries):
                start = segments_ref[1, e, d]
                inside = (start <= 0) & (start + segments_ref[2, e, d] > 0)
                adapter += jnp.where(inside, segments_ref[0, e, d], 0)
            slot_ref[d] = owner_ref[adapter]
        for d in range(devices):
            slot = slot_ref[d]
            need_ref[slot] = jnp.where(lax.div(slot, half) != d // half, 1, need_ref[slot])
        for j in range(half):
            out_ref[SEND, j] = 0
            out_ref[ARRIVED, j] = half
        counts = []
        for s in range(2):
            count = jnp.int32(0)
            for k in range(half):
                needed = need_ref[s * half + k]
                place_ref[s * half + k] = count

                @pl.when((side == s) & (needed == 1))
                def _(count=count, k=k):
                    out_ref[SEND, count] = k
                    out_ref[ARRIVED, count] = k

                count += needed
            counts.append(count)
        most = jnp.maximum(counts[0], counts[1])
        branch = jnp.int32(0)
        for capacity in capacities[:-1]:
            branch += jnp.where(most > capacity, 1, 0)
        branch_ref[0] = branch
        for u in range(half):
            slot = slot_ref[side * half + u]
            local = lax.div(slot, half) == side
            place = place_ref[slot]
            k = lax.rem(slot, half)
            out_ref[FETCH, u] = jnp.where(local, k, half + place)
            out_ref[CROSS, u] = jnp.where(local, half, place)
            out_ref[LOCAL, u] = jnp.where(local, k, half)

    return pl.pallas_call(
        kernel,
        out_shape=[jax.ShapeDtypeStruct((5, half), I32), jax.ShapeDtypeStruct((1,), I32)],
        in_specs=[SMEM] * 2,
        out_specs=[SMEM] * 2,
        scratch_shapes=[pltpu.SMEM((devices,), I32)] * 3,
    )(jnp.transpose(segments, (2, 1, 0)), owner_map)


def split_pieces(stacked, after=()):
    half = stacked.shape[0]

    def kernel(stacked_ref, *out_refs):
        for ref, p in zip(out_refs, partners(True)):
            ref[...] = stacked_ref[p]

    piece = jax.ShapeDtypeStruct(stacked.shape[1:], BF16)
    return call(kernel, [], [stacked], [piece] * half, after=after)


def join_pieces(pieces):
    half = len(pieces)

    def kernel(*refs):
        for ref, p in zip(refs, partners(False)):
            refs[half][p] = ref[...]

    out = jax.ShapeDtypeStruct((half,) + pieces[0].shape, BF16)
    return call(kernel, [], pieces, [out])[0]


def pick_crossing(route, table, count, after=()):
    half = len(table)
    shape = table[0].shape

    def kernel(route_ref, *refs):
        out_ref, all_ref = refs[half:]
        for ref, p in zip(refs, partners(False)):
            all_ref[p] = ref[...]
        for j in range(count):
            out_ref[j] = all_ref[route_ref[SEND, j]]

    out = jax.ShapeDtypeStruct((count,) + shape, BF16)
    scratch = jax.ShapeDtypeStruct((half,) + shape, BF16)
    return call(kernel, [route], table, [out], [scratch], after)[0]


def pick_pieces(route, table, arrived, terms=None, after=()):
    half = len(table)
    count = arrived.shape[0]
    shape = table[0].shape
    arrays = list(table) + [arrived] + ([] if terms is None else [terms])

    def kernel(route_ref, *refs):
        out_refs, all_ref = refs[len(arrays) : -1], refs[-1]
        for ref, p in zip(refs[:half], partners(False)):
            all_ref[p] = ref[...]
        for j in range(count):
            all_ref[half + j] = refs[half][j]
        for ref, p in zip(out_refs, partners(True)):
            if terms is None:
                ref[...] = all_ref[route_ref[FETCH, p]]
            else:
                ref[0] = all_ref[route_ref[FETCH, p]]
                ref[1] = refs[half + 1][p]

    out = jax.ShapeDtypeStruct(shape if terms is None else (2,) + shape, BF16)
    scratch = jax.ShapeDtypeStruct((half + count,) + shape, BF16)
    return call(kernel, [route], arrays, [out] * half, [scratch], after)


def lower(ref):
    return ref[1] if len(ref.shape) == 3 else ref[...]


def upper(ref):
    return ref[0] if len(ref.shape) == 3 else ref[...]


def sum_crossing(route, pieces, count, after=()):
    half = len(pieces)
    shape = pieces[0].shape[-2:]

    def kernel(route_ref, *refs):
        out_ref, total_ref = refs[half:]
        total_ref[...] = jnp.zeros_like(total_ref)
        for ref, p in zip(refs[:half], partners(False)):
            place = route_ref[CROSS, p]
            total_ref[place] = total_ref[place] + lower(ref).astype(F32)
        for k in range(count):
            out_ref[k] = total_ref[k].astype(BF16)

    out = jax.ShapeDtypeStruct((count,) + shape, BF16)
    scratch = jax.ShapeDtypeStruct((half + 1,) + shape, F32)
    return call(kernel, [route], pieces, [out], [scratch], after)[0]


def sum_pieces(route, pieces, arrived, after=()):
    half = len(pieces)
    count = arrived.shape[0]
    shape = pieces[0].shape[-2:]

    def kernel(route_ref, *refs):
        out_refs, total_ref = refs[half + 1 : -1], refs[-1]
        total_ref[...] = jnp.zeros_like(total_ref)
        for ref, p in zip(refs[:half], partners(False)):
            place = route_ref[LOCAL, p]
            total_ref[place] = total_ref[place] + lower(ref).astype(F32)
        for j in range(count):
            place = route_ref[ARRIVED, j]
            total_ref[place] = total_ref[place] + refs[half][j].astype(F32)
        for ref, p in zip(out_refs, partners(True)):
            ref[...] = (total_ref[p] * (1.0 / BLOCK)).astype(BF16)

    out = jax.ShapeDtypeStruct(shape, BF16)
    scratch = jax.ShapeDtypeStruct((half + 1,) + shape, F32)
    arrays = list(pieces) + [arrived]
    return call(kernel, [route], arrays, [out] * half, [scratch], after)


def term_pieces(pieces, first, second, whole, after=()):
    half = len(pieces)
    rows, width = first.shape
    piece = pieces[0].shape[-2]
    rank = half * piece
    step = max(s for s in (128, 256, 512, 640, 1024) if width % s == 0)

    def kernel(*refs):
        first_ref, second_ref = refs[half : half + 2]
        if whole:
            adapter_ref, term_ref = refs[half + 2 :]
        else:
            projected_ref, out_refs = refs[half + 2], refs[half + 3 : -2]
            adapter_ref, term_ref = refs[-2:]
        for ref, p in zip(refs[:half], partners(False)):
            adapter_ref[p] = upper(ref)
        total = jnp.zeros((rows, rank), F32)
        for low in range(0, width, step):
            total += lax.dot_general(
                first_ref[:, low : low + step],
                adapter_ref[:, :, low : low + step].reshape(rank, step),
                (((1,), (1,)), ((), ())),
                preferred_element_type=F32,
            )
        if not whole:
            projected_ref[...] = total.astype(BF16)
        turned = total.T.astype(BF16)
        for low in range(0, width, step):
            term = jnp.dot(turned, second_ref[:, low : low + step], preferred_element_type=F32)
            term_ref[:, :, low : low + step] = term.astype(BF16).reshape(half, piece, step)
        if not whole:
            for ref, p in zip(out_refs, partners(True)):
                ref[...] = term_ref[p]

    stacked = jax.ShapeDtypeStruct((half, piece, width), BF16)
    out = jax.ShapeDtypeStruct((piece, width), BF16)
    projected = jax.ShapeDtypeStruct((rows, rank), BF16)
    arrays = list(pieces) + [first, second]
    if whole:
        adapter, term = call(kernel, [], arrays, [stacked, stacked], after=after)
        return adapter.reshape(rank, width), term
    got = call(
        kernel, [], arrays, [projected] + [out] * half, [stacked, stacked], after
    )
    return got[0], got[1:]


def three_step(capacity, route, tokens, cotangent, table_down, up):
    devices = lax.axis_size("dp")
    half = devices // 2
    pairs = [(i, (i + half) % devices) for i in range(devices)]

    def across(array):
        return lax.ppermute(array, "dp", pairs)

    crossing_down = pick_crossing(route, table_down, capacity)
    arrived_down = across(crossing_down)
    table_up = exchange(split_pieces(up, [crossing_down]))
    crossing_up = pick_crossing(route, table_up, capacity, [arrived_down])
    arrived_up = across(crossing_up)
    got_down = exchange(pick_pieces(route, table_down, arrived_down))
    down, term_up = term_pieces(got_down, tokens, cotangent, True)
    got_both = exchange(pick_pieces(route, table_up, arrived_up, term_up))
    crossing_sums_up = sum_crossing(route, got_both, capacity)
    sums_up = across(crossing_sums_up)
    inner, term_down = term_pieces(got_both, cotangent, tokens, False, [crossing_sums_up])
    pieces_down = exchange(term_down)
    crossing_sums_down = sum_crossing(route, pieces_down, capacity, [sums_up])
    sums_down = across(crossing_sums_down)
    grad_up = exchange(sum_pieces(route, got_both, sums_up))
    grad_rows = dot("tr,rd->td", inner, down).astype(BF16)
    return grad_rows, sum_pieces(route, pieces_down, sums_down), grad_up


def exchange(pieces):
    devices = lax.axis_size("dp")
    got = [pieces[0]]
    for piece, step in zip(pieces[1:], STEPS[1:]):
        got.append(lax.ppermute(piece, "dp", [(i, i ^ step[i % 2]) for i in range(devices)]))
    return got


def shards(tokens, cotangent, segments, owner_map, down_t, up):
    devices = lax.axis_size("dp")
    if devices != 2 * len(STEPS):
        slots = block_slots(segments, owner_map, 1, devices)
        return two_step(slots, tokens, cotangent, down_t, up)
    half = devices // 2
    rank, width = down_t.shape[1:]
    shape = (half, rank // half, width)
    capacities = [3, 4, 5, half]
    route, branch = routes(segments, owner_map, devices, capacities)
    table_down = exchange(split_pieces(down_t.reshape(shape)))
    grad_rows, grad_down, grad_up = lax.switch(
        branch[0],
        [functools.partial(three_step, c) for c in capacities],
        route,
        tokens,
        cotangent,
        table_down,
        up.reshape(shape),
    )
    grad_down = exchange(grad_down)
    return (
        grad_rows,
        join_pieces(grad_down).reshape(1, rank, width),
        join_pieces(grad_up).reshape(1, rank, width),
    )


def solution(mesh):
    in_specs = (
        P(("groups", "dp"), None),
        P(("groups", "dp"), None),
        P("groups", None, None),
        P("groups"),
        P(("groups", "dp"), None, None),
        P(("groups", "dp"), None, None),
    )
    out_specs = (
        P(("groups", "dp"), None),
        P(("groups", "dp"), None, None),
        P(("groups", "dp"), None, None),
    )
    return jax.shard_map(shards, mesh=mesh, in_specs=in_specs, out_specs=out_specs, check_vma=False)
```
